32 devices in a mesh: sec: 2 (over core), seq: 4 (over z), tp: 4 (over y, x).
Axes of the slice: x: 2, y: 2, z: 4, core: 2. Of those that a mesh axis runs over, the one named last changes fastest.
Arguments:
- vis_hidden: bfloat16 [768, 8192], P('tp', 'seq'), may hold values from -6 to 6
- proj_weight: bfloat16 [8192, 8192], P('seq', 'tp'), may hold values from -0.0625 to 0.0625
- proj_bias: float32 [8192], P('tp'), may hold values from -3 to 3
- text_embed: bfloat16 [4096, 8192], P('seq', 'tp'), may hold values from -6 to 6
- norm_gain: float32 [8192], P('tp'), may hold values from 0.1 to 1.9
- key_weight: bfloat16 [8192, 1024], P('tp'), may hold values from -0.0625 to 0.0625
- key_cotangent: bfloat16 [4096, 1024], P('seq'), may hold values from -0.119628906 to 0.119628906
- tile_counts: int32 [4], replicated, may hold values from 0 to 2, as said below
- text_counts: int32 [4], replicated, may hold values from 1 to 1024, as said below
- owner_map: int32 [4], replicated, may hold values from 0 to 3, each once
Outputs:
- proj_weight_grad: float32 [8192, 4, 2, 1024], P('seq', 'tp', 'sec')
- proj_bias_grad: float32 [8192], P('tp')
- key_weight_grad: float32 [8192, 1024], P('tp', ('sec', 'seq'))
- key_bias_grad: float32 [1024], replicated
- gain_grad: float32 [8192], P('tp')
The draws below stay inside these ranges and needn't reach their ends.
Inputs may be any that keep to these rules, and one draw needn't show every extreme that they name: `tile_counts`: tiles of all samples sum to exactly 3; some sample has 2. 256 * tile_counts + text_counts is at most 1024 for every sample; some sample without tiles has 1024 text tokens. `owner_map`: each owner index appears once.
All inputs are finite; a program needn't handle non-finite values.
Results may differ from the reference program's by a relative error of at most 0.02.
Values may be sent and summed in bfloat16 or wider, within the bound.
No kernel may reach another device: no remote copies, remote signals or barrier semaphores. Data moves between devices by JAX's collectives and lax.ppermute only.
A program may use at most 128 MiB of HBM per device.

```python
import jax
import jax.numpy as jnp
from jax import lax

D = 8192
KW = 1024
TILE = 256
MAXT = 2
SEQ_L = 1024
TILES_ALL = 3
NV = 768
N_SEQ = 4
N_TP = 4


def tile_plan(key):
    order_key, count_key = jax.random.split(key)
    order = jax.random.permutation(order_key, N_SEQ)
    ranking = jnp.argsort(order, stable=True).astype(jnp.int32)
    doubles = jax.random.randint(count_key, (), 1, TILES_ALL // MAXT + 1)
    singles = TILES_ALL - MAXT * doubles
    tiles = jnp.where(ranking < doubles, MAXT, jnp.where(ranking < doubles + singles, 1, 0))
    return (tiles.astype(jnp.int32), ranking)


def draw_tile_counts(key, part):
    tiles, ranking = tile_plan(key)
    return tiles


def draw_text_counts(key, part):
    tiles, ranking = tile_plan(key)
    key = jax.random.fold_in(key, 12)
    room = SEQ_L - TILE * tiles
    spread_key = jax.random.fold_in(key, 0)
    raw_draw = jax.random.randint(spread_key, (N_SEQ,), 0, 1 << 20)
    counts = 1 + raw_draw % room
    counts = jnp.where(ranking == N_SEQ - 1, room, counts)
    return counts.astype(jnp.int32)


def strengthened(values, stream_key, source, target, blocks, factor):
    owner, partner = [(jnp.arange(values.shape[axis_at]) // (values.shape[axis_at] // blocks)).reshape([-1 if axis == axis_at else 1 for axis in range(values.ndim)]) for axis_at in (source, target)]
    chosen = jax.random.permutation(stream_key, blocks)[partner]
    strong = (owner == chosen) | (owner == (partner + blocks // 2) % blocks)
    return jnp.where(strong, factor * values, values)


def level_of(own_key, dims, cuts, least, top_value):
    gain, own = 1.0, jax.random.fold_in(own_key, 6)
    for position, shards_of in cuts:
        heights = jnp.exp(jax.random.uniform(jax.random.fold_in(own, position), (shards_of,), jnp.float32, least / len(cuts), top_value / len(cuts)))
        gain = gain * jnp.repeat(heights, dims[position] // shards_of).reshape([-1 if axis == position else 1 for axis in range(len(dims))])
    return gain


def gaussian(key, shape, spread, most, cuts=(), held_as=jnp.bfloat16):
    result = spread * jax.random.normal(key, shape, jnp.float32)
    if cuts:
        result = result * level_of(key, shape, cuts, -0.22, 0.18)
    return jnp.clip(result, -most, most).astype(held_as)


def heavy_noise(key, shape, spread, limit, shards, heavy, held_as=jnp.bfloat16):
    array = spread * jax.random.normal(key, shape, jnp.float32)
    if shards:
        array = array * level_of(key, shape, shards, -0.22, 0.18)
    return jnp.clip(strengthened(array, jax.random.fold_in(key, 3), *heavy), -limit, limit).astype(held_as)


def setup_inputs(seed: int = 0) -> dict:
    seeds = jax.random.split(jax.random.key(seed), 11)
    return {
        "vis_hidden": gaussian(seeds[0], (NV, D), 1.0, 6.0, ((0, 4), (1, 4))),
        "proj_weight": gaussian(seeds[1], (D, D), D ** -0.5, 0.0625, ((0, 4), (1, 4))),
        "proj_bias": gaussian(seeds[2], (D,), 0.5, 3.0, ((0, 4),), jnp.float32),
        "text_embed": gaussian(seeds[3], (N_SEQ * SEQ_L, D), 1.0, 6.0, ((0, 4), (1, 4))),
        "norm_gain": jnp.clip(1.0 + 0.18 * jax.random.normal(seeds[4], (D,), jnp.float32), 0.1, 1.9),
        "key_weight": gaussian(seeds[5], (D, KW), D ** -0.5, 0.0625, ((0, 4),)),
        "key_cotangent": heavy_noise(seeds[6], (N_SEQ * SEQ_L, KW), 0.02, 0.119628906, ((0, 4),), (0, 1, 4, 2.0)),
        "tile_counts": draw_tile_counts(jax.random.fold_in(seeds[10], 71), 0),
        "text_counts": draw_text_counts(jax.random.fold_in(seeds[10], 71), 0),
        "owner_map": jax.random.permutation(seeds[9], N_SEQ).astype(jnp.int32),
    }


epsilon = 1e-06

def reference(vis_hidden, proj_weight, proj_bias, text_embed, norm_gain, key_weight, key_cotangent, tile_counts, text_counts, owner_map):
    activated = jax.nn.gelu(vis_hidden.astype(jnp.float32), approximate=False).astype(jnp.bfloat16)
    block_width = D // N_SEQ

    def add_block(running, block_index):
        col_block = lax.dynamic_slice_in_dim(activated, block_index * block_width, block_width, 1)
        rows_block = lax.dynamic_slice_in_dim(proj_weight, block_index * block_width, block_width, 0)
        partial_value = jnp.dot(col_block, rows_block, preferred_element_type=jnp.float32).astype(jnp.bfloat16)
        partial_value = lax.optimization_barrier(partial_value)
        return (running + partial_value.astype(jnp.float32), None)
    summed, unused = lax.scan(add_block, jnp.zeros((NV, D), jnp.float32), jnp.arange(N_SEQ, dtype=jnp.int32))
    image_embed = (summed + proj_bias).astype(jnp.bfloat16)
    image_slots = MAXT * TILE
    starts = (TILE * (jnp.cumsum(tile_counts) - tile_counts)).astype(jnp.int32)
    padded_embed = jnp.concatenate([image_embed, jnp.zeros((image_slots, D), jnp.bfloat16)], 0)
    positions = jnp.arange(SEQ_L, dtype=jnp.int32)
    image_pos = jnp.arange(image_slots, dtype=jnp.int32)

    def per_owner(carried, owner_index):
        weight_acc, gain_acc, bias_acc, grad_rows = carried
        is_mine = owner_map == owner_index
        image_count = (TILE * jnp.sum(jnp.where(is_mine, tile_counts, 0))).astype(jnp.int32)
        image_start = jnp.sum(jnp.where(is_mine, starts, 0)).astype(jnp.int32)
        text_count = jnp.sum(jnp.where(is_mine, text_counts, 0)).astype(jnp.int32)
        image_rows = lax.dynamic_slice_in_dim(padded_embed, image_start, image_slots, 0)
        image_full = jnp.concatenate([image_rows, jnp.zeros((SEQ_L - image_slots, D), jnp.bfloat16)], 0)
        own_text = lax.dynamic_slice_in_dim(text_embed, (owner_index * SEQ_L).astype(jnp.int32), SEQ_L, 0)
        text_padded = jnp.concatenate([jnp.zeros((image_slots, D), jnp.bfloat16), own_text], 0)
        shifted = lax.dynamic_slice_in_dim(text_padded, (image_slots - image_count).astype(jnp.int32), SEQ_L, 0)
        seq_input = jnp.where((positions < image_count)[:, None], image_full, jnp.where((positions < image_count + text_count)[:, None], shifted, jnp.zeros_like(shifted)))
        values = seq_input.astype(jnp.float32)
        inv_rms = lax.rsqrt(lax.optimization_barrier(jnp.sum(values * values, 1)) / D + epsilon)
        unit_rows = values * inv_rms[:, None]
        normed = (unit_rows * norm_gain).astype(jnp.bfloat16)
        own_cotangent = lax.dynamic_slice_in_dim(key_cotangent, (owner_index * SEQ_L).astype(jnp.int32), SEQ_L, 0)
        weight_acc = weight_acc + jnp.dot(normed.T, own_cotangent, preferred_element_type=jnp.float32)
        bias_acc = bias_acc + lax.optimization_barrier(jnp.sum(own_cotangent.astype(jnp.float32), 0))
        normed_grad = jnp.dot(own_cotangent, key_weight.T, preferred_element_type=jnp.float32)
        gain_acc = gain_acc + lax.optimization_barrier(jnp.sum(normed_grad * unit_rows, 0))
        scaled = normed_grad[:image_slots] * norm_gain
        image_unit = unit_rows[:image_slots]
        mean_term = lax.optimization_barrier(jnp.sum(scaled * image_unit, 1)) / D
        input_grad = inv_rms[:image_slots, None] * (scaled - image_unit * mean_term[:, None])
        input_grad = jnp.where((image_pos < image_count)[:, None], input_grad, jnp.zeros_like(input_grad)).astype(jnp.bfloat16)
        current = lax.dynamic_slice_in_dim(grad_rows, image_start, image_slots, 0)
        grad_rows = lax.dynamic_update_slice_in_dim(grad_rows, current + input_grad.astype(jnp.float32), image_start, 0)
        return ((weight_acc, gain_acc, bias_acc, grad_rows), None)
    start_state = (jnp.zeros((D, KW), jnp.float32), jnp.zeros((D,), jnp.float32), jnp.zeros((KW,), jnp.float32), jnp.zeros((NV + image_slots, D), jnp.float32))
    final_state, unused = lax.scan(per_owner, start_state, jnp.arange(N_SEQ, dtype=jnp.int32))
    key_weight_grad, gain_grad, key_bias_grad, grad_rows = final_state
    embed_grad = grad_rows[:NV].astype(jnp.bfloat16)
    proj_weight_grad = jnp.dot(activated.T, embed_grad, preferred_element_type=jnp.float32)
    proj_weight_grad = proj_weight_grad.reshape(D, N_TP, 2, D // (2 * N_TP))
    proj_bias_grad = lax.optimization_barrier(jnp.sum(embed_grad.astype(jnp.float32), 0))
    return (proj_weight_grad, proj_bias_grad, key_weight_grad, key_bias_grad, gain_grad)
```

```python
import jax
import jax.numpy as jnp
from jax import lax
from jax.experimental import pallas as pl
from jax.experimental.pallas import tpu as pltpu
from jax.sharding import PartitionSpec as P

D = 8192
TILE = 256
MAXT = 2
LANES = 128
EPSILON = 1e-06


def swap(x, axis, mask):
    count = lax.axis_size(axis)
    return lax.ppermute(x, axis, [(i, i ^ mask) for i in range(count)])


def butterfly(x, axes):
    for axis in axes:
        mask = 1
        while mask < lax.axis_size(axis):
            x = x + swap(x, axis, mask)
            mask *= 2
    return x


def in_order(pieces, index):
    pieces = list(pieces)
    mask = 1
    while mask < len(pieces):
        odd = (index & mask) != 0
        pieces = [jnp.where(odd, pieces[m ^ mask], pieces[m]) for m in range(len(pieces))]
        mask *= 2
    return pieces


def weight_kernel(act_ref, grad_ref, out_ref):
    width = grad_ref.shape[1]
    rows = act_ref.shape[1]
    groups = width // LANES
    product = lax.dot_general(
        act_ref[...], grad_ref[...], (((0,), (0,)), ((), ())), preferred_element_type=jnp.float32
    )
    for c in range(groups):
        out_ref[pl.ds(c, rows, stride=groups), :] = product[:, c * LANES : (c + 1) * LANES]


def weight_product(act, grad):
    rows, features = act.shape
    width = grad.shape[1]
    groups = width // LANES
    step = 256
    return pl.pallas_call(
        weight_kernel,
        grid=(features // step,),
        in_specs=[
            pl.BlockSpec((rows, step), lambda i: (0, i)),
            pl.BlockSpec((rows, width), lambda i: (0, 0)),
        ],
        out_specs=pl.BlockSpec((step * groups, LANES), lambda i: (i, 0)),
        out_shape=jax.ShapeDtypeStruct((features * groups, LANES), jnp.float32),
        compiler_params=pltpu.CompilerParams(vmem_limit_bytes=32 * 1024 * 1024),
        cost_estimate=pl.CostEstimate(
            flops=2 * rows * features * width,
            bytes_accessed=4 * features * width + 2 * rows * (features + width),
            transcendentals=0,
        ),
    )(act, grad)


def on_device(
    vis_hidden,
    proj_weight,
    proj_bias,
    text_embed,
    norm_gain,
    key_weight,
    key_cotangent,
    tile_counts,
    text_counts,
    owner_map,
):
    f32, bf16 = jnp.float32, jnp.bfloat16
    n_sec, n_seq, n_tp = (lax.axis_size(a) for a in ("sec", "seq", "tp"))
    core, z, t = (lax.axis_index(a) for a in ("sec", "seq", "tp"))
    block_rows, features = vis_hidden.shape
    columns = proj_weight.shape[1]
    stream = block_rows * n_tp
    own = stream // n_seq
    half = own // n_sec
    groups = block_rows // own
    keys = key_weight.shape[1]
    seq_len = text_embed.shape[0]
    tiles = stream // TILE

    grouped = vis_hidden.reshape(groups, n_sec, half, features)
    mine = lax.dynamic_index_in_dim(grouped, core, 1, keepdims=False)
    act = jax.nn.gelu(mine.astype(f32), approximate=False).astype(bf16)
    act = act.reshape(groups * half, features)
    pieces = [act] + [swap(act, "tp", m) for m in range(1, n_tp)]
    act_half = jnp.concatenate(in_order(pieces, t), 0)
    partial = jnp.dot(act_half, proj_weight, preferred_element_type=f32).astype(bf16)
    summed = lax.psum_scatter(partial, "seq", scatter_dimension=0, tiled=True).astype(f32)
    image_mine = (summed + proj_bias).astype(bf16)
    image = jnp.concatenate(in_order([image_mine, swap(image_mine, "sec", 1)], core), 0)

    act_other = swap(act_half, "sec", 1)
    act_full = jnp.stack(
        in_order([a.reshape(n_seq, half, features) for a in (act_half, act_other)], core), 1
    ).reshape(stream, features)

    starts = jnp.cumsum(tile_counts) - tile_counts
    tile_ids = jnp.arange(tiles, dtype=jnp.int32)[:, None]
    held = (tile_ids >= starts[None]) & (tile_ids < (starts + tile_counts)[None])
    tile_owner = jnp.sum(jnp.where(held, owner_map[None], 0), 1)
    tile_place = jnp.sum(jnp.where(held, tile_ids - starts[None], 0), 1)
    share = keys // (n_sec * n_tp)
    from_col = (core * n_tp + t) * share
    front = lax.dynamic_slice_in_dim(key_cotangent[: MAXT * TILE], from_col, share, 1)
    front = front.reshape(MAXT, TILE, share)
    given = jnp.zeros((tiles, TILE, share), bf16)
    for place in range(MAXT):
        chosen = (tile_owner == z) & (tile_place == place)
        given = jnp.where(chosen[:, None, None], front[place][None], given)
    taken = lax.psum_scatter(
        given.reshape(stream, share), "seq", scatter_dimension=0, tiled=True
    )
    taken = lax.all_gather(taken, ("sec", "tp"), axis=0, tiled=False)
    image_cot = taken.transpose(1, 0, 2).reshape(own, keys)

    is_mine = owner_map == z
    image_count = TILE * jnp.sum(jnp.where(is_mine, tile_counts, 0))
    text_count = jnp.sum(jnp.where(is_mine, text_counts, 0))
    text_values = text_embed.astype(f32)
    text_sq = butterfly(jnp.sum(text_values * text_values, 1), ("tp",))
    text_inv = lax.rsqrt(text_sq / D + EPSILON)
    text_scale = jnp.where(jnp.arange(seq_len) < text_count, text_inv, 0.0)
    key_half = keys // n_sec
    cot_half = lax.dynamic_slice_in_dim(key_cotangent, core * key_half, key_half, 1)
    cot_padded = jnp.concatenate([cot_half, jnp.zeros((MAXT * TILE, key_half), bf16)], 0)
    cot_text = lax.dynamic_slice_in_dim(cot_padded, image_count, seq_len, 0)
    cot_text = (cot_text.astype(f32) * text_scale[:, None]).astype(bf16)

    values = image.astype(f32)
    scaled = lax.dot_general(
        image_cot, key_weight, (((1,), (1,)), ((), ())), preferred_element_type=f32
    ) * norm_gain
    sums = butterfly(jnp.stack([jnp.sum(values * values, 1), jnp.sum(scaled * values, 1)]), ("tp",))
    inv = lax.rsqrt(sums[0] / D + EPSILON)
    mean = inv * sums[1] / D
    embed_grad = (inv[:, None] * (scaled - values * (inv * mean)[:, None])).astype(bf16)
    col_half = columns // n_sec
    grad_half = lax.dynamic_slice_in_dim(embed_grad, core * col_half, col_half, 1)
    grad_all = lax.all_gather(grad_half, "seq", axis=0, tiled=True)

    cot_image = lax.dynamic_slice_in_dim(image_cot, core * key_half, key_half, 1)
    cot_image = (cot_image.astype(f32) * inv[:, None]).astype(bf16)
    rows_first = (((0,), (0,)), ((), ()))
    moment = lax.dot_general(
        text_embed, cot_text, rows_first, preferred_element_type=f32
    ) + lax.dot_general(image, cot_image, rows_first, preferred_element_type=f32)
    weight_half = lax.dynamic_slice_in_dim(key_weight, core * key_half, key_half, 1)
    gain_part = jnp.sum(moment * weight_half.astype(f32), 1)
    shares = (moment * norm_gain[:, None]).astype(bf16)
    shares = shares.reshape(columns, n_seq, key_half // n_seq).transpose(1, 0, 2)
    key_weight_grad = lax.psum_scatter(shares, "seq", scatter_dimension=0, tiled=False)
    key_weight_grad = key_weight_grad.astype(f32)

    key_bias_part = jnp.sum(key_cotangent.astype(f32), 0)
    bias_part = jnp.sum(embed_grad.astype(f32), 0)
    once = jnp.concatenate([key_bias_part, bias_part])
    small = butterfly(jnp.concatenate([gain_part, jnp.where(core == 0, once, 0.0)]), ("sec", "seq"))
    gain_grad = small[:columns]
    key_bias_grad = small[columns : columns + keys]
    proj_bias_grad = small[columns + keys :]

    proj_weight_grad = weight_product(act_full, grad_all).reshape(features, 1, 1, col_half)
    return (proj_weight_grad, proj_bias_grad, key_weight_grad, key_bias_grad, gain_grad)


def solution(mesh):
    placed = (
        P("tp", "seq"),
        P("seq", "tp"),
        P("tp"),
        P("seq", "tp"),
        P("tp"),
        P("tp", None),
        P("seq", None),
        P(),
        P(),
        P(),
    )
    return jax.shard_map(
        on_device,
        mesh=mesh,
        in_specs=placed,
        out_specs=(P("seq", "tp", "sec", None), P("tp"), P("tp", ("sec", "seq")), P(), P("tp")),
        check_vma=False,
    )
```

```python
import jax
import jax.numpy as jnp
from jax import lax
from jax.experimental import pallas as pl
from jax.experimental.pallas import tpu as pltpu
from jax.sharding import PartitionSpec as P

D = 8192
TILE = 256
MAXT = 2
LANES = 128
EPSILON = 1e-06


def swap(x, axis, mask):
    count = lax.axis_size(axis)
    return lax.ppermute(x, axis, [(i, i ^ mask) for i in range(count)])


def total(x, axis):
    pieces = [x] + [swap(x, axis, m) for m in range(1, lax.axis_size(axis))]
    while len(pieces) > 1:
        pieces = [pieces[i] + pieces[i + 1] for i in range(0, len(pieces), 2)]
    return pieces[0]


def butterfly(x, axes):
    for axis in axes:
        mask = 1
        while mask < lax.axis_size(axis):
            x = x + swap(x, axis, mask)
            mask *= 2
    return x


def in_order(pieces, index):
    pieces = list(pieces)
    mask = 1
    while mask < len(pieces):
        odd = (index & mask) != 0
        pieces = [jnp.where(odd, pieces[m ^ mask], pieces[m]) for m in range(len(pieces))]
        mask *= 2
    return pieces


def reduce_to_owner(parts, axis):
    index = lax.axis_index(axis)
    count = parts.shape[0]
    while count > 1:
        pairs = parts.reshape(count // 2, 2, *parts.shape[1:])
        mask = lax.axis_size(axis) // count
        bit = (index // mask) % 2
        sent = lax.dynamic_index_in_dim(pairs, 1 - bit, 1, keepdims=False)
        kept = lax.dynamic_index_in_dim(pairs, bit, 1, keepdims=False)
        came = swap(sent.astype(jnp.bfloat16), axis, mask)
        parts = kept.astype(jnp.float32) + came.astype(jnp.float32)
        count //= 2
    return parts[0]


def along_line(x, axis):
    count = lax.axis_size(axis)
    up, down = [], []
    right = left = x
    for i in range(1, count):
        right = lax.ppermute(right, axis, [(j, j + 1) for j in range(i - 1, count - 1)])
        left = lax.ppermute(left, axis, [(j, j - 1) for j in range(1, count - i + 1)])
        up.append(right)
        down.append(left)
    return up, down


def weight_kernel(*refs):
    act_ref, own_ref, out_ref, grad_ref = refs[0], refs[1], refs[-2], refs[-1]
    others = refs[2:-2]
    count = len(others) // 2
    rows, width = own_ref.shape

    @pl.when(pl.program_id(0) == 0)
    def _():
        grad_ref[:rows, :] = own_ref[...]
        for i in range(count):
            grad_ref[(i + 1) * rows : (i + 2) * rows, :] = (
                others[i][...] + others[count + count - 1 - i][...]
            )

    step = act_ref.shape[1]
    groups = width // LANES
    product = lax.dot_general(
        act_ref[...], grad_ref[...], (((0,), (0,)), ((), ())), preferred_element_type=jnp.float32
    )
    for c in range(groups):
        out_ref[pl.ds(c, step, stride=groups), :] = product[:, c * LANES : (c + 1) * LANES]


def weight_product(act, own, others):
    rows, features = act.shape
    width = own.shape[1]
    groups = width // LANES
    step = 256
    piece = pl.BlockSpec(own.shape, lambda i: (0, 0))
    return pl.pallas_call(
        weight_kernel,
        grid=(features // step,),
        in_specs=[pl.BlockSpec((rows, step), lambda i: (0, i))] + [piece] * (1 + len(others)),
        out_specs=pl.BlockSpec((step * groups, LANES), lambda i: (i, 0)),
        out_shape=jax.ShapeDtypeStruct((features * groups, LANES), jnp.float32),
        scratch_shapes=[pltpu.VMEM((rows, width), jnp.bfloat16)],
        compiler_params=pltpu.CompilerParams(vmem_limit_bytes=40 * 1024 * 1024),
        cost_estimate=pl.CostEstimate(
            flops=2 * rows * features * width,
            bytes_accessed=4 * features * width + 2 * rows * (features + width),
            transcendentals=0,
        ),
    )(act, own, *others)


def on_device(
    vis_hidden,
    proj_weight,
    proj_bias,
    text_embed,
    norm_gain,
    key_weight,
    key_cotangent,
    tile_counts,
    text_counts,
    owner_map,
):
    f32, bf16 = jnp.float32, jnp.bfloat16
    n_sec, n_seq, n_tp = (lax.axis_size(a) for a in ("sec", "seq", "tp"))
    core, z, t = (lax.axis_index(a) for a in ("sec", "seq", "tp"))
    block_rows, features = vis_hidden.shape
    columns = proj_weight.shape[1]
    stream = block_rows * n_tp
    own = stream // n_seq
    part_rows = block_rows // n_sec
    sub = part_rows // n_seq
    keys = key_weight.shape[1]
    seq_len = text_embed.shape[0]
    tiles = stream // TILE

    mine = lax.dynamic_slice_in_dim(vis_hidden, core * part_rows, part_rows, 0)
    act = jax.nn.gelu(mine.astype(f32), approximate=False).astype(bf16)
    pieces = [act] + [swap(act, "tp", m) for m in range(1, n_tp)]
    pieces = [p.reshape(n_seq, sub, features) for p in pieces]

    starts = jnp.cumsum(tile_counts) - tile_counts
    tile_ids = jnp.arange(tiles, dtype=jnp.int32)[:, None]
    held = (tile_ids >= starts[None]) & (tile_ids < (starts + tile_counts)[None])
    tile_owner = jnp.sum(jnp.where(held, owner_map[None], 0), 1)
    tile_place = jnp.sum(jnp.where(held, tile_ids - starts[None], 0), 1)
    share = keys // n_tp
    front = lax.dynamic_slice_in_dim(key_cotangent[: MAXT * TILE], t * share, share, 1)
    front = front.reshape(MAXT, TILE, share)
    given = jnp.zeros((tiles, TILE, share), bf16)
    for place in range(MAXT):
        chosen = (tile_owner == z) & (tile_place == place)
        given = jnp.where(chosen[:, None, None], front[place][None], given)
    given = given.reshape(n_tp, n_sec, n_seq, sub, share).transpose(2, 1, 0, 3, 4)
    taken = lax.psum_scatter(
        given.reshape(stream, share), "seq", scatter_dimension=0, tiled=True
    )
    taken = [taken] + [swap(taken, "tp", m) for m in range(1, n_tp)]
    image_cot = jnp.concatenate(in_order(taken, t), 1)
    scaled = lax.dot_general(
        image_cot, key_weight, (((1,), (1,)), ((), ())), preferred_element_type=f32
    ) * norm_gain

    images = []
    for first in range(0, n_tp, 2):
        chunk = jnp.stack(pieces[first : first + 2], 1).reshape(2 * part_rows, features)
        partial = jnp.dot(chunk, proj_weight, preferred_element_type=f32).astype(bf16)
        summed = reduce_to_owner(partial.reshape(n_seq, 2 * sub, columns), "seq")
        images += list((summed + proj_bias).astype(bf16).reshape(2, sub, columns))
    image_mine = jnp.concatenate(in_order(images, t), 0)
    image = jnp.concatenate(in_order([image_mine, swap(image_mine, "sec", 1)], core), 0)

    act_half = jnp.stack(in_order(pieces, t), 1)
    act_pair = in_order([act_half, swap(act_half, "sec", 1)], core)
    act_full = jnp.stack(act_pair, 1).reshape(n_seq, own, features)

    is_mine = owner_map == z
    image_count = TILE * jnp.sum(jnp.where(is_mine, tile_counts, 0))
    text_count = jnp.sum(jnp.where(is_mine, text_counts, 0))
    text_values = text_embed.astype(f32)
    text_sq = total(jnp.sum(text_values * text_values, 1), "tp")
    text_inv = lax.rsqrt(text_sq / D + EPSILON)
    text_scale = jnp.where(jnp.arange(seq_len) < text_count, text_inv, 0.0)
    key_half = keys // n_sec
    cot_half = lax.dynamic_slice_in_dim(key_cotangent, core * key_half, key_half, 1)
    cot_padded = jnp.concatenate([cot_half, jnp.zeros((MAXT * TILE, key_half), bf16)], 0)
    cot_text = lax.dynamic_slice_in_dim(cot_padded, image_count, seq_len, 0)
    cot_text = (cot_text.astype(f32) * text_scale[:, None]).astype(bf16)
    rows_first = (((0,), (0,)), ((), ()))
    text_moment = lax.dot_general(text_embed, cot_text, rows_first, preferred_element_type=f32)

    values = image.astype(f32)
    sums = total(jnp.stack([jnp.sum(values * values, 1), jnp.sum(scaled * values, 1)]), "tp")
    inv = lax.rsqrt(sums[0] / D + EPSILON)
    mean = inv * sums[1] / D
    embed_grad = (inv[:, None] * (scaled - values * (inv * mean)[:, None])).astype(bf16)
    col_half = columns // n_sec
    grad_half = lax.dynamic_slice_in_dim(embed_grad, core * col_half, col_half, 1)

    cot_image = lax.dynamic_slice_in_dim(image_cot, core * key_half, key_half, 1)
    cot_image = (cot_image.astype(f32) * inv[:, None]).astype(bf16)
    moment = text_moment + lax.dot_general(
        image, cot_image, rows_first, preferred_element_type=f32
    )
    weight_half = lax.dynamic_slice_in_dim(key_weight, core * key_half, key_half, 1)
    gain_part = jnp.sum(moment * weight_half.astype(f32), 1)
    shares = (moment * norm_gain[:, None]).astype(bf16)
    shares = shares.reshape(columns, n_seq, key_half // n_seq).transpose(1, 0, 2)
    key_weight_grad = lax.psum_scatter(shares, "seq", scatter_dimension=0, tiled=False)
    key_weight_grad = key_weight_grad.astype(f32)

    key_bias_part = jnp.sum(key_cotangent.astype(f32), 0)
    bias_part = jnp.sum(embed_grad.astype(f32), 0)
    once = jnp.concatenate([key_bias_part, bias_part])
    small = butterfly(jnp.concatenate([gain_part, jnp.where(core == 0, once, 0.0)]), ("sec", "seq"))
    gain_grad = small[:columns]
    key_bias_grad = small[columns : columns + keys]
    proj_bias_grad = small[columns + keys :]

    if n_seq <= 4:
        up, down = along_line(grad_half, "seq")
        around = jnp.concatenate([act_full[::-1], act_full[::-1]], 0)
        act_used = lax.dynamic_slice_in_dim(around, n_seq - 1 - z, n_seq, 0)
        product = weight_product(act_used.reshape(stream, features), grad_half, up + down)
    else:
        grads = lax.all_gather(grad_half, "seq", axis=0, tiled=True)
        product = weight_product(act_full.reshape(stream, features), grads, [])
    proj_weight_grad = product.reshape(features, 1, 1, col_half)
    return (proj_weight_grad, proj_bias_grad, key_weight_grad, key_bias_grad, gain_grad)


def solution(mesh):
    placed = (
        P("tp", "seq"),
        P("seq", "tp"),
        P("tp"),
        P("seq", "tp"),
        P("tp"),
        P("tp", None),
        P("seq", None),
        P(),
        P(),
        P(),
    )
    return jax.shard_map(
        on_device,
        mesh=mesh,
        in_specs=placed,
        out_specs=(P("seq", "tp", "sec", None), P("tp"), P("tp", ("sec", "seq")), P(), P("tp")),
        check_vma=False,
    )
```

```python
import jax
import jax.numpy as jnp
from jax import lax
from jax.experimental import pallas as pl
from jax.experimental.pallas import tpu as pltpu
from jax.sharding import PartitionSpec as P

D = 8192
TILE = 256
MAXT = 2
LANES = 128
EPSILON = 1e-06


def swap(x, axis, mask):
    count = lax.axis_size(axis)
    return lax.ppermute(x, axis, [(i, i ^ mask) for i in range(count)])


def total(x, axis):
    pieces = [x] + [swap(x, axis, m) for m in range(1, lax.axis_size(axis))]
    while len(pieces) > 1:
        pieces = [pieces[i] + pieces[i + 1] for i in range(0, len(pieces), 2)]
    return pieces[0]


def butterfly(x, axes):
    for axis in axes:
        mask = 1
        while mask < lax.axis_size(axis):
            x = x + swap(x, axis, mask)
            mask *= 2
    return x


def in_order(pieces, index):
    pieces = list(pieces)
    mask = 1
    while mask < len(pieces):
        odd = (index & mask) != 0
        pieces = [jnp.where(odd, pieces[m ^ mask], pieces[m]) for m in range(len(pieces))]
        mask *= 2
    return pieces


def reduce_to_owner(parts, axis):
    index = lax.axis_index(axis)
    count = parts.shape[0]
    while count > 1:
        pairs = parts.reshape(count // 2, 2, *parts.shape[1:])
        mask = lax.axis_size(axis) // count
        bit = (index // mask) % 2
        sent = lax.dynamic_index_in_dim(pairs, 1 - bit, 1, keepdims=False)
        kept = lax.dynamic_index_in_dim(pairs, bit, 1, keepdims=False)
        came = swap(sent.astype(jnp.bfloat16), axis, mask)
        parts = kept.astype(jnp.float32) + came.astype(jnp.float32)
        count //= 2
    return parts[0]


def along_line(x, axis):
    count = lax.axis_size(axis)
    up, down = [], []
    right = left = x
    for i in range(1, count):
        right = lax.ppermute(right, axis, [(j, j + 1) for j in range(i - 1, count - 1)])
        left = lax.ppermute(left, axis, [(j, j - 1) for j in range(1, count - i + 1)])
        up.append(right)
        down.append(left)
    return up, down


def columns_of(row, count):
    parts = []
    for i in range(count // LANES):
        part = row[:, i * LANES : (i + 1) * LANES]
        parts.append(jnp.broadcast_to(part, (LANES, LANES)).T)
    return jnp.concatenate(parts, 0)


def row_of(folded):
    count = folded.shape[0]
    parts = [
        jnp.sum(folded[i * LANES : (i + 1) * LANES, :].T, 0, keepdims=True)
        for i in range(count // LANES)
    ]
    return jnp.concatenate(parts, 1)


def fold(values):
    width = values.shape[1]
    out = values[:, :LANES]
    for i in range(1, width // LANES):
        out = out + values[:, i * LANES : (i + 1) * LANES]
    return out


def text_kernel(text_ref, cot_ref, weight_ref, moment_ref, gain_ref):
    moment = lax.dot_general(
        text_ref[...], cot_ref[...], (((0,), (0,)), ((), ())), preferred_element_type=jnp.float32
    )
    for i in range(moment_ref.shape[0]):
        moment_ref[i] = moment[:, i * LANES : (i + 1) * LANES].astype(jnp.bfloat16)
    gain_ref[...] = row_of(fold(moment * weight_ref[...].astype(jnp.float32)))


def text_product(text, cot, weight):
    seq_len, columns = text.shape
    width = cot.shape[1]
    groups = width // LANES
    step = 256
    return pl.pallas_call(
        text_kernel,
        grid=(columns // step,),
        in_specs=[
            pl.BlockSpec((seq_len, step), lambda i: (0, i)),
            pl.BlockSpec((seq_len, width), lambda i: (0, 0)),
            pl.BlockSpec((step, width), lambda i: (i, 0)),
        ],
        out_specs=[
            pl.BlockSpec((groups, step, LANES), lambda i: (0, i, 0)),
            pl.BlockSpec((1, step), lambda i: (0, i)),
        ],
        out_shape=[
            jax.ShapeDtypeStruct((groups, columns, LANES), jnp.bfloat16),
            jax.ShapeDtypeStruct((1, columns), jnp.float32),
        ],
        compiler_params=pltpu.CompilerParams(vmem_limit_bytes=32 * 1024 * 1024),
        cost_estimate=pl.CostEstimate(
            flops=2 * seq_len * columns * width,
            bytes_accessed=2 * (seq_len * (columns + width) + 2 * columns * width),
            transcendentals=0,
        ),
    )(text, cot, weight)


def sums_kernel(*refs):
    order_ref, grad_ref, gain_ref, own_ref = refs[:4]
    rows_ref, sums_ref = refs[-2:]
    others = refs[4:-2]
    count = len(others) // 2
    rows = own_ref.shape[0]
    z = order_ref[0]
    for i in range(count + 1):
        at = lax.rem(z + count + 1 - i, count + 1) * rows
        if i == 0:
            piece = own_ref[...]
        else:
            piece = others[i - 1][...] + others[2 * count - i][...]
        rows_ref[pl.ds(pl.multiple_of(at, rows), rows), :] = piece
    values = rows_ref[...].astype(jnp.float32)
    sums_ref[0:1, :] = row_of(fold(values * values))
    sums_ref[1:2, :] = row_of(fold(values * grad_ref[...] * gain_ref[...]))


def row_sums(z, grad, gain, own, others):
    stream, width = grad.shape
    whole = pl.BlockSpec(memory_space=pltpu.VMEM)
    return pl.pallas_call(
        sums_kernel,
        in_specs=[pl.BlockSpec(memory_space=pltpu.SMEM)] + [whole] * (3 + len(others)),
        out_specs=[whole, whole],
        out_shape=[
            jax.ShapeDtypeStruct((stream, width), jnp.bfloat16),
            jax.ShapeDtypeStruct((2, stream), jnp.float32),
        ],
        compiler_params=pltpu.CompilerParams(vmem_limit_bytes=56 * 1024 * 1024),
        cost_estimate=pl.CostEstimate(
            flops=8 * stream * width, bytes_accessed=10 * stream * width, transcendentals=0
        ),
    )(z, grad, gain, own, *others)


def image_kernel(*refs):
    grad_ref, gain_ref, rows_ref, cot_ref = refs[:4]
    embed_ref, here_ref, there_ref, small_ref = refs[-4:]
    parts = [r[...] for r in refs[4:-4]]
    while len(parts) > 1:
        parts = [parts[i] + parts[i + 1] for i in range(0, len(parts), 2)]
    stream, width = rows_ref.shape
    inv_row = lax.rsqrt(parts[0][0:1, :] / D + EPSILON)
    mean_row = inv_row * inv_row * inv_row * parts[0][1:2, :] / D
    inv = columns_of(inv_row, stream)
    mean = columns_of(mean_row, stream)
    for i in range(width // LANES):
        at = slice(i * LANES, (i + 1) * LANES)
        values = rows_ref[:, at].astype(jnp.float32)
        scaled = grad_ref[:, at] * inv
        embed = (scaled * gain_ref[:, at] - values * mean).astype(jnp.bfloat16)
        embed_ref[:, at] = embed
        small_ref[0:1, at] = jnp.sum(scaled * values, 0, keepdims=True)
        small_ref[1:2, at] = jnp.sum(embed.astype(jnp.float32), 0, keepdims=True)
    lanes = cot_ref.shape[1]
    wide = [inv] * (lanes // LANES) if lanes >= LANES else [inv[:, :lanes]]
    cot = (cot_ref[...].astype(jnp.float32) * jnp.concatenate(wide, 1)).astype(jnp.bfloat16)
    moment = lax.dot_general(
        rows_ref[...], cot, (((0,), (0,)), ((), ())), preferred_element_type=jnp.float32
    )
    share = here_ref.shape[1]
    here_ref[...] = moment[:, :share]
    there_ref[...] = moment[:, share:].astype(jnp.bfloat16)


def image_grads(grad, gain, rows, cot, sums):
    stream, width = grad.shape
    share = cot.shape[1] // 2
    whole = pl.BlockSpec(memory_space=pltpu.VMEM)
    return pl.pallas_call(
        image_kernel,
        in_specs=[whole] * (4 + len(sums)),
        out_specs=[whole] * 4,
        out_shape=[
            jax.ShapeDtypeStruct((stream, width), jnp.bfloat16),
            jax.ShapeDtypeStruct((width, share), jnp.float32),
            jax.ShapeDtypeStruct((width, share), jnp.bfloat16),
            jax.ShapeDtypeStruct((2, width), jnp.float32),
        ],
        compiler_params=pltpu.CompilerParams(vmem_limit_bytes=56 * 1024 * 1024),
        cost_estimate=pl.CostEstimate(
            flops=4 * stream * width * share, bytes_accessed=8 * stream * width, transcendentals=0
        ),
    )(grad, gain, rows, cot, *sums)


def weight_kernel(act_ref, grad_ref, out_ref):
    step = act_ref.shape[1]
    groups = grad_ref.shape[1] // LANES
    product = lax.dot_general(
        act_ref[...], grad_ref[...], (((0,), (0,)), ((), ())), preferred_element_type=jnp.float32
    )
    for c in range(groups):
        out_ref[pl.ds(c, step, stride=groups), :] = product[:, c * LANES : (c + 1) * LANES]


def weight_product(act, grad):
    rows, features = act.shape
    width = grad.shape[1]
    groups = width // LANES
    step = 256
    return pl.pallas_call(
        weight_kernel,
        grid=(features // step,),
        in_specs=[
            pl.BlockSpec((rows, step), lambda i: (0, i)),
            pl.BlockSpec((rows, width), lambda i: (0, 0)),
        ],
        out_specs=pl.BlockSpec((step * groups, LANES), lambda i: (i, 0)),
        out_shape=jax.ShapeDtypeStruct((features * groups, LANES), jnp.float32),
        compiler_params=pltpu.CompilerParams(vmem_limit_bytes=32 * 1024 * 1024),
        cost_estimate=pl.CostEstimate(
            flops=2 * rows * features * width,
            bytes_accessed=4 * features * width + 2 * rows * (features + width),
            transcendentals=0,
        ),
    )(act, grad)


def on_device(
    vis_hidden,
    proj_weight,
    proj_bias,
    text_embed,
    norm_gain,
    key_weight,
    key_cotangent,
    tile_counts,
    text_counts,
    owner_map,
):
    f32, bf16 = jnp.float32, jnp.bfloat16
    n_sec, n_seq, n_tp = (lax.axis_size(a) for a in ("sec", "seq", "tp"))
    core, z, t = (lax.axis_index(a) for a in ("sec", "seq", "tp"))
    block_rows, features = vis_hidden.shape
    columns = proj_weight.shape[1]
    col_half = columns // n_sec
    stream = block_rows * n_tp
    own = stream // n_seq
    part_rows = block_rows // n_sec
    sub = part_rows // n_seq
    keys = key_weight.shape[1]
    key_half = keys // n_sec
    seq_len = text_embed.shape[0]
    tiles = stream // TILE

    text_values = text_embed.astype(f32)
    text_sq = total(jnp.sum(text_values * text_values, 1), "tp")

    mine = lax.dynamic_slice_in_dim(vis_hidden, core * part_rows, part_rows, 0)
    act = jax.nn.gelu(mine.astype(f32), approximate=False).astype(bf16)
    pieces = [act] + [swap(act, "tp", m) for m in range(1, n_tp)]
    pieces = [p.reshape(n_seq, sub, features) for p in pieces]

    is_mine = owner_map == z
    image_count = TILE * jnp.sum(jnp.where(is_mine, tile_counts, 0))
    text_count = jnp.sum(jnp.where(is_mine, text_counts, 0))
    text_inv = lax.rsqrt(text_sq / D + EPSILON)
    text_scale = jnp.where(jnp.arange(seq_len) < text_count, text_inv, 0.0)
    cot_half = lax.dynamic_slice_in_dim(key_cotangent, core * key_half, key_half, 1)
    cot_padded = jnp.concatenate([cot_half, jnp.zeros((MAXT * TILE, key_half), bf16)], 0)
    cot_text = lax.dynamic_slice_in_dim(cot_padded, image_count, seq_len, 0)
    cot_text = (cot_text.astype(f32) * text_scale[:, None]).astype(bf16)
    weight_half = lax.dynamic_slice_in_dim(key_weight, core * key_half, key_half, 1)
    moment, gain_text = text_product(text_embed, cot_text, weight_half)
    if n_seq != moment.shape[0]:
        share = key_half // n_seq
        moment = moment.reshape(-1, columns, LANES // share, share).transpose(0, 2, 1, 3)
        moment = moment.reshape(n_seq, columns, share)
    moment = lax.psum_scatter(moment, "seq", scatter_dimension=0, tiled=False)

    starts = jnp.cumsum(tile_counts) - tile_counts
    tile_ids = jnp.arange(tiles, dtype=jnp.int32)[:, None]
    held = (tile_ids >= starts[None]) & (tile_ids < (starts + tile_counts)[None])
    tile_owner = jnp.sum(jnp.where(held, owner_map[None], 0), 1)
    tile_place = jnp.sum(jnp.where(held, tile_ids - starts[None], 0), 1)
    share = key_half // n_tp
    from_col = (core * n_tp + t) * share
    front = lax.dynamic_slice_in_dim(key_cotangent[: MAXT * TILE], from_col, share, 1)
    front = front.reshape(MAXT, TILE, share)
    given = jnp.zeros((tiles, TILE, share), bf16)
    for place in range(MAXT):
        chosen = (tile_owner == z) & (tile_place == place)
        given = jnp.where(chosen[:, None, None], front[place][None], given)
    given = given.reshape(n_tp, n_sec, n_seq, sub, share).transpose(2, 1, 0, 3, 4)
    taken = butterfly(given.reshape(stream, share), ("seq",))
    taken = [taken] + [swap(taken, "tp", m) for m in range(1, n_tp)]
    half_cot = jnp.concatenate(in_order(taken, t), 1)
    other_cot = swap(half_cot, "sec", 1)
    image_cot = jnp.concatenate(in_order([half_cot, other_cot], core), 1)
    weight_rows = lax.dynamic_slice_in_dim(key_weight, core * col_half, col_half, 0)
    normed_grad = lax.dot_general(
        image_cot, weight_rows, (((1,), (1,)), ((), ())), preferred_element_type=f32
    )
    key_share = key_half // n_seq
    cot_own = jnp.concatenate(
        [lax.dynamic_slice_in_dim(c, z * key_share, key_share, 1) for c in (half_cot, other_cot)], 1
    )

    images = []
    for first in range(0, n_tp, 2):
        chunk = jnp.stack(pieces[first : first + 2], 1).reshape(2 * part_rows, features)
        partial = jnp.dot(chunk, proj_weight, preferred_element_type=f32).astype(bf16)
        summed = reduce_to_owner(partial.reshape(n_seq, 2 * sub, columns), "seq")
        images += list((summed + proj_bias).astype(bf16).reshape(2, sub, columns))
    image_mine = jnp.concatenate(in_order(images, t), 0)
    low, high = image_mine[:, :col_half], image_mine[:, col_half:]
    first_core = core == 0
    came = swap(jnp.where(first_core, high, low), "sec", 1)
    image = jnp.concatenate(in_order([jnp.where(first_core, low, high), came], core), 0)

    act_half = jnp.stack(in_order(pieces, t), 1)
    act_pair = in_order([act_half, swap(act_half, "sec", 1)], core)
    act_full = jnp.stack(act_pair, 1).reshape(stream, features)

    gain_half = lax.dynamic_slice_in_dim(norm_gain, core * col_half, col_half, 0)[None]
    if n_seq <= 4:
        up, down = along_line(image, "seq")
        rows, sums = row_sums(z[None], normed_grad, gain_half, image, up + down)
    else:
        gathered = lax.all_gather(image, "seq", axis=0, tiled=True)
        rows, sums = row_sums(jnp.zeros((1,), jnp.int32), normed_grad, gain_half, gathered, [])
    sums = sums + swap(sums, "sec", 1)
    sums = [sums] + [swap(sums, "tp", m) for m in range(1, n_tp)]
    embed_grad, here, there, small = image_grads(normed_grad, gain_half, rows, cot_own, sums)
    there = swap(there, "sec", 1)
    small_other = swap(small, "sec", 1)
    product = weight_product(act_full, embed_grad)
    proj_weight_grad = product.reshape(features, 1, 1, col_half)

    both = in_order([here, there.astype(f32)], core)
    key_weight_grad = (moment.astype(f32) + jnp.concatenate(both, 0)) * norm_gain[:, None]
    gain_image, proj_bias_grad = jnp.concatenate(in_order([small, small_other], core), 1)

    key_bias_part = jnp.sum(key_cotangent.astype(f32), 0)
    early = jnp.concatenate([gain_text[0], jnp.where(core == 0, key_bias_part, 0.0)])
    early = butterfly(early, ("sec", "seq"))
    gain_grad = early[:columns] + gain_image
    key_bias_grad = early[columns:]
    return (proj_weight_grad, proj_bias_grad, key_weight_grad, key_bias_grad, gain_grad)


def solution(mesh):
    placed = (
        P("tp", "seq"),
        P("seq", "tp"),
        P("tp"),
        P("seq", "tp"),
        P("tp"),
        P("tp", None),
        P("seq", None),
        P(),
        P(),
        P(),
    )
    return jax.shard_map(
        on_device,
        mesh=mesh,
        in_specs=placed,
        out_specs=(P("seq", "tp", "sec", None), P("tp"), P("tp", ("sec", "seq")), P(), P("tp")),
        check_vma=False,
    )
```

```python
import jax
import jax.numpy as jnp
from jax import lax
from jax.experimental import pallas as pl
from jax.experimental.pallas import tpu as pltpu
from jax.sharding import PartitionSpec as P

D = 8192
TILE = 256
MAXT = 2
LANES = 128
EPSILON = 1e-06


def swap(x, axis, mask):
    count = lax.axis_size(axis)
    return lax.ppermute(x, axis, [(i, i ^ mask) for i in range(count)])


def total(x, axis):
    pieces = [x] + [swap(x, axis, m) for m in range(1, lax.axis_size(axis))]
    while len(pieces) > 1:
        pieces = [pieces[i] + pieces[i + 1] for i in range(0, len(pieces), 2)]
    return pieces[0]


def butterfly(x, axes):
    for axis in axes:
        mask = 1
        while mask < lax.axis_size(axis):
            x = x + swap(x, axis, mask)
            mask *= 2
    return x


def in_order(pieces, index):
    pieces = list(pieces)
    mask = 1
    while mask < len(pieces):
        odd = (index & mask) != 0
        pieces = [jnp.where(odd, pieces[m ^ mask], pieces[m]) for m in range(len(pieces))]
        mask *= 2
    return pieces


def reduce_to_owner(parts, axis):
    index = lax.axis_index(axis)
    count = parts.shape[0]
    while count > 1:
        pairs = parts.reshape(count // 2, 2, *parts.shape[1:])
        mask = lax.axis_size(axis) // count
        bit = (index // mask) % 2
        sent = lax.dynamic_index_in_dim(pairs, 1 - bit, 1, keepdims=False)
        kept = lax.dynamic_index_in_dim(pairs, bit, 1, keepdims=False)
        came = swap(sent.astype(jnp.bfloat16), axis, mask)
        parts = kept.astype(jnp.float32) + came.astype(jnp.float32)
        count //= 2
    return parts[0]


def along_line(x, axis):
    count = lax.axis_size(axis)
    up, down = [], []
    right = left = x
    for i in range(1, count):
        right = lax.ppermute(right, axis, [(j, j + 1) for j in range(i - 1, count - 1)])
        left = lax.ppermute(left, axis, [(j, j - 1) for j in range(1, count - i + 1)])
        up.append(right)
        down.append(left)
    return up, down


def columns_of(row, count):
    parts = []
    for i in range(count // LANES):
        part = row[:, i * LANES : (i + 1) * LANES]
        parts.append(jnp.broadcast_to(part, (LANES, LANES)).T)
    return jnp.concatenate(parts, 0)


def row_of(folded):
    count = folded.shape[0]
    parts = [
        jnp.sum(folded[i * LANES : (i + 1) * LANES, :].T, 0, keepdims=True)
        for i in range(count // LANES)
    ]
    return jnp.concatenate(parts, 1)


def fold(values):
    width = values.shape[1]
    out = values[:, :LANES]
    for i in range(1, width // LANES):
        out = out + values[:, i * LANES : (i + 1) * LANES]
    return out


def text_kernel(text_ref, cot_ref, weight_ref, moment_ref, gain_ref):
    moment = lax.dot_general(
        text_ref[...], cot_ref[...], (((0,), (0,)), ((), ())), preferred_element_type=jnp.float32
    )
    for i in range(moment_ref.shape[0]):
        moment_ref[i] = moment[:, i * LANES : (i + 1) * LANES].astype(jnp.bfloat16)
    gain_ref[...] = row_of(fold(moment * weight_ref[...].astype(jnp.float32)))


def text_product(text, cot, weight):
    seq_len, columns = text.shape
    width = cot.shape[1]
    groups = width // LANES
    step = 256
    return pl.pallas_call(
        text_kernel,
        grid=(columns // step,),
        in_specs=[
            pl.BlockSpec((seq_len, step), lambda i: (0, i)),
            pl.BlockSpec((seq_len, width), lambda i: (0, 0)),
            pl.BlockSpec((step, width), lambda i: (i, 0)),
        ],
        out_specs=[
            pl.BlockSpec((groups, step, LANES), lambda i: (0, i, 0)),
            pl.BlockSpec((1, step), lambda i: (0, i)),
        ],
        out_shape=[
            jax.ShapeDtypeStruct((groups, columns, LANES), jnp.bfloat16),
            jax.ShapeDtypeStruct((1, columns), jnp.float32),
        ],
        compiler_params=pltpu.CompilerParams(vmem_limit_bytes=32 * 1024 * 1024),
        cost_estimate=pl.CostEstimate(
            flops=2 * seq_len * columns * width,
            bytes_accessed=2 * (seq_len * (columns + width) + 2 * columns * width),
            transcendentals=0,
        ),
    )(text, cot, weight)


def sums_kernel(rows_ref, grad_ref, gain_ref, sums_ref):
    values = rows_ref[...].astype(jnp.float32)
    more = sums_ref.shape[1] - values.shape[0]
    for i, terms in enumerate((values * values, values * grad_ref[...] * gain_ref[...])):
        folded = jnp.concatenate([fold(terms), jnp.zeros((more, LANES), jnp.float32)], 0)
        sums_ref[i : i + 1, :] = row_of(folded)


def row_sums(rows, grad, gain):
    count, width = rows.shape
    padded = -(-count // LANES) * LANES
    whole = pl.BlockSpec(memory_space=pltpu.VMEM)
    return pl.pallas_call(
        sums_kernel,
        in_specs=[whole] * 3,
        out_specs=whole,
        out_shape=jax.ShapeDtypeStruct((2, padded), jnp.float32),
        compiler_params=pltpu.CompilerParams(vmem_limit_bytes=16 * 1024 * 1024),
        cost_estimate=pl.CostEstimate(
            flops=8 * count * width, bytes_accessed=6 * count * width, transcendentals=0
        ),
    )(rows, grad, gain)


def image_kernel(*refs):
    order_ref, grad_ref, gain_ref, cot_ref, sums_ref, own_ref = refs[:6]
    embed_ref, here_ref, there_ref, small_ref, rows_ref = refs[-5:]
    others = refs[6:-5]
    count = len(others) // 2
    rows = own_ref.shape[0]
    stream, width = embed_ref.shape
    for i in range(count + 1):
        at = lax.rem(order_ref[0] + count + 1 - i, count + 1) * rows
        if i == 0:
            piece = own_ref[...]
        else:
            piece = others[i - 1][...] + others[2 * count - i][...]
        rows_ref[pl.ds(pl.multiple_of(at, rows), rows), :] = piece
    groups = sums_ref.shape[0]
    inv, mean = [], []
    for i in range(groups):
        inv_row = lax.rsqrt(sums_ref[i, 0:1, :] / D + EPSILON)
        mean_row = inv_row * inv_row * inv_row * sums_ref[i, 1:2, :] / D
        inv.append(columns_of(inv_row, inv_row.shape[1])[: stream // groups])
        mean.append(columns_of(mean_row, mean_row.shape[1])[: stream // groups])
    inv = jnp.concatenate(inv, 0)
    mean = jnp.concatenate(mean, 0)
    for i in range(width // LANES):
        at = slice(i * LANES, (i + 1) * LANES)
        values = rows_ref[:, at].astype(jnp.float32)
        scaled = grad_ref[:, at] * inv
        embed = (scaled * gain_ref[:, at] - values * mean).astype(jnp.bfloat16)
        embed_ref[:, at] = embed
        small_ref[0:1, at] = jnp.sum(scaled * values, 0, keepdims=True)
        small_ref[1:2, at] = jnp.sum(embed.astype(jnp.float32), 0, keepdims=True)
    lanes = cot_ref.shape[1]
    wide = [inv] * (lanes // LANES) if lanes >= LANES else [inv[:, :lanes]]
    cot = (cot_ref[...].astype(jnp.float32) * jnp.concatenate(wide, 1)).astype(jnp.bfloat16)
    moment = lax.dot_general(
        rows_ref[...], cot, (((0,), (0,)), ((), ())), preferred_element_type=jnp.float32
    )
    share = here_ref.shape[1]
    here_ref[...] = moment[:, :share]
    there_ref[...] = moment[:, share:].astype(jnp.bfloat16)


def image_grads(z, grad, gain, cot, sums, own, others):
    stream, width = grad.shape
    share = cot.shape[1] // 2
    whole = pl.BlockSpec(memory_space=pltpu.VMEM)
    return pl.pallas_call(
        image_kernel,
        in_specs=[pl.BlockSpec(memory_space=pltpu.SMEM)] + [whole] * (5 + len(others)),
        out_specs=[whole] * 4,
        out_shape=[
            jax.ShapeDtypeStruct((stream, width), jnp.bfloat16),
            jax.ShapeDtypeStruct((width, share), jnp.float32),
            jax.ShapeDtypeStruct((width, share), jnp.bfloat16),
            jax.ShapeDtypeStruct((2, width), jnp.float32),
        ],
        scratch_shapes=[pltpu.VMEM((stream, width), jnp.bfloat16)],
        compiler_params=pltpu.CompilerParams(vmem_limit_bytes=56 * 1024 * 1024),
        cost_estimate=pl.CostEstimate(
            flops=4 * stream * width * share, bytes_accessed=8 * stream * width, transcendentals=0
        ),
    )(z, grad, gain, cot, sums, own, *others)


def weight_kernel(act_ref, grad_ref, out_ref):
    step = act_ref.shape[1]
    groups = grad_ref.shape[1] // LANES
    product = lax.dot_general(
        act_ref[...], grad_ref[...], (((0,), (0,)), ((), ())), preferred_element_type=jnp.float32
    )
    for c in range(groups):
        out_ref[pl.ds(c, step, stride=groups), :] = product[:, c * LANES : (c + 1) * LANES]


def weight_product(act, grad):
    rows, features = act.shape
    width = grad.shape[1]
    groups = width // LANES
    step = 256
    return pl.pallas_call(
        weight_kernel,
        grid=(features // step,),
        in_specs=[
            pl.BlockSpec((rows, step), lambda i: (0, i)),
            pl.BlockSpec((rows, width), lambda i: (0, 0)),
        ],
        out_specs=pl.BlockSpec((step * groups, LANES), lambda i: (i, 0)),
        out_shape=jax.ShapeDtypeStruct((features * groups, LANES), jnp.float32),
        compiler_params=pltpu.CompilerParams(vmem_limit_bytes=32 * 1024 * 1024),
        cost_estimate=pl.CostEstimate(
            flops=2 * rows * features * width,
            bytes_accessed=4 * features * width + 2 * rows * (features + width),
            transcendentals=0,
        ),
    )(act, grad)


def on_device(
    vis_hidden,
    proj_weight,
    proj_bias,
    text_embed,
    norm_gain,
    key_weight,
    key_cotangent,
    tile_counts,
    text_counts,
    owner_map,
):
    f32, bf16 = jnp.float32, jnp.bfloat16
    n_sec, n_seq, n_tp = (lax.axis_size(a) for a in ("sec", "seq", "tp"))
    core, z, t = (lax.axis_index(a) for a in ("sec", "seq", "tp"))
    block_rows, features = vis_hidden.shape
    columns = proj_weight.shape[1]
    col_half = columns // n_sec
    stream = block_rows * n_tp
    own = stream // n_seq
    part_rows = block_rows // n_sec
    sub = part_rows // n_seq
    keys = key_weight.shape[1]
    key_half = keys // n_sec
    seq_len = text_embed.shape[0]
    tiles = stream // TILE

    mine = lax.dynamic_slice_in_dim(vis_hidden, core * part_rows, part_rows, 0)
    act = jax.nn.gelu(mine.astype(f32), approximate=False).astype(bf16)
    pieces = [act] + [swap(act, "tp", m) for m in range(1, n_tp)]
    pieces = [p.reshape(n_seq, sub, features) for p in pieces]

    images = []
    for first, last in ((0, 1), (1, 2), (2, n_tp)):
        blocks = last - first
        chunk = jnp.stack(pieces[first:last], 1).reshape(blocks * part_rows, features)
        partial = jnp.dot(chunk, proj_weight, preferred_element_type=f32).astype(bf16)
        summed = reduce_to_owner(partial.reshape(n_seq, blocks * sub, columns), "seq")
        images += list((summed + proj_bias).astype(bf16).reshape(blocks, sub, columns))
    image_mine = jnp.concatenate(in_order(images, t), 0)
    low, high = image_mine[:, :col_half], image_mine[:, col_half:]
    first_core = core == 0
    came = swap(jnp.where(first_core, high, low), "sec", 1)
    image = jnp.concatenate(in_order([jnp.where(first_core, low, high), came], core), 0)

    act, text_embed, key_cotangent = lax.optimization_barrier((act, text_embed, key_cotangent))
    text_values = text_embed.astype(f32)
    text_sq = total(jnp.sum(text_values * text_values, 1), "tp")
    is_mine = owner_map == z
    image_count = TILE * jnp.sum(jnp.where(is_mine, tile_counts, 0))
    text_count = jnp.sum(jnp.where(is_mine, text_counts, 0))
    text_inv = lax.rsqrt(text_sq / D + EPSILON)
    text_scale = jnp.where(jnp.arange(seq_len) < text_count, text_inv, 0.0)
    cot_half = lax.dynamic_slice_in_dim(key_cotangent, core * key_half, key_half, 1)
    cot_padded = jnp.concatenate([cot_half, jnp.zeros((MAXT * TILE, key_half), bf16)], 0)
    cot_text = lax.dynamic_slice_in_dim(cot_padded, image_count, seq_len, 0)
    cot_text = (cot_text.astype(f32) * text_scale[:, None]).astype(bf16)
    weight_half = lax.dynamic_slice_in_dim(key_weight, core * key_half, key_half, 1)
    moment, gain_text = text_product(text_embed, cot_text, weight_half)
    if n_seq != moment.shape[0]:
        share = key_half // n_seq
        moment = moment.reshape(-1, columns, LANES // share, share).transpose(0, 2, 1, 3)
        moment = moment.reshape(n_seq, columns, share)
    moment, image_mine = lax.optimization_barrier((moment, image_mine))
    moment = lax.psum_scatter(moment, "seq", scatter_dimension=0, tiled=False)

    starts = jnp.cumsum(tile_counts) - tile_counts
    tile_ids = jnp.arange(tiles, dtype=jnp.int32)[:, None]
    held = (tile_ids >= starts[None]) & (tile_ids < (starts + tile_counts)[None])
    tile_owner = jnp.sum(jnp.where(held, owner_map[None], 0), 1)
    tile_place = jnp.sum(jnp.where(held, tile_ids - starts[None], 0), 1)
    share = key_half // n_tp
    from_col = (core * n_tp + t) * share
    front = lax.dynamic_slice_in_dim(key_cotangent[: MAXT * TILE], from_col, share, 1)
    front = front.reshape(MAXT, TILE, share)
    given = jnp.zeros((tiles, TILE, share), bf16)
    for place in range(MAXT):
        chosen = (tile_owner == z) & (tile_place == place)
        given = jnp.where(chosen[:, None, None], front[place][None], given)
    given = given.reshape(n_tp, n_sec, n_seq, sub, share).transpose(2, 1, 0, 3, 4)
    taken = butterfly(given.reshape(stream, share), ("seq",))
    taken = [taken] + [swap(taken, "tp", m) for m in range(1, n_tp)]
    half_cot = jnp.concatenate(in_order(taken, t), 1)
    other_cot = swap(half_cot, "sec", 1)
    image_cot = jnp.concatenate(in_order([half_cot, other_cot], core), 1)
    weight_rows = lax.dynamic_slice_in_dim(key_weight, core * col_half, col_half, 0)
    normed_grad = lax.dot_general(
        image_cot, weight_rows, (((1,), (1,)), ((), ())), preferred_element_type=f32
    )
    key_share = key_half // n_seq
    cot_own = jnp.concatenate(
        [lax.dynamic_slice_in_dim(c, z * key_share, key_share, 1) for c in (half_cot, other_cot)], 1
    )

    act_half = jnp.stack(in_order(pieces, t), 1)
    act_pair = in_order([act_half, swap(act_half, "sec", 1)], core)
    act_full = jnp.stack(act_pair, 1).reshape(stream, features)

    own_cot = lax.dynamic_slice_in_dim(image_cot, (z * n_sec + core) * (own // n_sec), own // n_sec, 0)
    own_grad = lax.dot_general(
        own_cot, key_weight, (((1,), (1,)), ((), ())), preferred_element_type=f32
    )
    sums = total(row_sums(image_mine, own_grad, norm_gain[None]), "tp")
    gain_half = lax.dynamic_slice_in_dim(norm_gain, core * col_half, col_half, 0)[None]
    if n_seq <= 4:
        up, down = along_line(image, "seq")
        sums = jnp.stack(in_order([sums] + [swap(sums, "seq", m) for m in range(1, n_seq)], z), 0)
        others = up + down
    else:
        image = lax.all_gather(image, "seq", axis=0, tiled=True)
        sums = lax.all_gather(sums, "seq", axis=0, tiled=False)
        others = []
    sums = jnp.stack(in_order([sums, swap(sums, "sec", 1)], core), 1)
    sums = sums.reshape(n_seq * n_sec, *sums.shape[2:])
    embed_grad, here, there, small = image_grads(
        z[None], normed_grad, gain_half, cot_own, sums, image, others
    )
    there = swap(there, "sec", 1)
    small_other = swap(small, "sec", 1)
    product = weight_product(act_full, embed_grad)
    proj_weight_grad = product.reshape(features, 1, 1, col_half)

    both = in_order([here, there.astype(f32)], core)
    key_weight_grad = (moment.astype(f32) + jnp.concatenate(both, 0)) * norm_gain[:, None]
    gain_image, proj_bias_grad = jnp.concatenate(in_order([small, small_other], core), 1)

    key_bias_part = jnp.sum(key_cotangent.astype(f32), 0)
    early = jnp.concatenate([gain_text[0], jnp.where(core == 0, key_bias_part, 0.0)])
    early = total(early, "seq") if n_seq <= 4 else butterfly(early, ("seq",))
    early = total(early, "sec")
    gain_grad = early[:columns] + gain_image
    key_bias_grad = early[columns:]
    return (proj_weight_grad, proj_bias_grad, key_weight_grad, key_bias_grad, gain_grad)


def solution(mesh):
    placed = (
        P("tp", "seq"),
        P("seq", "tp"),
        P("tp"),
        P("seq", "tp"),
        P("tp"),
        P("tp", None),
        P("seq", None),
        P(),
        P(),
        P(),
    )
    return jax.shard_map(
        on_device,
        mesh=mesh,
        in_specs=placed,
        out_specs=(P("seq", "tp", "sec", None), P("tp"), P("tp", ("sec", "seq")), P(), P("tp")),
        check_vma=False,
    )
```

```python
import jax
import jax.numpy as jnp
from jax import lax
from jax.experimental import pallas as pl
from jax.experimental.pallas import tpu as pltpu
from jax.sharding import PartitionSpec as P

D = 8192
TILE = 256
MAXT = 2
LANES = 128
EPSILON = 1e-06


def swap(x, axis, mask):
    count = lax.axis_size(axis)
    return lax.ppermute(x, axis, [(i, i ^ mask) for i in range(count)])


def total(x, axis):
    pieces = [x] + [swap(x, axis, m) for m in range(1, lax.axis_size(axis))]
    while len(pieces) > 1:
        pieces = [pieces[i] + pieces[i + 1] for i in range(0, len(pieces), 2)]
    return pieces[0]


def butterfly(x, axes):
    for axis in axes:
        mask = 1
        while mask < lax.axis_size(axis):
            x = x + swap(x, axis, mask)
            mask *= 2
    return x


def in_order(pieces, index):
    pieces = list(pieces)
    mask = 1
    while mask < len(pieces):
        odd = (index & mask) != 0
        pieces = [jnp.where(odd, pieces[m ^ mask], pieces[m]) for m in range(len(pieces))]
        mask *= 2
    return pieces


def together(*values):
    return lax.optimization_barrier(values)


def reduce_to_owner(parts, axis, then=None):
    index = lax.axis_index(axis)
    count = parts.shape[0]
    after = None
    while count > 1:
        pairs = parts.reshape(count // 2, 2, *parts.shape[1:])
        mask = lax.axis_size(axis) // count
        bit = (index // mask) % 2
        sent = lax.dynamic_index_in_dim(pairs, 1 - bit, 1, keepdims=False)
        kept = lax.dynamic_index_in_dim(pairs, bit, 1, keepdims=False)
        came = swap(sent.astype(jnp.bfloat16), axis, mask)
        if after is None and then is not None:
            came, *after = together(came, *then)
        parts = kept.astype(jnp.float32) + came.astype(jnp.float32)
        count //= 2
    return parts[0], after


def along_line(x, axis):
    count = lax.axis_size(axis)
    up, down = [], []
    right = left = x
    for i in range(1, count):
        right = lax.ppermute(right, axis, [(j, j + 1) for j in range(i - 1, count - 1)])
        left = lax.ppermute(left, axis, [(j, j - 1) for j in range(1, count - i + 1)])
        up.append(right)
        down.append(left)
    return up, down


def columns_of(row, count):
    parts = []
    for i in range(count // LANES):
        part = row[:, i * LANES : (i + 1) * LANES]
        parts.append(jnp.broadcast_to(part, (LANES, LANES)).T)
    return jnp.concatenate(parts, 0)


def row_of(folded):
    count = folded.shape[0]
    parts = [
        jnp.sum(folded[i * LANES : (i + 1) * LANES, :].T, 0, keepdims=True)
        for i in range(count // LANES)
    ]
    return jnp.concatenate(parts, 1)


def fold(values):
    width = values.shape[1]
    out = values[:, :LANES]
    for i in range(1, width // LANES):
        out = out + values[:, i * LANES : (i + 1) * LANES]
    return out


def text_kernel(text_ref, cot_ref, weight_ref, moment_ref, gain_ref):
    moment = lax.dot_general(
        text_ref[...], cot_ref[...], (((0,), (0,)), ((), ())), preferred_element_type=jnp.float32
    )
    for i in range(moment_ref.shape[0]):
        moment_ref[i] = moment[:, i * LANES : (i + 1) * LANES].astype(jnp.bfloat16)
    gain_ref[...] = row_of(fold(moment * weight_ref[...].astype(jnp.float32)))


def text_product(text, cot, weight):
    seq_len, columns = text.shape
    width = cot.shape[1]
    groups = width // LANES
    step = 256
    return pl.pallas_call(
        text_kernel,
        grid=(columns // step,),
        in_specs=[
            pl.BlockSpec((seq_len, step), lambda i: (0, i)),
            pl.BlockSpec((seq_len, width), lambda i: (0, 0)),
            pl.BlockSpec((step, width), lambda i: (i, 0)),
        ],
        out_specs=[
            pl.BlockSpec((groups, step, LANES), lambda i: (0, i, 0)),
            pl.BlockSpec((1, step), lambda i: (0, i)),
        ],
        out_shape=[
            jax.ShapeDtypeStruct((groups, columns, LANES), jnp.bfloat16),
            jax.ShapeDtypeStruct((1, columns), jnp.float32),
        ],
        compiler_params=pltpu.CompilerParams(vmem_limit_bytes=32 * 1024 * 1024),
        cost_estimate=pl.CostEstimate(
            flops=2 * seq_len * columns * width,
            bytes_accessed=2 * (seq_len * (columns + width) + 2 * columns * width),
            transcendentals=0,
        ),
    )(text, cot, weight)


def sums_kernel(rows_ref, grad_ref, gain_ref, sums_ref):
    values = rows_ref[...].astype(jnp.float32)
    more = sums_ref.shape[1] - values.shape[0]
    for i, terms in enumerate((values * values, values * grad_ref[...] * gain_ref[...])):
        folded = jnp.concatenate([fold(terms), jnp.zeros((more, LANES), jnp.float32)], 0)
        sums_ref[i : i + 1, :] = row_of(folded)


def row_sums(rows, grad, gain):
    count, width = rows.shape
    padded = -(-count // LANES) * LANES
    whole = pl.BlockSpec(memory_space=pltpu.VMEM)
    return pl.pallas_call(
        sums_kernel,
        in_specs=[whole] * 3,
        out_specs=whole,
        out_shape=jax.ShapeDtypeStruct((2, padded), jnp.float32),
        compiler_params=pltpu.CompilerParams(vmem_limit_bytes=16 * 1024 * 1024),
        cost_estimate=pl.CostEstimate(
            flops=8 * count * width, bytes_accessed=6 * count * width, transcendentals=0
        ),
    )(rows, grad, gain)


def image_kernel(*refs):
    order_ref, grad_ref, gain_ref, cot_ref, sums_ref, own_ref = refs[:6]
    embed_ref, here_ref, there_ref, small_ref, rows_ref = refs[-5:]
    others = refs[6:-5]
    count = len(others) // 2
    rows = own_ref.shape[0]
    stream, width = embed_ref.shape
    for i in range(count + 1):
        at = lax.rem(order_ref[0] + count + 1 - i, count + 1) * rows
        if i == 0:
            piece = own_ref[...]
        else:
            piece = others[i - 1][...] + others[2 * count - i][...]
        rows_ref[pl.ds(pl.multiple_of(at, rows), rows), :] = piece
    groups = sums_ref.shape[0]
    inv, mean = [], []
    for i in range(groups):
        inv_row = lax.rsqrt(sums_ref[i, 0:1, :] / D + EPSILON)
        mean_row = inv_row * inv_row * inv_row * sums_ref[i, 1:2, :] / D
        inv.append(columns_of(inv_row, inv_row.shape[1])[: stream // groups])
        mean.append(columns_of(mean_row, mean_row.shape[1])[: stream // groups])
    inv = jnp.concatenate(inv, 0)
    mean = jnp.concatenate(mean, 0)
    for i in range(width // LANES):
        at = slice(i * LANES, (i + 1) * LANES)
        values = rows_ref[:, at].astype(jnp.float32)
        scaled = grad_ref[:, at] * inv
        embed = (scaled * gain_ref[:, at] - values * mean).astype(jnp.bfloat16)
        embed_ref[:, at] = embed
        small_ref[0:1, at] = jnp.sum(scaled * values, 0, keepdims=True)
        small_ref[1:2, at] = jnp.sum(embed.astype(jnp.float32), 0, keepdims=True)
    lanes = cot_ref.shape[1]
    wide = [inv] * (lanes // LANES) if lanes >= LANES else [inv[:, :lanes]]
    cot = (cot_ref[...].astype(jnp.float32) * jnp.concatenate(wide, 1)).astype(jnp.bfloat16)
    moment = lax.dot_general(
        rows_ref[...], cot, (((0,), (0,)), ((), ())), preferred_element_type=jnp.float32
    )
    share = here_ref.shape[1]
    here_ref[...] = moment[:, :share]
    there_ref[...] = moment[:, share:].astype(jnp.bfloat16)


def image_grads(z, grad, gain, cot, sums, own, others):
    stream, width = grad.shape
    share = cot.shape[1] // 2
    whole = pl.BlockSpec(memory_space=pltpu.VMEM)
    return pl.pallas_call(
        image_kernel,
        in_specs=[pl.BlockSpec(memory_space=pltpu.SMEM)] + [whole] * (5 + len(others)),
        out_specs=[whole] * 4,
        out_shape=[
            jax.ShapeDtypeStruct((stream, width), jnp.bfloat16),
            jax.ShapeDtypeStruct((width, share), jnp.float32),
            jax.ShapeDtypeStruct((width, share), jnp.bfloat16),
            jax.ShapeDtypeStruct((2, width), jnp.float32),
        ],
        scratch_shapes=[pltpu.VMEM((stream, width), jnp.bfloat16)],
        compiler_params=pltpu.CompilerParams(vmem_limit_bytes=56 * 1024 * 1024),
        cost_estimate=pl.CostEstimate(
            flops=4 * stream * width * share, bytes_accessed=8 * stream * width, transcendentals=0
        ),
    )(z, grad, gain, cot, sums, own, *others)


def weight_kernel(act_ref, grad_ref, out_ref):
    step = act_ref.shape[1]
    groups = grad_ref.shape[1] // LANES
    product = lax.dot_general(
        act_ref[...], grad_ref[...], (((0,), (0,)), ((), ())), preferred_element_type=jnp.float32
    )
    for c in range(groups):
        out_ref[pl.ds(c, step, stride=groups), :] = product[:, c * LANES : (c + 1) * LANES]


def weight_product(act, grad):
    rows, features = act.shape
    width = grad.shape[1]
    groups = width // LANES
    step = 256
    return pl.pallas_call(
        weight_kernel,
        grid=(features // step,),
        in_specs=[
            pl.BlockSpec((rows, step), lambda i: (0, i)),
            pl.BlockSpec((rows, width), lambda i: (0, 0)),
        ],
        out_specs=pl.BlockSpec((step * groups, LANES), lambda i: (i, 0)),
        out_shape=jax.ShapeDtypeStruct((features * groups, LANES), jnp.float32),
        compiler_params=pltpu.CompilerParams(vmem_limit_bytes=32 * 1024 * 1024),
        cost_estimate=pl.CostEstimate(
            flops=2 * rows * features * width,
            bytes_accessed=4 * features * width + 2 * rows * (features + width),
            transcendentals=0,
        ),
    )(act, grad)


def on_device(
    vis_hidden,
    proj_weight,
    proj_bias,
    text_embed,
    norm_gain,
    key_weight,
    key_cotangent,
    tile_counts,
    text_counts,
    owner_map,
):
    f32, bf16 = jnp.float32, jnp.bfloat16
    n_sec, n_seq, n_tp = (lax.axis_size(a) for a in ("sec", "seq", "tp"))
    core, z, t = (lax.axis_index(a) for a in ("sec", "seq", "tp"))
    block_rows, features = vis_hidden.shape
    columns = proj_weight.shape[1]
    col_half = columns // n_sec
    stream = block_rows * n_tp
    own = stream // n_seq
    part_rows = block_rows // n_sec
    sub = part_rows // n_seq
    keys = key_weight.shape[1]
    key_half = keys // n_sec
    seq_len = text_embed.shape[0]
    tiles = stream // TILE

    mine = lax.dynamic_slice_in_dim(vis_hidden, core * part_rows, part_rows, 0)
    act = jax.nn.gelu(mine.astype(f32), approximate=False).astype(bf16)
    pieces = [act] + [swap(act, "tp", m) for m in range(1, n_tp)]
    pieces = [p.reshape(n_seq, sub, features) for p in pieces]

    def product(blocks):
        chunk = jnp.stack(blocks, 1).reshape(len(blocks) * part_rows, features)
        partial = jnp.dot(chunk, proj_weight, preferred_element_type=f32).astype(bf16)
        return partial.reshape(n_seq, len(blocks) * sub, columns)

    partials = [product(pieces[:1]), product(pieces[1:2])]

    text_values = text_embed.astype(f32)
    text_sq, *pieces = together(jnp.sum(text_values * text_values, 1), *pieces)
    text_sq = total(text_sq, "tp")
    is_mine = owner_map == z
    image_count = TILE * jnp.sum(jnp.where(is_mine, tile_counts, 0))
    text_count = jnp.sum(jnp.where(is_mine, text_counts, 0))
    text_inv = lax.rsqrt(text_sq / D + EPSILON)
    text_scale = jnp.where(jnp.arange(seq_len) < text_count, text_inv, 0.0)
    cot_half = lax.dynamic_slice_in_dim(key_cotangent, core * key_half, key_half, 1)
    cot_padded = jnp.concatenate([cot_half, jnp.zeros((MAXT * TILE, key_half), bf16)], 0)
    cot_text = lax.dynamic_slice_in_dim(cot_padded, image_count, seq_len, 0)
    cot_text = (cot_text.astype(f32) * text_scale[:, None]).astype(bf16)
    weight_half = lax.dynamic_slice_in_dim(key_weight, core * key_half, key_half, 1)
    moment, gain_text = text_product(text_embed, cot_text, weight_half)
    if n_seq != moment.shape[0]:
        share = key_half // n_seq
        moment = moment.reshape(-1, columns, LANES // share, share).transpose(0, 2, 1, 3)
        moment = moment.reshape(n_seq, columns, share)

    starts = jnp.cumsum(tile_counts) - tile_counts
    tile_ids = jnp.arange(tiles, dtype=jnp.int32)[:, None]
    held = (tile_ids >= starts[None]) & (tile_ids < (starts + tile_counts)[None])
    tile_owner = jnp.sum(jnp.where(held, owner_map[None], 0), 1)
    tile_place = jnp.sum(jnp.where(held, tile_ids - starts[None], 0), 1)
    share = key_half // n_tp
    from_col = (core * n_tp + t) * share
    front = lax.dynamic_slice_in_dim(key_cotangent[: MAXT * TILE], from_col, share, 1)
    front = front.reshape(MAXT, TILE, share)
    given = jnp.zeros((tiles, TILE, share), bf16)
    for place in range(MAXT):
        chosen = (tile_owner == z) & (tile_place == place)
        given = jnp.where(chosen[:, None, None], front[place][None], given)
    given = given.reshape(n_tp, n_sec, n_seq, sub, share).transpose(2, 1, 0, 3, 4)
    given = given.reshape(stream, share)
    given, partials[0] = together(given, partials[0])
    taken = butterfly(given, ("seq",))

    partials.append(product(pieces[2:]))
    images = []
    for i, partial in enumerate(partials):
        held_back = (moment, taken) if i == len(partials) - 1 else None
        summed, after = reduce_to_owner(partial, "seq", held_back)
        images += list((summed + proj_bias).astype(bf16).reshape(-1, sub, columns))
    moment, taken = after
    moment = lax.psum_scatter(moment, "seq", scatter_dimension=0, tiled=False)
    image_mine = jnp.concatenate(in_order(images, t), 0)
    low, high = image_mine[:, :col_half], image_mine[:, col_half:]
    first_core = core == 0
    came = swap(jnp.where(first_core, high, low), "sec", 1)
    image = jnp.concatenate(in_order([jnp.where(first_core, low, high), came], core), 0)

    taken = [taken] + [swap(taken, "tp", m) for m in range(1, n_tp)]
    half_cot = jnp.concatenate(in_order(taken, t), 1)
    other_cot = swap(half_cot, "sec", 1)
    image_cot = jnp.concatenate(in_order([half_cot, other_cot], core), 1)
    weight_rows = lax.dynamic_slice_in_dim(key_weight, core * col_half, col_half, 0)
    normed_grad = lax.dot_general(
        image_cot, weight_rows, (((1,), (1,)), ((), ())), preferred_element_type=f32
    )
    key_share = key_half // n_seq
    cot_own = jnp.concatenate(
        [lax.dynamic_slice_in_dim(c, z * key_share, key_share, 1) for c in (half_cot, other_cot)], 1
    )

    act_half = jnp.stack(in_order(pieces, t), 1)
    act_pair = in_order([act_half, swap(act_half, "sec", 1)], core)
    act_full = jnp.stack(act_pair, 1).reshape(stream, features)

    key_bias_part = jnp.sum(key_cotangent.astype(f32), 0)
    early = jnp.concatenate([gain_text[0], jnp.where(core == 0, key_bias_part, 0.0)])
    early = total(early, "sec")

    own_cot = lax.dynamic_slice_in_dim(image_cot, (z * n_sec + core) * (own // n_sec), own // n_sec, 0)
    own_grad = lax.dot_general(
        own_cot, key_weight, (((1,), (1,)), ((), ())), preferred_element_type=f32
    )
    sums = total(row_sums(image_mine, own_grad, norm_gain[None]), "tp")
    gain_half = lax.dynamic_slice_in_dim(norm_gain, core * col_half, col_half, 0)[None]
    if n_seq <= 4:
        up, down = along_line(image, "seq")
        sums, up[-2], down[-2] = together(sums, up[-2], down[-2])
        sums = jnp.stack(in_order([sums] + [swap(sums, "seq", m) for m in range(1, n_seq)], z), 0)
        others = up + down
    else:
        image = lax.all_gather(image, "seq", axis=0, tiled=True)
        sums = lax.all_gather(sums, "seq", axis=0, tiled=False)
        others = []
    sums = jnp.stack(in_order([sums, swap(sums, "sec", 1)], core), 1)
    sums = sums.reshape(n_seq * n_sec, *sums.shape[2:])
    embed_grad, here, there, small = image_grads(
        z[None], normed_grad, gain_half, cot_own, sums, image, others
    )
    early, embed_grad = together(early, embed_grad)
    early = total(early, "seq") if n_seq <= 4 else butterfly(early, ("seq",))
    there = swap(there, "sec", 1)
    small_other = swap(small, "sec", 1)
    weight_grad = weight_product(act_full, embed_grad)
    proj_weight_grad = weight_grad.reshape(features, 1, 1, col_half)

    both = in_order([here, there.astype(f32)], core)
    key_weight_grad = (moment.astype(f32) + jnp.concatenate(both, 0)) * norm_gain[:, None]
    gain_image, proj_bias_grad = jnp.concatenate(in_order([small, small_other], core), 1)

    gain_grad = early[:columns] + gain_image
    key_bias_grad = early[columns:]
    return (proj_weight_grad, proj_bias_grad, key_weight_grad, key_bias_grad, gain_grad)


def solution(mesh):
    placed = (
        P("tp", "seq"),
        P("seq", "tp"),
        P("tp"),
        P("seq", "tp"),
        P("tp"),
        P("tp", None),
        P("seq", None),
        P(),
        P(),
        P(),
    )
    return jax.shard_map(
        on_device,
        mesh=mesh,
        in_specs=placed,
        out_specs=(P("seq", "tp", "sec", None), P("tp"), P("tp", ("sec", "seq")), P(), P("tp")),
        check_vma=False,
    )
```

```python
import jax
import jax.numpy as jnp
from jax import lax
from jax.experimental import pallas as pl
from jax.experimental.pallas import tpu as pltpu
from jax.sharding import PartitionSpec as P

D = 8192
TILE = 256
MAXT = 2
LANES = 128
EPSILON = 1e-06


def swap(x, axis, mask):
    count = lax.axis_size(axis)
    return lax.ppermute(x, axis, [(i, i ^ mask) for i in range(count)])


def total(x, axis):
    pieces = [x] + [swap(x, axis, m) for m in range(1, lax.axis_size(axis))]
    while len(pieces) > 1:
        pieces = [pieces[i] + pieces[i + 1] for i in range(0, len(pieces), 2)]
    return pieces[0]


def butterfly(x, axes):
    for axis in axes:
        mask = 1
        while mask < lax.axis_size(axis):
            x = x + swap(x, axis, mask)
            mask *= 2
    return x


def in_order(pieces, index):
    pieces = list(pieces)
    mask = 1
    while mask < len(pieces):
        odd = (index & mask) != 0
        pieces = [jnp.where(odd, pieces[m ^ mask], pieces[m]) for m in range(len(pieces))]
        mask *= 2
    return pieces


def together(*values):
    return lax.optimization_barrier(values)


def reduce_to_owner(parts, axis):
    index = lax.axis_index(axis)
    count = parts.shape[0]
    while count > 1:
        pairs = parts.reshape(count // 2, 2, *parts.shape[1:])
        mask = lax.axis_size(axis) // count
        bit = (index // mask) % 2
        sent = lax.dynamic_index_in_dim(pairs, 1 - bit, 1, keepdims=False)
        kept = lax.dynamic_index_in_dim(pairs, bit, 1, keepdims=False)
        came = swap(sent.astype(jnp.bfloat16), axis, mask)
        parts = kept.astype(jnp.float32) + came.astype(jnp.float32)
        count //= 2
    return parts[0]


def columns_of(row, count):
    parts = []
    for i in range(count // LANES):
        part = row[:, i * LANES : (i + 1) * LANES]
        parts.append(jnp.broadcast_to(part, (LANES, LANES)).T)
    return jnp.concatenate(parts, 0)


def row_of(folded):
    count = folded.shape[0]
    parts = [
        jnp.sum(folded[i * LANES : (i + 1) * LANES, :].T, 0, keepdims=True)
        for i in range(count // LANES)
    ]
    return jnp.concatenate(parts, 1)


def fold(values):
    width = values.shape[1]
    out = values[:, :LANES]
    for i in range(1, width // LANES):
        out = out + values[:, i * LANES : (i + 1) * LANES]
    return out


def project_kernel(*refs):
    index_ref, weight_ref = refs[:2]
    partial_ref, act_ref = refs[-2:]
    pieces = refs[2:-2]
    rows = pieces[0].shape[0]

    @pl.when(pl.program_id(0) == 0)
    def _():
        for m, piece in enumerate(pieces):
            at = jnp.bitwise_xor(index_ref[0], m) * rows
            act_ref[pl.ds(pl.multiple_of(at, rows), rows), :] = piece[...]

    product = jnp.dot(act_ref[...], weight_ref[...], preferred_element_type=jnp.float32)
    partial_ref[...] = product.astype(jnp.bfloat16)


def project(index, pieces, weight):
    rows, features = pieces[0].shape
    columns = weight.shape[1]
    total_rows = rows * len(pieces)
    step = 512
    return pl.pallas_call(
        project_kernel,
        grid=(columns // step,),
        in_specs=[
            pl.BlockSpec(memory_space=pltpu.SMEM),
            pl.BlockSpec((features, step), lambda i: (0, i)),
        ]
        + [pl.BlockSpec((rows, features), lambda i: (0, 0))] * len(pieces),
        out_specs=[
            pl.BlockSpec((total_rows, step), lambda i: (0, i)),
            pl.BlockSpec((total_rows, features), lambda i: (0, 0)),
        ],
        out_shape=[
            jax.ShapeDtypeStruct((total_rows, columns), jnp.bfloat16),
            jax.ShapeDtypeStruct((total_rows, features), jnp.bfloat16),
        ],
        compiler_params=pltpu.CompilerParams(vmem_limit_bytes=40 * 1024 * 1024),
        cost_estimate=pl.CostEstimate(
            flops=2 * total_rows * features * columns,
            bytes_accessed=2 * (features * columns + total_rows * (columns + 2 * features)),
            transcendentals=0,
        ),
    )(index, weight, *pieces)


def text_kernel(text_ref, cot_ref, weight_ref, moment_ref, gain_ref):
    moment = lax.dot_general(
        text_ref[...], cot_ref[...], (((0,), (0,)), ((), ())), preferred_element_type=jnp.float32
    )
    for i in range(moment_ref.shape[0]):
        moment_ref[i] = moment[:, i * LANES : (i + 1) * LANES].astype(jnp.bfloat16)
    gain_ref[...] = row_of(fold(moment * weight_ref[...].astype(jnp.float32)))


def text_product(text, cot, weight):
    seq_len, columns = text.shape
    width = cot.shape[1]
    groups = width // LANES
    step = 256
    return pl.pallas_call(
        text_kernel,
        grid=(columns // step,),
        in_specs=[
            pl.BlockSpec((seq_len, step), lambda i: (0, i)),
            pl.BlockSpec((seq_len, width), lambda i: (0, 0)),
            pl.BlockSpec((step, width), lambda i: (i, 0)),
        ],
        out_specs=[
            pl.BlockSpec((groups, step, LANES), lambda i: (0, i, 0)),
            pl.BlockSpec((1, step), lambda i: (0, i)),
        ],
        out_shape=[
            jax.ShapeDtypeStruct((groups, columns, LANES), jnp.bfloat16),
            jax.ShapeDtypeStruct((1, columns), jnp.float32),
        ],
        compiler_params=pltpu.CompilerParams(vmem_limit_bytes=32 * 1024 * 1024),
        cost_estimate=pl.CostEstimate(
            flops=2 * seq_len * columns * width,
            bytes_accessed=2 * (seq_len * (columns + width) + 2 * columns * width),
            transcendentals=0,
        ),
    )(text, cot, weight)


def sums_kernel(rows_ref, grad_ref, gain_ref, sums_ref):
    values = rows_ref[...].astype(jnp.float32)
    more = sums_ref.shape[1] - values.shape[0]
    for i, terms in enumerate((values * values, values * grad_ref[...] * gain_ref[...])):
        folded = jnp.concatenate([fold(terms), jnp.zeros((more, LANES), jnp.float32)], 0)
        sums_ref[i : i + 1, :] = row_of(folded)


def row_sums(rows, grad, gain):
    count, width = rows.shape
    padded = -(-count // LANES) * LANES
    whole = pl.BlockSpec(memory_space=pltpu.VMEM)
    return pl.pallas_call(
        sums_kernel,
        in_specs=[whole] * 3,
        out_specs=whole,
        out_shape=jax.ShapeDtypeStruct((2, padded), jnp.float32),
        compiler_params=pltpu.CompilerParams(vmem_limit_bytes=16 * 1024 * 1024),
        cost_estimate=pl.CostEstimate(
            flops=8 * count * width, bytes_accessed=6 * count * width, transcendentals=0
        ),
    )(rows, grad, gain)


def image_kernel(core_ref, grad_ref, gain_ref, cot_ref, sums_ref, rows_ref, *out):
    embed_ref, here_ref, there_ref, small_ref = out
    stream, width = rows_ref.shape
    groups = sums_ref.shape[0]
    size = stream // groups
    inv, mean = [], []
    for i in range(groups):
        inv_row = lax.rsqrt(sums_ref[i, 0:1, :] / D + EPSILON)
        mean_row = inv_row * inv_row * inv_row * sums_ref[i, 1:2, :] / D
        inv.append(columns_of(inv_row, inv_row.shape[1])[:size])
        mean.append(columns_of(mean_row, mean_row.shape[1])[:size])
    all_inv = jnp.concatenate(inv, 0)
    gain_parts = [jnp.zeros((1, LANES), jnp.float32)] * (width // LANES)
    bias_parts = list(gain_parts)
    for g in range(groups):
        rows = slice(g * size, (g + 1) * size)
        to_rows = slice((g // 2) * size, (g // 2 + 1) * size)
        side = jnp.bitwise_xor(core_ref[0], g % 2)
        for i in range(width // LANES):
            at = slice(i * LANES, (i + 1) * LANES)
            values = rows_ref[rows, at].astype(jnp.float32)
            scaled = grad_ref[rows, at] * inv[g]
            embed = (scaled * gain_ref[:, at] - values * mean[g]).astype(jnp.bfloat16)
            embed_ref[side, to_rows, at] = embed
            gain_parts[i] = gain_parts[i] + jnp.sum(scaled * values, 0, keepdims=True)
            bias_parts[i] = bias_parts[i] + jnp.sum(embed.astype(jnp.float32), 0, keepdims=True)
    small_ref[0:1, :] = jnp.concatenate(gain_parts, 1)
    small_ref[1:2, :] = jnp.concatenate(bias_parts, 1)
    lanes = cot_ref.shape[1]
    wide = [all_inv] * (lanes // LANES) if lanes >= LANES else [all_inv[:, :lanes]]
    cot = (cot_ref[...].astype(jnp.float32) * jnp.concatenate(wide, 1)).astype(jnp.bfloat16)
    moment = lax.dot_general(
        rows_ref[...], cot, (((0,), (0,)), ((), ())), preferred_element_type=jnp.float32
    )
    share = here_ref.shape[1]
    here_ref[...] = moment[:, :share]
    there_ref[...] = moment[:, share:].astype(jnp.bfloat16)


def image_grads(core, grad, gain, cot, sums, rows):
    stream, width = grad.shape
    share = cot.shape[1] // 2
    whole = pl.BlockSpec(memory_space=pltpu.VMEM)
    return pl.pallas_call(
        image_kernel,
        in_specs=[pl.BlockSpec(memory_space=pltpu.SMEM)] + [whole] * 5,
        out_specs=[whole] * 4,
        out_shape=[
            jax.ShapeDtypeStruct((2, stream // 2, width), jnp.bfloat16),
            jax.ShapeDtypeStruct((width, share), jnp.float32),
            jax.ShapeDtypeStruct((width, share), jnp.bfloat16),
            jax.ShapeDtypeStruct((2, width), jnp.float32),
        ],
        compiler_params=pltpu.CompilerParams(vmem_limit_bytes=56 * 1024 * 1024),
        cost_estimate=pl.CostEstimate(
            flops=4 * stream * width * share, bytes_accessed=8 * stream * width, transcendentals=0
        ),
    )(core, grad, gain, cot, sums, rows)


def weight_kernel(mine_ref, other_ref, grad_ref, out_ref):
    step = mine_ref.shape[1]
    groups = grad_ref.shape[2] // LANES
    rows_first = (((0,), (0,)), ((), ()))
    product = lax.dot_general(
        mine_ref[...], grad_ref[0], rows_first, preferred_element_type=jnp.float32
    ) + lax.dot_general(
        other_ref[...], grad_ref[1], rows_first, preferred_element_type=jnp.float32
    )
    for c in range(groups):
        out_ref[pl.ds(c, step, stride=groups), :] = product[:, c * LANES : (c + 1) * LANES]


def weight_product(mine, other, grad):
    rows, features = mine.shape
    width = grad.shape[2]
    groups = width // LANES
    step = 256
    return pl.pallas_call(
        weight_kernel,
        grid=(features // step,),
        in_specs=[
            pl.BlockSpec((rows, step), lambda i: (0, i)),
            pl.BlockSpec((rows, step), lambda i: (0, i)),
            pl.BlockSpec(grad.shape, lambda i: (0, 0, 0)),
        ],
        out_specs=pl.BlockSpec((step * groups, LANES), lambda i: (i, 0)),
        out_shape=jax.ShapeDtypeStruct((features * groups, LANES), jnp.float32),
        compiler_params=pltpu.CompilerParams(vmem_limit_bytes=32 * 1024 * 1024),
        cost_estimate=pl.CostEstimate(
            flops=4 * rows * features * width,
            bytes_accessed=4 * features * width + 4 * rows * (features + width),
            transcendentals=0,
        ),
    )(mine, other, grad)


def on_device(
    vis_hidden,
    proj_weight,
    proj_bias,
    text_embed,
    norm_gain,
    key_weight,
    key_cotangent,
    tile_counts,
    text_counts,
    owner_map,
):
    f32, bf16 = jnp.float32, jnp.bfloat16
    n_sec, n_seq, n_tp = (lax.axis_size(a) for a in ("sec", "seq", "tp"))
    core, z, t = (lax.axis_index(a) for a in ("sec", "seq", "tp"))
    block_rows, features = vis_hidden.shape
    columns = proj_weight.shape[1]
    col_half = columns // n_sec
    stream = block_rows * n_tp
    own = stream // n_seq
    half = own // n_sec
    groups = block_rows // own
    keys = key_weight.shape[1]
    key_half = keys // n_sec
    seq_len = text_embed.shape[0]
    tiles = stream // TILE

    text_values = text_embed.astype(f32)
    text_sq = total(jnp.sum(text_values * text_values, 1), "tp")

    grouped = vis_hidden.reshape(groups, n_sec, half, features)
    mine = lax.dynamic_index_in_dim(grouped, core, 1, keepdims=False)
    act = jax.nn.gelu(mine.astype(f32), approximate=False).astype(bf16)
    act = act.reshape(groups * half, features)
    pieces = [act] + [swap(act, "tp", m) for m in range(1, n_tp)]
    partial, act_mine = project(t[None], pieces, proj_weight)

    is_mine = owner_map == z
    image_count = TILE * jnp.sum(jnp.where(is_mine, tile_counts, 0))
    text_count = jnp.sum(jnp.where(is_mine, text_counts, 0))
    text_inv = lax.rsqrt(text_sq / D + EPSILON)
    text_scale = jnp.where(jnp.arange(seq_len) < text_count, text_inv, 0.0)
    cot_half = lax.dynamic_slice_in_dim(key_cotangent, core * key_half, key_half, 1)
    cot_padded = jnp.concatenate([cot_half, jnp.zeros((MAXT * TILE, key_half), bf16)], 0)
    cot_text = lax.dynamic_slice_in_dim(cot_padded, image_count, seq_len, 0)
    cot_text = (cot_text.astype(f32) * text_scale[:, None]).astype(bf16)
    weight_half = lax.dynamic_slice_in_dim(key_weight, core * key_half, key_half, 1)
    moment, gain_text = text_product(text_embed, cot_text, weight_half)
    if n_seq != moment.shape[0]:
        share = key_half // n_seq
        moment = moment.reshape(-1, columns, LANES // share, share).transpose(0, 2, 1, 3)
        moment = moment.reshape(n_seq, columns, share)
    moment = reduce_to_owner(moment, "seq")

    starts = jnp.cumsum(tile_counts) - tile_counts
    tile_ids = jnp.arange(tiles, dtype=jnp.int32)[:, None]
    held = (tile_ids >= starts[None]) & (tile_ids < (starts + tile_counts)[None])
    tile_owner = jnp.sum(jnp.where(held, owner_map[None], 0), 1)
    tile_place = jnp.sum(jnp.where(held, tile_ids - starts[None], 0), 1)
    share = key_half // n_tp
    from_col = (core * n_tp + t) * share
    front = lax.dynamic_slice_in_dim(key_cotangent[: MAXT * TILE], from_col, share, 1)
    front = front.reshape(MAXT, TILE, share)
    given = jnp.zeros((tiles, TILE, share), bf16)
    for place in range(MAXT):
        chosen = (tile_owner == z) & (tile_place == place)
        given = jnp.where(chosen[:, None, None], front[place][None], given)
    taken = butterfly(given.reshape(stream, share), ("seq",))
    key_bias_part = jnp.sum(key_cotangent.astype(f32), 0)
    early = jnp.concatenate([gain_text[0], jnp.where(core == 0, key_bias_part, 0.0)])

    taken, early, act_mine, partial = together(taken, early, act_mine, partial)
    summed = lax.psum_scatter(partial, "seq", scatter_dimension=0, tiled=True)
    early = total(early, "seq") if n_seq <= 4 else butterfly(early, ("seq",))
    early = total(early, "sec")
    act_other = swap(act_mine, "sec", 1)
    taken = [taken] + [swap(taken, "tp", m) for m in range(1, n_tp)]
    half_cot = jnp.concatenate(in_order(taken, t), 1)
    other_cot = swap(half_cot, "sec", 1)
    image_cot = jnp.concatenate(in_order([half_cot, other_cot], core), 1)
    weight_rows = lax.dynamic_slice_in_dim(key_weight, core * col_half, col_half, 0)
    normed_grad = lax.dot_general(
        image_cot, weight_rows, (((1,), (1,)), ((), ())), preferred_element_type=f32
    )
    own_cot = lax.dynamic_slice_in_dim(image_cot, (z * n_sec + core) * half, half, 0)
    own_grad = lax.dot_general(
        own_cot, key_weight, (((1,), (1,)), ((), ())), preferred_element_type=f32
    )
    key_share = key_half // n_seq
    cot_own = jnp.concatenate(
        [lax.dynamic_slice_in_dim(c, z * key_share, key_share, 1) for c in (half_cot, other_cot)], 1
    )

    image_mine = (summed.astype(f32) + proj_bias).astype(bf16)
    low, high = image_mine[:, :col_half], image_mine[:, col_half:]
    first_core = core == 0
    came = swap(jnp.where(first_core, high, low), "sec", 1)
    image = jnp.concatenate(in_order([jnp.where(first_core, low, high), came], core), 0)
    rows = lax.all_gather(image, "seq", axis=0, tiled=True)

    sums = total(row_sums(image_mine, own_grad, norm_gain[None]), "tp")
    if n_seq <= 4:
        sums = jnp.stack(in_order([sums] + [swap(sums, "seq", m) for m in range(1, n_seq)], z), 0)
    else:
        sums = lax.all_gather(sums, "seq", axis=0, tiled=False)
    sums = jnp.stack(in_order([sums, swap(sums, "sec", 1)], core), 1)
    sums = sums.reshape(n_seq * n_sec, *sums.shape[2:])

    gain_half = lax.dynamic_slice_in_dim(norm_gain, core * col_half, col_half, 0)[None]
    embed_grad, here, there, small = image_grads(
        core[None], normed_grad, gain_half, cot_own, sums, rows
    )
    there = swap(there, "sec", 1)
    small_other = swap(small, "sec", 1)
    weight_grad = weight_product(act_mine, act_other, embed_grad)
    proj_weight_grad = weight_grad.reshape(features, 1, 1, col_half)

    both = in_order([here, there.astype(f32)], core)
    key_weight_grad = (moment + jnp.concatenate(both, 0)) * norm_gain[:, None]
    gain_image, proj_bias_grad = jnp.concatenate(in_order([small, small_other], core), 1)
    gain_grad = early[:columns] + gain_image
    key_bias_grad = early[columns:]
    return (proj_weight_grad, proj_bias_grad, key_weight_grad, key_bias_grad, gain_grad)


def solution(mesh):
    placed = (
        P("tp", "seq"),
        P("seq", "tp"),
        P("tp"),
        P("seq", "tp"),
        P("tp"),
        P("tp", None),
        P("seq", None),
        P(),
        P(),
        P(),
    )
    return jax.shard_map(
        on_device,
        mesh=mesh,
        in_specs=placed,
        out_specs=(P("seq", "tp", "sec", None), P("tp"), P("tp", ("sec", "seq")), P(), P("tp")),
        check_vma=False,
    )
```

```python
import jax
import jax.numpy as jnp
from jax import lax
from jax.experimental import pallas as pl
from jax.experimental.pallas import tpu as pltpu
from jax.sharding import PartitionSpec as P

D = 8192
TILE = 256
MAXT = 2
LANES = 128
EPSILON = 1e-06


def swap(x, axis, mask):
    count = lax.axis_size(axis)
    return lax.ppermute(x, axis, [(i, i ^ mask) for i in range(count)])


def total(x, axis):
    pieces = [x] + [swap(x, axis, m) for m in range(1, lax.axis_size(axis))]
    while len(pieces) > 1:
        pieces = [pieces[i] + pieces[i + 1] for i in range(0, len(pieces), 2)]
    return pieces[0]


def butterfly(x, axes):
    for axis in axes:
        mask = 1
        while mask < lax.axis_size(axis):
            x = x + swap(x, axis, mask)
            mask *= 2
    return x


def in_order(pieces, index):
    pieces = list(pieces)
    mask = 1
    while mask < len(pieces):
        odd = (index & mask) != 0
        pieces = [jnp.where(odd, pieces[m ^ mask], pieces[m]) for m in range(len(pieces))]
        mask *= 2
    return pieces


def together(*values):
    return lax.optimization_barrier(values)


def reduce_to_owner(parts, axis):
    index = lax.axis_index(axis)
    count = parts.shape[0]
    while count > 1:
        pairs = parts.reshape(count // 2, 2, *parts.shape[1:])
        mask = lax.axis_size(axis) // count
        bit = (index // mask) % 2
        sent = lax.dynamic_index_in_dim(pairs, 1 - bit, 1, keepdims=False)
        kept = lax.dynamic_index_in_dim(pairs, bit, 1, keepdims=False)
        came = swap(sent.astype(jnp.bfloat16), axis, mask)
        parts = kept.astype(jnp.float32) + came.astype(jnp.float32)
        count //= 2
    return parts[0]


def line_step(parts, axis, step, before):
    count = lax.axis_size(axis)
    index = lax.axis_index(axis)
    out = []
    for sign in (1, -1):
        place = index + sign * (count - step)
        place = jnp.clip(place, 0, count - 1)
        sent = lax.dynamic_index_in_dim(parts, place, 0, keepdims=False)
        if before is not None:
            sent = (sent.astype(jnp.float32) + before[len(out)].astype(jnp.float32)).astype(sent.dtype)
        first = 0 if sign > 0 else count - 1
        pairs = [(first + sign * j, first + sign * (j + 1)) for j in range(step)]
        out.append(lax.ppermute(sent, axis, pairs))
    return out


def columns_of(row, count):
    parts = []
    for i in range(count // LANES):
        part = row[:, i * LANES : (i + 1) * LANES]
        parts.append(jnp.broadcast_to(part, (LANES, LANES)).T)
    return jnp.concatenate(parts, 0)


def row_of(folded):
    count = folded.shape[0]
    parts = [
        jnp.sum(folded[i * LANES : (i + 1) * LANES, :].T, 0, keepdims=True)
        for i in range(count // LANES)
    ]
    return jnp.concatenate(parts, 1)


def fold(values):
    width = values.shape[1]
    out = values[:, :LANES]
    for i in range(1, width // LANES):
        out = out + values[:, i * LANES : (i + 1) * LANES]
    return out


def project_kernel(*refs):
    index_ref, weight_ref = refs[:2]
    partial_ref, act_ref = refs[-2:]
    pieces = refs[2:-2]
    rows = pieces[0].shape[0]

    @pl.when(pl.program_id(0) == 0)
    def _():
        for m, piece in enumerate(pieces):
            at = jnp.bitwise_xor(index_ref[0], m) * rows
            act_ref[pl.ds(pl.multiple_of(at, rows), rows), :] = piece[...]

    product = jnp.dot(act_ref[...], weight_ref[...], preferred_element_type=jnp.float32)
    partial_ref[...] = product.astype(jnp.bfloat16)


def project(index, pieces, weight):
    rows, features = pieces[0].shape
    columns = weight.shape[1]
    total_rows = rows * len(pieces)
    step = 512
    return pl.pallas_call(
        project_kernel,
        grid=(columns // step,),
        in_specs=[
            pl.BlockSpec(memory_space=pltpu.SMEM),
            pl.BlockSpec((features, step), lambda i: (0, i)),
        ]
        + [pl.BlockSpec((rows, features), lambda i: (0, 0))] * len(pieces),
        out_specs=[
            pl.BlockSpec((total_rows, step), lambda i: (0, i)),
            pl.BlockSpec((total_rows, features), lambda i: (0, 0)),
        ],
        out_shape=[
            jax.ShapeDtypeStruct((total_rows, columns), jnp.bfloat16),
            jax.ShapeDtypeStruct((total_rows, features), jnp.bfloat16),
        ],
        compiler_params=pltpu.CompilerParams(vmem_limit_bytes=40 * 1024 * 1024),
        cost_estimate=pl.CostEstimate(
            flops=2 * total_rows * features * columns,
            bytes_accessed=2 * (features * columns + total_rows * (columns + 2 * features)),
            transcendentals=0,
        ),
    )(index, weight, *pieces)


def opening_kernel(core_ref, text_ref, *refs):
    del core_ref
    sums_ref, act_ref = refs[-2:]
    groups = refs[:-2]

    @pl.when(pl.program_id(0) == 0)
    def _():
        rows = groups[0].shape[0]
        for i, group in enumerate(groups):
            hidden = group[...].astype(jnp.float32)
            act = 0.5 * hidden * (1.0 + lax.erf(hidden * 0.7071067811865476))
            act_ref[i * rows : (i + 1) * rows, :] = act.astype(jnp.bfloat16)

    values = text_ref[...].astype(jnp.float32)
    sums_ref[...] = row_of(fold(values * values))


def opening(core, text, hidden, groups, n_sec):
    seq_len, columns = text.shape
    rows, features = hidden.shape
    half = rows // (groups * n_sec)
    step = 256
    part = [
        pl.BlockSpec((half, features), lambda i, c, q=q: (q * n_sec + c[0], 0)) for q in range(groups)
    ]
    return pl.pallas_call(
        opening_kernel,
        grid_spec=pltpu.PrefetchScalarGridSpec(
            num_scalar_prefetch=1,
            grid=(seq_len // step,),
            in_specs=[pl.BlockSpec((step, columns), lambda i, c: (i, 0))] + part,
            out_specs=[
                pl.BlockSpec((1, step), lambda i, c: (0, i)),
                pl.BlockSpec((groups * half, features), lambda i, c: (0, 0)),
            ],
        ),
        out_shape=[
            jax.ShapeDtypeStruct((1, seq_len), jnp.float32),
            jax.ShapeDtypeStruct((groups * half, features), jnp.bfloat16),
        ],
        compiler_params=pltpu.CompilerParams(vmem_limit_bytes=24 * 1024 * 1024),
        cost_estimate=pl.CostEstimate(
            flops=2 * seq_len * columns + 40 * groups * half * features,
            bytes_accessed=2 * seq_len * columns,
            transcendentals=0,
        ),
    )(core, text, *[hidden] * groups)


def text_kernel(
    at_ref, text_ref, weight_ref, cot_ref, *refs
):
    moment_ref, gain_ref, long_ref, scaled_ref = refs[-4:]
    squares = refs[:-4]
    seq_len, width = cot_ref.shape

    @pl.when(pl.program_id(0) == 0)
    def _():
        parts = [r[...] for r in squares]
        while len(parts) > 1:
            parts = [parts[i] + parts[i + 1] for i in range(0, len(parts), 2)]
        places = lax.broadcasted_iota(jnp.int32, (1, seq_len), 1)
        scale = lax.rsqrt(parts[0] / D + EPSILON)
        scale = columns_of(jnp.where(places < at_ref[2], scale, 0.0), seq_len)
        long_ref[:seq_len, :] = cot_ref[...]
        long_ref[seq_len:, :] = jnp.zeros((MAXT * TILE, width), jnp.bfloat16)
        for i in range(width // LANES):
            lanes = slice(i * LANES, (i + 1) * LANES)
            shifted = long_ref[pl.ds(pl.multiple_of(at_ref[1] * TILE, TILE), seq_len), lanes]
            scaled_ref[:, lanes] = (shifted.astype(jnp.float32) * scale).astype(jnp.bfloat16)

    moment = lax.dot_general(
        text_ref[...], scaled_ref[...], (((0,), (0,)), ((), ())), preferred_element_type=jnp.float32
    )
    for i in range(moment_ref.shape[0]):
        moment_ref[i] = moment[:, i * LANES : (i + 1) * LANES].astype(jnp.bfloat16)
    gain_ref[...] = row_of(fold(moment * weight_ref[...].astype(jnp.float32)))


def text_product(at, text, weight, cot, squares, width):
    seq_len, columns = text.shape
    groups = width // LANES
    step = 256
    return pl.pallas_call(
        text_kernel,
        grid_spec=pltpu.PrefetchScalarGridSpec(
            num_scalar_prefetch=1,
            grid=(columns // step,),
            in_specs=[
                pl.BlockSpec((seq_len, step), lambda i, a: (0, i)),
                pl.BlockSpec((step, width), lambda i, a: (i, a[0])),
                pl.BlockSpec((seq_len, width), lambda i, a: (0, a[0])),
            ]
            + [pl.BlockSpec((1, seq_len), lambda i, a: (0, 0))] * len(squares),
            out_specs=[
                pl.BlockSpec((groups, step, LANES), lambda i, a: (0, i, 0)),
                pl.BlockSpec((1, step), lambda i, a: (0, i)),
            ],
            scratch_shapes=[
                pltpu.VMEM((seq_len + MAXT * TILE, width), jnp.bfloat16),
                pltpu.VMEM((seq_len, width), jnp.bfloat16),
            ],
        ),
        out_shape=[
            jax.ShapeDtypeStruct((groups, columns, LANES), jnp.bfloat16),
            jax.ShapeDtypeStruct((1, columns), jnp.float32),
        ],
        compiler_params=pltpu.CompilerParams(vmem_limit_bytes=32 * 1024 * 1024),
        cost_estimate=pl.CostEstimate(
            flops=2 * seq_len * columns * width,
            bytes_accessed=2 * (seq_len * (columns + width) + 2 * columns * width),
            transcendentals=0,
        ),
    )(at, text, weight, cot, *squares)


def sums_kernel(rows_ref, grad_ref, gain_ref, sums_ref):
    values = rows_ref[...].astype(jnp.float32)
    more = sums_ref.shape[1] - values.shape[0]
    for i, terms in enumerate((values * values, values * grad_ref[...] * gain_ref[...])):
        folded = jnp.concatenate([fold(terms), jnp.zeros((more, LANES), jnp.float32)], 0)
        sums_ref[i : i + 1, :] = row_of(folded)


def row_sums(rows, grad, gain):
    count, width = rows.shape
    padded = -(-count // LANES) * LANES
    whole = pl.BlockSpec(memory_space=pltpu.VMEM)
    return pl.pallas_call(
        sums_kernel,
        in_specs=[whole] * 3,
        out_specs=whole,
        out_shape=jax.ShapeDtypeStruct((2, padded), jnp.float32),
        compiler_params=pltpu.CompilerParams(vmem_limit_bytes=16 * 1024 * 1024),
        cost_estimate=pl.CostEstimate(
            flops=8 * count * width, bytes_accessed=6 * count * width, transcendentals=0
        ),
    )(rows, grad, gain)


def image_kernel(core_ref, grad_ref, gain_ref, cot_ref, sums_ref, rows_ref, *out):
    embed_ref, here_ref, there_ref, small_ref = out
    stream, width = rows_ref.shape
    groups = sums_ref.shape[0]
    size = stream // groups
    inv, mean = [], []
    for i in range(groups):
        inv_row = lax.rsqrt(sums_ref[i, 0:1, :] / D + EPSILON)
        mean_row = inv_row * inv_row * inv_row * sums_ref[i, 1:2, :] / D
        inv.append(columns_of(inv_row, inv_row.shape[1])[:size])
        mean.append(columns_of(mean_row, mean_row.shape[1])[:size])
    all_inv = jnp.concatenate(inv, 0)
    gain_parts = [jnp.zeros((1, LANES), jnp.float32)] * (width // LANES)
    bias_parts = list(gain_parts)
    for g in range(groups):
        rows = slice(g * size, (g + 1) * size)
        to = jnp.bitwise_xor(core_ref[0], g % 2) * (stream // 2) + (g // 2) * size
        to_rows = pl.ds(pl.multiple_of(to, 16), size)
        for i in range(width // LANES):
            at = slice(i * LANES, (i + 1) * LANES)
            values = rows_ref[rows, at].astype(jnp.float32)
            scaled = grad_ref[rows, at] * inv[g]
            embed = (scaled * gain_ref[:, at] - values * mean[g]).astype(jnp.bfloat16)
            embed_ref[to_rows, at] = embed
            gain_parts[i] = gain_parts[i] + jnp.sum(scaled * values, 0, keepdims=True)
            bias_parts[i] = bias_parts[i] + jnp.sum(embed.astype(jnp.float32), 0, keepdims=True)
    small_ref[0:1, :] = jnp.concatenate(gain_parts, 1)
    small_ref[1:2, :] = jnp.concatenate(bias_parts, 1)
    lanes = cot_ref.shape[1]
    wide = [all_inv] * (lanes // LANES) if lanes >= LANES else [all_inv[:, :lanes]]
    cot = (cot_ref[...].astype(jnp.float32) * jnp.concatenate(wide, 1)).astype(jnp.bfloat16)
    moment = lax.dot_general(
        rows_ref[...], cot, (((0,), (0,)), ((), ())), preferred_element_type=jnp.float32
    )
    share = here_ref.shape[1]
    here_ref[...] = moment[:, :share]
    there_ref[...] = moment[:, share:].astype(jnp.bfloat16)


def image_grads(core, grad, gain, cot, sums, rows):
    stream, width = grad.shape
    share = cot.shape[1] // 2
    whole = pl.BlockSpec(memory_space=pltpu.VMEM)
    return pl.pallas_call(
        image_kernel,
        in_specs=[pl.BlockSpec(memory_space=pltpu.SMEM)] + [whole] * 5,
        out_specs=[whole] * 4,
        out_shape=[
            jax.ShapeDtypeStruct((stream, width), jnp.bfloat16),
            jax.ShapeDtypeStruct((width, share), jnp.float32),
            jax.ShapeDtypeStruct((width, share), jnp.bfloat16),
            jax.ShapeDtypeStruct((2, width), jnp.float32),
        ],
        compiler_params=pltpu.CompilerParams(vmem_limit_bytes=56 * 1024 * 1024),
        cost_estimate=pl.CostEstimate(
            flops=4 * stream * width * share, bytes_accessed=8 * stream * width, transcendentals=0
        ),
    )(core, grad, gain, cot, sums, rows)


def weight_kernel(act_ref, grad_ref, out_ref):
    step = act_ref.shape[0]
    groups = grad_ref.shape[1] // LANES
    product = jnp.dot(act_ref[...], grad_ref[...], preferred_element_type=jnp.float32)
    for c in range(groups):
        out_ref[pl.ds(c, step, stride=groups), :] = product[:, c * LANES : (c + 1) * LANES]


def weight_product(act, grad):
    features, rows = act.shape
    width = grad.shape[1]
    groups = width // LANES
    step = 256
    return pl.pallas_call(
        weight_kernel,
        grid=(features // step,),
        in_specs=[
            pl.BlockSpec((step, rows), lambda i: (i, 0)),
            pl.BlockSpec((rows, width), lambda i: (0, 0)),
        ],
        out_specs=pl.BlockSpec((step * groups, LANES), lambda i: (i, 0)),
        out_shape=jax.ShapeDtypeStruct((features * groups, LANES), jnp.float32),
        compiler_params=pltpu.CompilerParams(vmem_limit_bytes=32 * 1024 * 1024),
        cost_estimate=pl.CostEstimate(
            flops=2 * rows * features * width,
            bytes_accessed=4 * features * width + 2 * rows * (features + width),
            transcendentals=0,
        ),
    )(act, grad)


def on_device(
    vis_hidden,
    proj_weight,
    proj_bias,
    text_embed,
    norm_gain,
    key_weight,
    key_cotangent,
    tile_counts,
    text_counts,
    owner_map,
):
    f32, bf16 = jnp.float32, jnp.bfloat16
    n_sec, n_seq, n_tp = (lax.axis_size(a) for a in ("sec", "seq", "tp"))
    core, z, t = (lax.axis_index(a) for a in ("sec", "seq", "tp"))
    block_rows, features = vis_hidden.shape
    columns = proj_weight.shape[1]
    col_half = columns // n_sec
    stream = block_rows * n_tp
    own = stream // n_seq
    half = own // n_sec
    groups = block_rows // own
    keys = key_weight.shape[1]
    key_half = keys // n_sec
    seq_len = text_embed.shape[0]
    tiles = stream // TILE

    text_sq, act = opening(core[None], text_embed, vis_hidden, groups, n_sec)
    text_sq = [text_sq] + [swap(text_sq, "tp", m) for m in range(1, n_tp)]
    pieces = [act] + [swap(act, "tp", m) for m in range(1, n_tp)]

    is_mine = owner_map == z
    image_tiles = jnp.sum(jnp.where(is_mine, tile_counts, 0))
    text_count = jnp.sum(jnp.where(is_mine, text_counts, 0))
    at = jnp.stack([core, image_tiles, text_count]).astype(jnp.int32)
    moment, gain_text = text_product(at, text_embed, key_weight, key_cotangent, text_sq, key_half)
    if n_seq <= 4:
        way = line_step(moment, "seq", 1, None)
        way[0], way[1], *pieces = together(*way, *pieces)
        way = line_step(moment, "seq", 2, way)
    else:
        share = key_half // n_seq
        moment = moment.reshape(-1, columns, LANES // share, share).transpose(0, 2, 1, 3)
        moment = reduce_to_owner(moment.reshape(n_seq, columns, share), "seq")
    partial, act_mine = project(t[None], pieces, proj_weight)

    starts = jnp.cumsum(tile_counts) - tile_counts
    tile_ids = jnp.arange(tiles, dtype=jnp.int32)[:, None]
    held = (tile_ids >= starts[None]) & (tile_ids < (starts + tile_counts)[None])
    tile_owner = jnp.sum(jnp.where(held, owner_map[None], 0), 1)
    tile_place = jnp.sum(jnp.where(held, tile_ids - starts[None], 0), 1)
    share = key_half // n_tp
    from_col = (core * n_tp + t) * share
    front = lax.dynamic_slice_in_dim(key_cotangent[: MAXT * TILE], from_col, share, 1)
    front = front.reshape(MAXT, TILE, share)
    given = jnp.zeros((tiles, TILE, share), bf16)
    for place in range(MAXT):
        chosen = (tile_owner == z) & (tile_place == place)
        given = jnp.where(chosen[:, None, None], front[place][None], given)
    taken = butterfly(given.reshape(stream, share), ("seq",))
    key_bias_part = jnp.sum(key_cotangent.astype(f32), 0)
    early = jnp.concatenate([gain_text[0], jnp.where(core == 0, key_bias_part, 0.0)])

    taken, early, act_mine, partial = together(taken, early, act_mine, partial)
    summed = lax.psum_scatter(partial, "seq", scatter_dimension=0, tiled=True)
    act_other = swap(act_mine, "sec", 1)
    taken = [taken] + [swap(taken, "tp", m) for m in range(1, n_tp)]
    half_cot = jnp.concatenate(in_order(taken, t), 1)
    other_cot = swap(half_cot, "sec", 1)
    image_cot = jnp.concatenate(in_order([half_cot, other_cot], core), 1)
    weight_rows = lax.dynamic_slice_in_dim(key_weight, core * col_half, col_half, 0)
    normed_grad = lax.dot_general(
        image_cot, weight_rows, (((1,), (1,)), ((), ())), preferred_element_type=f32
    )
    own_cot = lax.dynamic_slice_in_dim(image_cot, (z * n_sec + core) * half, half, 0)
    own_grad = lax.dot_general(
        own_cot, key_weight, (((1,), (1,)), ((), ())), preferred_element_type=f32
    )
    key_share = key_half // n_seq
    cot_own = jnp.concatenate(
        [lax.dynamic_slice_in_dim(c, z * key_share, key_share, 1) for c in (half_cot, other_cot)], 1
    )

    image_mine = (summed.astype(f32) + proj_bias).astype(bf16)
    if n_seq <= 4:
        way[0], way[1], image_mine = together(*way, image_mine)
        for step in range(3, n_seq):
            way = line_step(moment, "seq", step, way)
        moment = lax.dynamic_index_in_dim(moment, z, 0, keepdims=False).astype(f32)
        moment = moment + way[0].astype(f32) + way[1].astype(f32)
    low, high = image_mine[:, :col_half], image_mine[:, col_half:]
    first_core = core == 0
    came = swap(jnp.where(first_core, high, low), "sec", 1)
    image = jnp.concatenate(in_order([jnp.where(first_core, low, high), came], core), 0)
    rows = lax.all_gather(image, "seq", axis=0, tiled=True)

    sums = total(row_sums(image_mine, own_grad, norm_gain[None]), "tp")
    size = sums.size
    sums = jnp.concatenate([sums.reshape(-1), early])
    if n_seq <= 4:
        sums = jnp.stack(in_order([sums] + [swap(sums, "seq", m) for m in range(1, n_seq)], z), 0)
    else:
        sums = lax.all_gather(sums, "seq", axis=0, tiled=False)
    early = jnp.sum(sums[:, size:], 0)
    sums = jnp.concatenate([sums[:, :size].reshape(-1), early])
    sums = jnp.stack(in_order([sums, swap(sums, "sec", 1)], core), 0)
    early = jnp.sum(sums[:, n_seq * size :], 0)
    sums = sums[:, : n_seq * size].reshape(n_sec, n_seq, 2, -1).transpose(1, 0, 2, 3)
    sums = sums.reshape(n_seq * n_sec, 2, -1)

    gain_half = lax.dynamic_slice_in_dim(norm_gain, core * col_half, col_half, 0)[None]
    embed_grad, here, there, small = image_grads(
        core[None], normed_grad, gain_half, cot_own, sums, rows
    )
    there = swap(there, "sec", 1)
    small_other = swap(small, "sec", 1)
    act_turned = jnp.concatenate([act_mine, act_other], 0).T
    weight_grad = weight_product(act_turned, embed_grad)
    proj_weight_grad = weight_grad.reshape(features, 1, 1, col_half)

    both = in_order([here, there.astype(f32)], core)
    key_weight_grad = (moment + jnp.concatenate(both, 0)) * norm_gain[:, None]
    gain_image, proj_bias_grad = jnp.concatenate(in_order([small, small_other], core), 1)
    gain_grad = early[:columns] + gain_image
    key_bias_grad = early[columns:]
    return (proj_weight_grad, proj_bias_grad, key_weight_grad, key_bias_grad, gain_grad)


def solution(mesh):
    placed = (
        P("tp", "seq"),
        P("seq", "tp"),
        P("tp"),
        P("seq", "tp"),
        P("tp"),
        P("tp", None),
        P("seq", None),
        P(),
        P(),
        P(),
    )
    return jax.shard_map(
        on_device,
        mesh=mesh,
        in_specs=placed,
        out_specs=(P("seq", "tp", "sec", None), P("tp"), P("tp", ("sec", "seq")), P(), P("tp")),
        check_vma=False,
    )
```

```python
import jax
import jax.numpy as jnp
from jax import lax
from jax.experimental import pallas as pl
from jax.experimental.pallas import tpu as pltpu
from jax.sharding import PartitionSpec as P

D = 8192
TILE = 256
MAXT = 2
LANES = 128
EPSILON = 1e-06
VMEM = 60 * 1024 * 1024


def swap(x, axis, mask):
    count = lax.axis_size(axis)
    return lax.ppermute(x, axis, [(i, i ^ mask) for i in range(count)])


def total(x, axis):
    pieces = [x] + [swap(x, axis, m) for m in range(1, lax.axis_size(axis))]
    while len(pieces) > 1:
        pieces = [pieces[i] + pieces[i + 1] for i in range(0, len(pieces), 2)]
    return pieces[0]


def butterfly(x, axes):
    for axis in axes:
        mask = 1
        while mask < lax.axis_size(axis):
            x = x + swap(x, axis, mask)
            mask *= 2
    return x


def in_order(pieces, index):
    pieces = list(pieces)
    mask = 1
    while mask < len(pieces):
        odd = (index & mask) != 0
        pieces = [jnp.where(odd, pieces[m ^ mask], pieces[m]) for m in range(len(pieces))]
        mask *= 2
    return pieces


def together(*values):
    return lax.optimization_barrier(values)


def reduce_to_owner(parts, axis):
    index = lax.axis_index(axis)
    count = parts.shape[0]
    while count > 1:
        pairs = parts.reshape(count // 2, 2, *parts.shape[1:])
        mask = lax.axis_size(axis) // count
        bit = (index // mask) % 2
        sent = lax.dynamic_index_in_dim(pairs, 1 - bit, 1, keepdims=False)
        kept = lax.dynamic_index_in_dim(pairs, bit, 1, keepdims=False)
        came = swap(sent.astype(jnp.bfloat16), axis, mask)
        parts = kept.astype(jnp.float32) + came.astype(jnp.float32)
        count //= 2
    return parts[0]


def line_step(parts, axis, step, before):
    count = lax.axis_size(axis)
    index = lax.axis_index(axis)
    out = []
    for sign in (1, -1):
        place = index + sign * (count - step)
        place = jnp.clip(place, 0, count - 1)
        sent = lax.dynamic_index_in_dim(parts, place, 0, keepdims=False)
        if before is not None:
            sent = (sent.astype(jnp.float32) + before[len(out)].astype(jnp.float32)).astype(sent.dtype)
        first = 0 if sign > 0 else count - 1
        pairs = [(first + sign * j, first + sign * (j + 1)) for j in range(step)]
        out.append(lax.ppermute(sent, axis, pairs))
    return out


def columns_of(row, count):
    parts = []
    for i in range(count // LANES):
        part = row[:, i * LANES : (i + 1) * LANES]
        parts.append(jnp.broadcast_to(part, (LANES, LANES)).T)
    return jnp.concatenate(parts, 0)


def row_of(folded):
    count = folded.shape[0]
    parts = [
        jnp.sum(folded[i * LANES : (i + 1) * LANES, :].T, 0, keepdims=True)
        for i in range(count // LANES)
    ]
    return jnp.concatenate(parts, 1)


def fold(values):
    width = values.shape[1]
    out = values[:, :LANES]
    for i in range(1, width // LANES):
        out = out + values[:, i * LANES : (i + 1) * LANES]
    return out


def project_kernel(*refs):
    index_ref, weight_ref = refs[:2]
    partial_ref, act_ref = refs[-2:]
    pieces = refs[2:-2]
    rows = pieces[0].shape[0]

    @pl.when(pl.program_id(0) == 0)
    def _():
        for m, piece in enumerate(pieces):
            at = jnp.bitwise_xor(index_ref[0], m) * rows
            act_ref[pl.ds(pl.multiple_of(at, rows), rows), :] = piece[...]

    product = jnp.dot(act_ref[...], weight_ref[...], preferred_element_type=jnp.float32)
    partial_ref[...] = product.astype(jnp.bfloat16)


def project(index, pieces, weight):
    rows, features = pieces[0].shape
    columns = weight.shape[1]
    total_rows = rows * len(pieces)
    step = 512
    return pl.pallas_call(
        project_kernel,
        grid=(columns // step,),
        in_specs=[
            pl.BlockSpec(memory_space=pltpu.SMEM),
            pl.BlockSpec((features, step), lambda i: (0, i)),
        ]
        + [pl.BlockSpec((rows, features), lambda i: (0, 0))] * len(pieces),
        out_specs=[
            pl.BlockSpec((total_rows, step), lambda i: (0, i)),
            pl.BlockSpec((total_rows, features), lambda i: (0, 0)),
        ],
        out_shape=[
            jax.ShapeDtypeStruct((total_rows, columns), jnp.bfloat16),
            jax.ShapeDtypeStruct((total_rows, features), jnp.bfloat16),
        ],
        compiler_params=pltpu.CompilerParams(vmem_limit_bytes=VMEM),
        cost_estimate=pl.CostEstimate(
            flops=2 * total_rows * features * columns,
            bytes_accessed=2 * (features * columns + total_rows * (columns + 2 * features)),
            transcendentals=0,
        ),
    )(index, weight, *pieces)


def opening_kernel(
    core_ref, z_ref, t_ref, tiles_ref, owners_ref, text_ref, cot_ref, *refs
):
    del core_ref, t_ref
    sums_ref, act_ref, given_ref = refs[-3:]
    groups = refs[:-3]

    @pl.when(pl.program_id(0) == 0)
    def _():
        rows = groups[0].shape[0]
        for i, group in enumerate(groups):
            hidden = group[...].astype(jnp.float32)
            act = 0.5 * hidden * (1.0 + lax.erf(hidden * 0.7071067811865476))
            act_ref[i * rows : (i + 1) * rows, :] = act.astype(jnp.bfloat16)
        for tile in range(given_ref.shape[0] // TILE):
            start = owner = place = jnp.int32(0)
            for s in range(tiles_ref.shape[0]):
                inside = (tile >= start) & (tile < start + tiles_ref[s])
                owner = jnp.where(inside, owners_ref[s], owner)
                place = jnp.where(inside, tile - start, place)
                start = start + tiles_ref[s]
            at = pl.multiple_of(jnp.clip(place, 0, MAXT - 1) * TILE, TILE)
            here = jnp.where(owner == z_ref[0], 1.0, 0.0)
            rows_of_tile = cot_ref[pl.ds(at, TILE), :].astype(jnp.float32) * here
            given_ref[tile * TILE : (tile + 1) * TILE, :] = rows_of_tile.astype(jnp.bfloat16)

    values = text_ref[...].astype(jnp.float32)
    sums_ref[...] = row_of(fold(values * values))


def opening(core, z, t, tile_counts, owner_map, text, hidden, cot, groups, n_sec, n_tp, stream):
    seq_len, columns = text.shape
    rows, features = hidden.shape
    half = rows // (groups * n_sec)
    share = cot.shape[1] // (n_sec * n_tp)
    step = 256
    part = [
        pl.BlockSpec((half, features), lambda i, c, *_, q=q: (q * n_sec + c[0], 0))
        for q in range(groups)
    ]
    return pl.pallas_call(
        opening_kernel,
        grid_spec=pltpu.PrefetchScalarGridSpec(
            num_scalar_prefetch=5,
            grid=(seq_len // step,),
            in_specs=[
                pl.BlockSpec((step, columns), lambda i, *_: (i, 0)),
                pl.BlockSpec((MAXT * TILE, share), lambda i, c, z, t, *_: (0, c[0] * n_tp + t[0])),
            ]
            + part,
            out_specs=[
                pl.BlockSpec((1, step), lambda i, *_: (0, i)),
                pl.BlockSpec((groups * half, features), lambda i, *_: (0, 0)),
                pl.BlockSpec((stream, share), lambda i, *_: (0, 0)),
            ],
        ),
        out_shape=[
            jax.ShapeDtypeStruct((1, seq_len), jnp.float32),
            jax.ShapeDtypeStruct((groups * half, features), jnp.bfloat16),
            jax.ShapeDtypeStruct((stream, share), jnp.bfloat16),
        ],
        compiler_params=pltpu.CompilerParams(vmem_limit_bytes=VMEM),
        cost_estimate=pl.CostEstimate(
            flops=2 * seq_len * columns + 40 * groups * half * features,
            bytes_accessed=2 * seq_len * columns,
            transcendentals=0,
        ),
    )(core, z, t, tile_counts, owner_map, text, cot, *[hidden] * groups)


def text_kernel(
    core_ref, z_ref, tiles_ref, texts_ref, owners_ref, text_ref, weight_ref, cot_ref, *refs
):
    del core_ref
    moment_ref, gain_ref, long_ref, scaled_ref = refs[-4:]
    squares = refs[:-4]
    seq_len, width = cot_ref.shape

    @pl.when(pl.program_id(0) == 0)
    def _():
        parts = [r[...] for r in squares]
        while len(parts) > 1:
            parts = [parts[i] + parts[i + 1] for i in range(0, len(parts), 2)]
        image_tiles = text_count = jnp.int32(0)
        for s in range(owners_ref.shape[0]):
            mine = owners_ref[s] == z_ref[0]
            image_tiles = jnp.where(mine, tiles_ref[s], image_tiles)
            text_count = jnp.where(mine, texts_ref[s], text_count)
        begin = pl.multiple_of(jnp.clip(image_tiles, 0, MAXT) * TILE, TILE)
        places = lax.broadcasted_iota(jnp.int32, (1, seq_len), 1)
        scale = lax.rsqrt(parts[0] / D + EPSILON)
        scale = columns_of(jnp.where(places < text_count, scale, 0.0), seq_len)
        long_ref[:seq_len, :] = cot_ref[...]
        long_ref[seq_len:, :] = jnp.zeros((MAXT * TILE, width), jnp.bfloat16)
        for i in range(width // LANES):
            lanes = slice(i * LANES, (i + 1) * LANES)
            shifted = long_ref[pl.ds(begin, seq_len), lanes]
            scaled_ref[:, lanes] = (shifted.astype(jnp.float32) * scale).astype(jnp.bfloat16)

    moment = lax.dot_general(
        text_ref[...], scaled_ref[...], (((0,), (0,)), ((), ())), preferred_element_type=jnp.float32
    )
    for i in range(moment_ref.shape[0]):
        moment_ref[i] = moment[:, i * LANES : (i + 1) * LANES].astype(jnp.bfloat16)
    gain_ref[...] = row_of(fold(moment * weight_ref[...].astype(jnp.float32)))


def text_product(scalars, text, weight, cot, squares, width):
    seq_len, columns = text.shape
    groups = width // LANES
    step = 256
    return pl.pallas_call(
        text_kernel,
        grid_spec=pltpu.PrefetchScalarGridSpec(
            num_scalar_prefetch=len(scalars),
            grid=(columns // step,),
            in_specs=[
                pl.BlockSpec((seq_len, step), lambda i, *_: (0, i)),
                pl.BlockSpec((step, width), lambda i, c, *_: (i, c[0])),
                pl.BlockSpec((seq_len, width), lambda i, c, *_: (0, c[0])),
            ]
            + [pl.BlockSpec((1, seq_len), lambda i, *_: (0, 0))] * len(squares),
            out_specs=[
                pl.BlockSpec((groups, step, LANES), lambda i, *_: (0, i, 0)),
                pl.BlockSpec((1, step), lambda i, *_: (0, i)),
            ],
            scratch_shapes=[
                pltpu.VMEM((seq_len + MAXT * TILE, width), jnp.bfloat16),
                pltpu.VMEM((seq_len, width), jnp.bfloat16),
            ],
        ),
        out_shape=[
            jax.ShapeDtypeStruct((groups, columns, LANES), jnp.bfloat16),
            jax.ShapeDtypeStruct((1, columns), jnp.float32),
        ],
        compiler_params=pltpu.CompilerParams(vmem_limit_bytes=VMEM),
        cost_estimate=pl.CostEstimate(
            flops=2 * seq_len * columns * width,
            bytes_accessed=2 * (seq_len * (columns + width) + 2 * columns * width),
            transcendentals=0,
        ),
    )(*scalars, text, weight, cot, *squares)


def sums_kernel(rows_ref, grad_ref, gain_ref, sums_ref):
    values = rows_ref[...].astype(jnp.float32)
    more = sums_ref.shape[1] - values.shape[0]
    for i, terms in enumerate((values * values, values * grad_ref[...] * gain_ref[...])):
        folded = jnp.concatenate([fold(terms), jnp.zeros((more, LANES), jnp.float32)], 0)
        sums_ref[i : i + 1, :] = row_of(folded)


def row_sums(rows, grad, gain):
    count, width = rows.shape
    padded = -(-count // LANES) * LANES
    whole = pl.BlockSpec(memory_space=pltpu.VMEM)
    return pl.pallas_call(
        sums_kernel,
        in_specs=[whole] * 3,
        out_specs=whole,
        out_shape=jax.ShapeDtypeStruct((2, padded), jnp.float32),
        compiler_params=pltpu.CompilerParams(vmem_limit_bytes=16 * 1024 * 1024),
        cost_estimate=pl.CostEstimate(
            flops=8 * count * width, bytes_accessed=6 * count * width, transcendentals=0
        ),
    )(rows, grad, gain)


def image_kernel(core_ref, grad_ref, gain_ref, cot_ref, sums_ref, rows_ref, *out):
    embed_ref, here_ref, there_ref, small_ref = out
    stream, width = rows_ref.shape
    groups = sums_ref.shape[0]
    size = stream // groups
    inv, mean = [], []
    for i in range(groups):
        inv_row = lax.rsqrt(sums_ref[i, 0:1, :] / D + EPSILON)
        mean_row = inv_row * inv_row * inv_row * sums_ref[i, 1:2, :] / D
        inv.append(columns_of(inv_row, inv_row.shape[1])[:size])
        mean.append(columns_of(mean_row, mean_row.shape[1])[:size])
    all_inv = jnp.concatenate(inv, 0)
    gain_parts = [jnp.zeros((1, LANES), jnp.float32)] * (width // LANES)
    bias_parts = list(gain_parts)
    for g in range(groups):
        rows = slice(g * size, (g + 1) * size)
        to = jnp.bitwise_xor(core_ref[0], g % 2) * (stream // 2) + (g // 2) * size
        to_rows = pl.ds(pl.multiple_of(to, 16), size)
        for i in range(width // LANES):
            at = slice(i * LANES, (i + 1) * LANES)
            values = rows_ref[rows, at].astype(jnp.float32)
            scaled = grad_ref[rows, at] * inv[g]
            embed = (scaled * gain_ref[:, at] - values * mean[g]).astype(jnp.bfloat16)
            embed_ref[to_rows, at] = embed
            gain_parts[i] = gain_parts[i] + jnp.sum(scaled * values, 0, keepdims=True)
            bias_parts[i] = bias_parts[i] + jnp.sum(embed.astype(jnp.float32), 0, keepdims=True)
    small_ref[0:1, :] = jnp.concatenate(gain_parts, 1)
    small_ref[1:2, :] = jnp.concatenate(bias_parts, 1)
    lanes = cot_ref.shape[1]
    wide = [all_inv] * (lanes // LANES) if lanes >= LANES else [all_inv[:, :lanes]]
    cot = (cot_ref[...].astype(jnp.float32) * jnp.concatenate(wide, 1)).astype(jnp.bfloat16)
    moment = lax.dot_general(
        rows_ref[...], cot, (((0,), (0,)), ((), ())), preferred_element_type=jnp.float32
    )
    share = here_ref.shape[1]
    here_ref[...] = moment[:, :share]
    there_ref[...] = moment[:, share:].astype(jnp.bfloat16)


def image_grads(core, grad, gain, cot, sums, rows):
    stream, width = grad.shape
    share = cot.shape[1] // 2
    whole = pl.BlockSpec(memory_space=pltpu.VMEM)
    return pl.pallas_call(
        image_kernel,
        in_specs=[pl.BlockSpec(memory_space=pltpu.SMEM)] + [whole] * 5,
        out_specs=[whole] * 4,
        out_shape=[
            jax.ShapeDtypeStruct((stream, width), jnp.bfloat16),
            jax.ShapeDtypeStruct((width, share), jnp.float32),
            jax.ShapeDtypeStruct((width, share), jnp.bfloat16),
            jax.ShapeDtypeStruct((2, width), jnp.float32),
        ],
        compiler_params=pltpu.CompilerParams(vmem_limit_bytes=56 * 1024 * 1024),
        cost_estimate=pl.CostEstimate(
            flops=4 * stream * width * share, bytes_accessed=8 * stream * width, transcendentals=0
        ),
    )(core, grad, gain, cot, sums, rows)


def weight_kernel(act_ref, grad_ref, out_ref):
    step = act_ref.shape[0]
    groups = grad_ref.shape[1] // LANES
    product = jnp.dot(act_ref[...], grad_ref[...], preferred_element_type=jnp.float32)
    for c in range(groups):
        out_ref[pl.ds(c, step, stride=groups), :] = product[:, c * LANES : (c + 1) * LANES]


def weight_product(act, grad):
    features, rows = act.shape
    width = grad.shape[1]
    groups = width // LANES
    step = 256
    return pl.pallas_call(
        weight_kernel,
        grid=(features // step,),
        in_specs=[
            pl.BlockSpec((step, rows), lambda i: (i, 0)),
            pl.BlockSpec((rows, width), lambda i: (0, 0)),
        ],
        out_specs=pl.BlockSpec((step * groups, LANES), lambda i: (i, 0)),
        out_shape=jax.ShapeDtypeStruct((features * groups, LANES), jnp.float32),
        compiler_params=pltpu.CompilerParams(vmem_limit_bytes=VMEM),
        cost_estimate=pl.CostEstimate(
            flops=2 * rows * features * width,
            bytes_accessed=4 * features * width + 2 * rows * (features + width),
            transcendentals=0,
        ),
    )(act, grad)


def on_device(
    vis_hidden,
    proj_weight,
    proj_bias,
    text_embed,
    norm_gain,
    key_weight,
    key_cotangent,
    tile_counts,
    text_counts,
    owner_map,
):
    f32, bf16 = jnp.float32, jnp.bfloat16
    n_sec, n_seq, n_tp = (lax.axis_size(a) for a in ("sec", "seq", "tp"))
    core, z, t = (lax.axis_index(a) for a in ("sec", "seq", "tp"))
    block_rows, features = vis_hidden.shape
    columns = proj_weight.shape[1]
    col_half = columns // n_sec
    stream = block_rows * n_tp
    own = stream // n_seq
    half = own // n_sec
    groups = block_rows // own
    keys = key_weight.shape[1]
    key_half = keys // n_sec
    seq_len = text_embed.shape[0]

    text_sq, act, given = opening(
        core[None], z[None], t[None], tile_counts, owner_map,
        text_embed, vis_hidden, key_cotangent, groups, n_sec, n_tp, stream,
    )
    pieces = [act] + [swap(act, "tp", m) for m in range(1, n_tp)]
    pieces[1], text_sq = together(pieces[1], text_sq)
    text_sq = [text_sq] + [swap(text_sq, "tp", m) for m in range(1, n_tp)]
    partial, act_mine = project(t[None], pieces, proj_weight)
    text_sq[0], given, act_mine, partial = together(text_sq[0], given, act_mine, partial)
    summed = lax.psum_scatter(partial, "seq", scatter_dimension=0, tiled=True)

    scalars = (core[None], z[None], tile_counts, text_counts, owner_map)
    moment, gain_text = text_product(
        scalars, text_embed, key_weight, key_cotangent, text_sq, key_half
    )
    if n_seq <= 4:
        way = line_step(moment, "seq", 1, None)
    else:
        share = key_half // n_seq
        moment = moment.reshape(-1, columns, LANES // share, share).transpose(0, 2, 1, 3)
        moment = reduce_to_owner(moment.reshape(n_seq, columns, share), "seq")

    taken = butterfly(given, ("seq",))
    key_bias_part = jnp.sum(key_cotangent.astype(f32), 0)
    early = jnp.concatenate([gain_text[0], jnp.where(core == 0, key_bias_part, 0.0)])

    act_other = swap(act_mine, "sec", 1)
    taken = [taken] + [swap(taken, "tp", m) for m in range(1, n_tp)]
    half_cot = jnp.concatenate(in_order(taken, t), 1)
    other_cot = swap(half_cot, "sec", 1)
    image_cot = jnp.concatenate(in_order([half_cot, other_cot], core), 1)
    weight_rows = lax.dynamic_slice_in_dim(key_weight, core * col_half, col_half, 0)
    normed_grad = lax.dot_general(
        image_cot, weight_rows, (((1,), (1,)), ((), ())), preferred_element_type=f32
    )
    own_cot = lax.dynamic_slice_in_dim(image_cot, (z * n_sec + core) * half, half, 0)
    own_grad = lax.dot_general(
        own_cot, key_weight, (((1,), (1,)), ((), ())), preferred_element_type=f32
    )
    key_share = key_half // n_seq
    cot_own = jnp.concatenate(
        [lax.dynamic_slice_in_dim(c, z * key_share, key_share, 1) for c in (half_cot, other_cot)], 1
    )

    image_mine = (summed.astype(f32) + proj_bias).astype(bf16)
    if n_seq <= 4:
        way[0], way[1], image_mine = together(*way, image_mine)
        way = line_step(moment, "seq", 2, way)
    low, high = image_mine[:, :col_half], image_mine[:, col_half:]
    first_core = core == 0
    came = swap(jnp.where(first_core, high, low), "sec", 1)
    image = jnp.concatenate(in_order([jnp.where(first_core, low, high), came], core), 0)
    rows = lax.all_gather(image, "seq", axis=0, tiled=True)

    sums = total(row_sums(image_mine, own_grad, norm_gain[None]), "tp")
    size = sums.size
    sums = jnp.concatenate([sums.reshape(-1), early])
    if n_seq <= 4:
        sums = jnp.stack(in_order([sums] + [swap(sums, "seq", m) for m in range(1, n_seq)], z), 0)
    else:
        sums = lax.all_gather(sums, "seq", axis=0, tiled=False)
    early = jnp.sum(sums[:, size:], 0)
    sums = jnp.concatenate([sums[:, :size].reshape(-1), early])
    sums = jnp.stack(in_order([sums, swap(sums, "sec", 1)], core), 0)
    early = jnp.sum(sums[:, n_seq * size :], 0)
    sums = sums[:, : n_seq * size].reshape(n_sec, n_seq, 2, -1).transpose(1, 0, 2, 3)
    sums = sums.reshape(n_seq * n_sec, 2, -1)

    if n_seq <= 4:
        way[0], way[1], rows = together(*way, rows)
        for step in range(3, n_seq):
            way = line_step(moment, "seq", step, way)
        moment = lax.dynamic_index_in_dim(moment, z, 0, keepdims=False).astype(f32)
        moment = moment + way[0].astype(f32) + way[1].astype(f32)
    gain_half = lax.dynamic_slice_in_dim(norm_gain, core * col_half, col_half, 0)[None]
    embed_grad, here, there, small = image_grads(
        core[None], normed_grad, gain_half, cot_own, sums, rows
    )
    there = swap(there, "sec", 1)
    small_other = swap(small, "sec", 1)
    act_turned = jnp.concatenate([act_mine, act_other], 0).T
    weight_grad = weight_product(act_turned, embed_grad)
    proj_weight_grad = weight_grad.reshape(features, 1, 1, col_half)

    both = in_order([here, there.astype(f32)], core)
    key_weight_grad = (moment + jnp.concatenate(both, 0)) * norm_gain[:, None]
    gain_image, proj_bias_grad = jnp.concatenate(in_order([small, small_other], core), 1)
    gain_grad = early[:columns] + gain_image
    key_bias_grad = early[columns:]
    return (proj_weight_grad, proj_bias_grad, key_weight_grad, key_bias_grad, gain_grad)


def solution(mesh):
    placed = (
        P("tp", "seq"),
        P("seq", "tp"),
        P("tp"),
        P("seq", "tp"),
        P("tp"),
        P("tp", None),
        P("seq", None),
        P(),
        P(),
        P(),
    )
    return jax.shard_map(
        on_device,
        mesh=mesh,
        in_specs=placed,
        out_specs=(P("seq", "tp", "sec", None), P("tp"), P("tp", ("sec", "seq")), P(), P("tp")),
        check_vma=False,
    )
```

```python
import jax
import jax.numpy as jnp
from jax import lax
from jax.experimental import pallas as pl
from jax.experimental.pallas import tpu as pltpu
from jax.sharding import PartitionSpec as P

D = 8192
TILE = 256
MAXT = 2
LANES = 128
EPSILON = 1e-06
VMEM = 32 * 1024 * 1024


def swap(x, axis, mask):
    count = lax.axis_size(axis)
    return lax.ppermute(x, axis, [(i, i ^ mask) for i in range(count)])


def total(x, axis):
    pieces = [x] + [swap(x, axis, m) for m in range(1, lax.axis_size(axis))]
    while len(pieces) > 1:
        pieces = [pieces[i] + pieces[i + 1] for i in range(0, len(pieces), 2)]
    return pieces[0]


def butterfly(x, axes):
    for axis in axes:
        mask = 1
        while mask < lax.axis_size(axis):
            x = x + swap(x, axis, mask)
            mask *= 2
    return x


def in_order(pieces, index):
    pieces = list(pieces)
    mask = 1
    while mask < len(pieces):
        odd = (index & mask) != 0
        pieces = [jnp.where(odd, pieces[m ^ mask], pieces[m]) for m in range(len(pieces))]
        mask *= 2
    return pieces


def together(*values):
    return lax.optimization_barrier(values)


def reduce_to_owner(parts, axis):
    index = lax.axis_index(axis)
    count = parts.shape[0]
    while count > 1:
        pairs = parts.reshape(count // 2, 2, *parts.shape[1:])
        mask = lax.axis_size(axis) // count
        bit = (index // mask) % 2
        sent = lax.dynamic_index_in_dim(pairs, 1 - bit, 1, keepdims=False)
        kept = lax.dynamic_index_in_dim(pairs, bit, 1, keepdims=False)
        came = swap(sent.astype(jnp.bfloat16), axis, mask)
        parts = kept.astype(jnp.float32) + came.astype(jnp.float32)
        count //= 2
    return parts[0]


def line_step(parts, axis, step, before):
    count = lax.axis_size(axis)
    index = lax.axis_index(axis)
    out = []
    for sign in (1, -1):
        place = index + sign * (count - step)
        place = jnp.clip(place, 0, count - 1)
        sent = lax.dynamic_index_in_dim(parts, place, 0, keepdims=False)
        if before is not None:
            sent = (sent.astype(jnp.float32) + before[len(out)].astype(jnp.float32)).astype(sent.dtype)
        first = 0 if sign > 0 else count - 1
        pairs = [(first + sign * j, first + sign * (j + 1)) for j in range(step)]
        out.append(lax.ppermute(sent, axis, pairs))
    return out


def columns_of(row, count):
    parts = []
    for i in range(count // LANES):
        part = row[:, i * LANES : (i + 1) * LANES]
        parts.append(jnp.broadcast_to(part, (LANES, LANES)).T)
    return jnp.concatenate(parts, 0)


def row_of(folded):
    count = folded.shape[0]
    parts = [
        jnp.sum(folded[i * LANES : (i + 1) * LANES, :].T, 0, keepdims=True)
        for i in range(count // LANES)
    ]
    return jnp.concatenate(parts, 1)


def fold(values):
    width = values.shape[1]
    out = values[:, :LANES]
    for i in range(1, width // LANES):
        out = out + values[:, i * LANES : (i + 1) * LANES]
    return out


def project_kernel(*refs):
    index_ref, weight_ref = refs[:2]
    partial_ref, act_ref = refs[-2:]
    pieces = refs[2:-2]
    rows = pieces[0].shape[0]

    @pl.when(pl.program_id(0) == 0)
    def _():
        for m, piece in enumerate(pieces):
            at = jnp.bitwise_xor(index_ref[0], m) * rows
            act_ref[pl.ds(pl.multiple_of(at, rows), rows), :] = piece[...]

    product = jnp.dot(act_ref[...], weight_ref[...], preferred_element_type=jnp.float32)
    partial_ref[...] = product.astype(jnp.bfloat16)


def project(index, pieces, weight):
    rows, features = pieces[0].shape
    columns = weight.shape[1]
    total_rows = rows * len(pieces)
    step = 512
    return pl.pallas_call(
        project_kernel,
        grid=(columns // step,),
        in_specs=[
            pl.BlockSpec(memory_space=pltpu.SMEM),
            pl.BlockSpec((features, step), lambda i: (0, i)),
        ]
        + [pl.BlockSpec((rows, features), lambda i: (0, 0))] * len(pieces),
        out_specs=[
            pl.BlockSpec((total_rows, step), lambda i: (0, i)),
            pl.BlockSpec((total_rows, features), lambda i: (0, 0)),
        ],
        out_shape=[
            jax.ShapeDtypeStruct((total_rows, columns), jnp.bfloat16),
            jax.ShapeDtypeStruct((total_rows, features), jnp.bfloat16),
        ],
        compiler_params=pltpu.CompilerParams(vmem_limit_bytes=VMEM),
        cost_estimate=pl.CostEstimate(
            flops=2 * total_rows * features * columns,
            bytes_accessed=2 * (features * columns + total_rows * (columns + 2 * features)),
            transcendentals=0,
        ),
    )(index, weight, *pieces)


def opening_kernel(
    core_ref, z_ref, t_ref, tiles_ref, owners_ref, text_ref, cot_ref, *refs
):
    del core_ref, t_ref
    sums_ref, act_ref, given_ref = refs[-3:]
    groups = refs[:-3]

    @pl.when(pl.program_id(0) == 0)
    def _():
        rows = groups[0].shape[0]
        for i, group in enumerate(groups):
            hidden = group[...].astype(jnp.float32)
            act = 0.5 * hidden * (1.0 + lax.erf(hidden * 0.7071067811865476))
            act_ref[i * rows : (i + 1) * rows, :] = act.astype(jnp.bfloat16)
        for tile in range(given_ref.shape[0] // TILE):
            start = owner = place = jnp.int32(0)
            for s in range(tiles_ref.shape[0]):
                inside = (tile >= start) & (tile < start + tiles_ref[s])
                owner = jnp.where(inside, owners_ref[s], owner)
                place = jnp.where(inside, tile - start, place)
                start = start + tiles_ref[s]
            at = pl.multiple_of(jnp.clip(place, 0, MAXT - 1) * TILE, TILE)
            here = jnp.where(owner == z_ref[0], 1.0, 0.0)
            rows_of_tile = cot_ref[pl.ds(at, TILE), :].astype(jnp.float32) * here
            given_ref[tile * TILE : (tile + 1) * TILE, :] = rows_of_tile.astype(jnp.bfloat16)

    values = text_ref[...].astype(jnp.float32)
    sums_ref[...] = row_of(fold(values * values))


def opening(core, z, t, tile_counts, owner_map, text, hidden, cot, groups, n_sec, n_tp, stream):
    seq_len, columns = text.shape
    rows, features = hidden.shape
    half = rows // (groups * n_sec)
    share = cot.shape[1] // (n_sec * n_tp)
    step = 256
    part = [
        pl.BlockSpec((half, features), lambda i, c, *_, q=q: (q * n_sec + c[0], 0))
        for q in range(groups)
    ]
    return pl.pallas_call(
        opening_kernel,
        grid_spec=pltpu.PrefetchScalarGridSpec(
            num_scalar_prefetch=5,
            grid=(seq_len // step,),
            in_specs=[
                pl.BlockSpec((step, columns), lambda i, *_: (i, 0)),
                pl.BlockSpec((MAXT * TILE, share), lambda i, c, z, t, *_: (0, c[0] * n_tp + t[0])),
            ]
            + part,
            out_specs=[
                pl.BlockSpec((1, step), lambda i, *_: (0, i)),
                pl.BlockSpec((groups * half, features), lambda i, *_: (0, 0)),
                pl.BlockSpec((stream, share), lambda i, *_: (0, 0)),
            ],
        ),
        out_shape=[
            jax.ShapeDtypeStruct((1, seq_len), jnp.float32),
            jax.ShapeDtypeStruct((groups * half, features), jnp.bfloat16),
            jax.ShapeDtypeStruct((stream, share), jnp.bfloat16),
        ],
        compiler_params=pltpu.CompilerParams(vmem_limit_bytes=VMEM),
        cost_estimate=pl.CostEstimate(
            flops=2 * seq_len * columns + 40 * groups * half * features,
            bytes_accessed=2 * seq_len * columns,
            transcendentals=0,
        ),
    )(core, z, t, tile_counts, owner_map, text, cot, *[hidden] * groups)


def text_kernel(
    core_ref, z_ref, tiles_ref, texts_ref, owners_ref, text_ref, weight_ref, cot_ref, *refs
):
    del core_ref
    moment_ref, gain_ref, long_ref, scaled_ref = refs[-4:]
    squares = refs[:-4]
    seq_len, width = cot_ref.shape

    @pl.when(pl.program_id(0) == 0)
    def _():
        parts = [r[...] for r in squares]
        while len(parts) > 1:
            parts = [parts[i] + parts[i + 1] for i in range(0, len(parts), 2)]
        image_tiles = text_count = jnp.int32(0)
        for s in range(owners_ref.shape[0]):
            mine = owners_ref[s] == z_ref[0]
            image_tiles = jnp.where(mine, tiles_ref[s], image_tiles)
            text_count = jnp.where(mine, texts_ref[s], text_count)
        begin = pl.multiple_of(jnp.clip(image_tiles, 0, MAXT) * TILE, TILE)
        places = lax.broadcasted_iota(jnp.int32, (1, seq_len), 1)
        scale = lax.rsqrt(parts[0] / D + EPSILON)
        scale = columns_of(jnp.where(places < text_count, scale, 0.0), seq_len)
        long_ref[:seq_len, :] = cot_ref[...]
        long_ref[seq_len:, :] = jnp.zeros((MAXT * TILE, width), jnp.bfloat16)
        for i in range(width // LANES):
            lanes = slice(i * LANES, (i + 1) * LANES)
            shifted = long_ref[pl.ds(begin, seq_len), lanes]
            scaled_ref[:, lanes] = (shifted.astype(jnp.float32) * scale).astype(jnp.bfloat16)

    moment = lax.dot_general(
        text_ref[...], scaled_ref[...], (((0,), (0,)), ((), ())), preferred_element_type=jnp.float32
    )
    for i in range(moment_ref.shape[0]):
        moment_ref[i] = moment[:, i * LANES : (i + 1) * LANES].astype(jnp.bfloat16)
    gain_ref[...] = row_of(fold(moment * weight_ref[...].astype(jnp.float32)))


def text_product(scalars, text, weight, cot, squares, width):
    seq_len, columns = text.shape
    groups = width // LANES
    step = 256
    return pl.pallas_call(
        text_kernel,
        grid_spec=pltpu.PrefetchScalarGridSpec(
            num_scalar_prefetch=len(scalars),
            grid=(columns // step,),
            in_specs=[
                pl.BlockSpec((seq_len, step), lambda i, *_: (0, i)),
                pl.BlockSpec((step, width), lambda i, c, *_: (i, c[0])),
                pl.BlockSpec((seq_len, width), lambda i, c, *_: (0, c[0])),
            ]
            + [pl.BlockSpec((1, seq_len), lambda i, *_: (0, 0))] * len(squares),
            out_specs=[
                pl.BlockSpec((groups, step, LANES), lambda i, *_: (0, i, 0)),
                pl.BlockSpec((1, step), lambda i, *_: (0, i)),
            ],
            scratch_shapes=[
                pltpu.VMEM((seq_len + MAXT * TILE, width), jnp.bfloat16),
                pltpu.VMEM((seq_len, width), jnp.bfloat16),
            ],
        ),
        out_shape=[
            jax.ShapeDtypeStruct((groups, columns, LANES), jnp.bfloat16),
            jax.ShapeDtypeStruct((1, columns), jnp.float32),
        ],
        compiler_params=pltpu.CompilerParams(vmem_limit_bytes=VMEM),
        cost_estimate=pl.CostEstimate(
            flops=2 * seq_len * columns * width,
            bytes_accessed=2 * (seq_len * (columns + width) + 2 * columns * width),
            transcendentals=0,
        ),
    )(*scalars, text, weight, cot, *squares)


def sums_kernel(rows_ref, grad_ref, gain_ref, sums_ref):
    values = rows_ref[...].astype(jnp.float32)
    more = sums_ref.shape[1] - values.shape[0]
    for i, terms in enumerate((values * values, values * grad_ref[...] * gain_ref[...])):
        folded = jnp.concatenate([fold(terms), jnp.zeros((more, LANES), jnp.float32)], 0)
        sums_ref[i : i + 1, :] = row_of(folded)


def row_sums(rows, grad, gain):
    count, width = rows.shape
    padded = -(-count // LANES) * LANES
    whole = pl.BlockSpec(memory_space=pltpu.VMEM)
    return pl.pallas_call(
        sums_kernel,
        in_specs=[whole] * 3,
        out_specs=whole,
        out_shape=jax.ShapeDtypeStruct((2, padded), jnp.float32),
        compiler_params=pltpu.CompilerParams(vmem_limit_bytes=16 * 1024 * 1024),
        cost_estimate=pl.CostEstimate(
            flops=8 * count * width, bytes_accessed=6 * count * width, transcendentals=0
        ),
    )(rows, grad, gain)


def image_kernel(core_ref, grad_ref, gain_ref, cot_ref, sums_ref, rows_ref, *out):
    embed_ref, here_ref, there_ref, small_ref = out
    stream, width = rows_ref.shape
    groups = sums_ref.shape[0]
    size = stream // groups
    inv, mean = [], []
    for i in range(groups):
        inv_row = lax.rsqrt(sums_ref[i, 0:1, :] / D + EPSILON)
        mean_row = inv_row * inv_row * inv_row * sums_ref[i, 1:2, :] / D
        inv.append(columns_of(inv_row, inv_row.shape[1])[:size])
        mean.append(columns_of(mean_row, mean_row.shape[1])[:size])
    all_inv = jnp.concatenate(inv, 0)
    gain_parts = [jnp.zeros((1, LANES), jnp.float32)] * (width // LANES)
    bias_parts = list(gain_parts)
    for g in range(groups):
        rows = slice(g * size, (g + 1) * size)
        to = jnp.bitwise_xor(core_ref[0], g % 2) * (stream // 2) + (g // 2) * size
        to_rows = pl.ds(pl.multiple_of(to, 16), size)
        for i in range(width // LANES):
            at = slice(i * LANES, (i + 1) * LANES)
            values = rows_ref[rows, at].astype(jnp.float32)
            scaled = grad_ref[rows, at] * inv[g]
            embed = (scaled * gain_ref[:, at] - values * mean[g]).astype(jnp.bfloat16)
            embed_ref[to_rows, at] = embed
            gain_parts[i] = gain_parts[i] + jnp.sum(scaled * values, 0, keepdims=True)
            bias_parts[i] = bias_parts[i] + jnp.sum(embed.astype(jnp.float32), 0, keepdims=True)
    small_ref[0:1, :] = jnp.concatenate(gain_parts, 1)
    small_ref[1:2, :] = jnp.concatenate(bias_parts, 1)
    lanes = cot_ref.shape[1]
    wide = [all_inv] * (lanes // LANES) if lanes >= LANES else [all_inv[:, :lanes]]
    cot = (cot_ref[...].astype(jnp.float32) * jnp.concatenate(wide, 1)).astype(jnp.bfloat16)
    moment = lax.dot_general(
        rows_ref[...], cot, (((0,), (0,)), ((), ())), preferred_element_type=jnp.float32
    )
    share = here_ref.shape[1]
    here_ref[...] = moment[:, :share]
    there_ref[...] = moment[:, share:].astype(jnp.bfloat16)


def image_grads(core, grad, gain, cot, sums, rows):
    stream, width = grad.shape
    share = cot.shape[1] // 2
    whole = pl.BlockSpec(memory_space=pltpu.VMEM)
    return pl.pallas_call(
        image_kernel,
        in_specs=[pl.BlockSpec(memory_space=pltpu.SMEM)] + [whole] * 5,
        out_specs=[whole] * 4,
        out_shape=[
            jax.ShapeDtypeStruct((stream, width), jnp.bfloat16),
            jax.ShapeDtypeStruct((width, share), jnp.float32),
            jax.ShapeDtypeStruct((width, share), jnp.bfloat16),
            jax.ShapeDtypeStruct((2, width), jnp.float32),
        ],
        compiler_params=pltpu.CompilerParams(vmem_limit_bytes=56 * 1024 * 1024),
        cost_estimate=pl.CostEstimate(
            flops=4 * stream * width * share, bytes_accessed=8 * stream * width, transcendentals=0
        ),
    )(core, grad, gain, cot, sums, rows)


def weight_kernel(act_ref, grad_ref, out_ref):
    step = act_ref.shape[0]
    groups = grad_ref.shape[1] // LANES
    product = jnp.dot(act_ref[...], grad_ref[...], preferred_element_type=jnp.float32)
    for c in range(groups):
        out_ref[pl.ds(c, step, stride=groups), :] = product[:, c * LANES : (c + 1) * LANES]


def weight_product(act, grad):
    features, rows = act.shape
    width = grad.shape[1]
    groups = width // LANES
    step = 256
    return pl.pallas_call(
        weight_kernel,
        grid=(features // step,),
        in_specs=[
            pl.BlockSpec((step, rows), lambda i: (i, 0)),
            pl.BlockSpec((rows, width), lambda i: (0, 0)),
        ],
        out_specs=pl.BlockSpec((step * groups, LANES), lambda i: (i, 0)),
        out_shape=jax.ShapeDtypeStruct((features * groups, LANES), jnp.float32),
        compiler_params=pltpu.CompilerParams(vmem_limit_bytes=VMEM),
        cost_estimate=pl.CostEstimate(
            flops=2 * rows * features * width,
            bytes_accessed=4 * features * width + 2 * rows * (features + width),
            transcendentals=0,
        ),
    )(act, grad)


def on_device(
    vis_hidden,
    proj_weight,
    proj_bias,
    text_embed,
    norm_gain,
    key_weight,
    key_cotangent,
    tile_counts,
    text_counts,
    owner_map,
):
    f32, bf16 = jnp.float32, jnp.bfloat16
    n_sec, n_seq, n_tp = (lax.axis_size(a) for a in ("sec", "seq", "tp"))
    core, z, t = (lax.axis_index(a) for a in ("sec", "seq", "tp"))
    block_rows, features = vis_hidden.shape
    columns = proj_weight.shape[1]
    col_half = columns // n_sec
    stream = block_rows * n_tp
    own = stream // n_seq
    half = own // n_sec
    groups = block_rows // own
    keys = key_weight.shape[1]
    key_half = keys // n_sec
    seq_len = text_embed.shape[0]

    text_sq, act, given = opening(
        core[None], z[None], t[None], tile_counts, owner_map,
        text_embed, vis_hidden, key_cotangent, groups, n_sec, n_tp, stream,
    )
    pieces = [act] + [swap(act, "tp", m) for m in range(1, n_tp)]
    text_sq = [text_sq] + [swap(text_sq, "tp", m) for m in range(1, n_tp)]
    text_sq[0], pieces[1] = together(text_sq[0], pieces[1])

    scalars = (core[None], z[None], tile_counts, text_counts, owner_map)
    moment, gain_text = text_product(
        scalars, text_embed, key_weight, key_cotangent, text_sq, key_half
    )
    given, moment = together(given, moment)
    taken = butterfly(given, ("seq",))
    if n_seq <= 4:
        way = line_step(moment, "seq", 1, None)
    else:
        share = key_half // n_seq
        moment = moment.reshape(-1, columns, LANES // share, share).transpose(0, 2, 1, 3)
        moment = reduce_to_owner(moment.reshape(n_seq, columns, share), "seq")

    partial, act_mine = project(t[None], pieces, proj_weight)
    if n_seq <= 4:
        way[0], way[1], act_mine, partial = together(*way, act_mine, partial)
        way = line_step(moment, "seq", 2, way)
    taken, act_mine, partial = together(taken, act_mine, partial)
    summed = lax.psum_scatter(partial, "seq", scatter_dimension=0, tiled=True)

    key_bias_part = jnp.sum(key_cotangent.astype(f32), 0)
    early = jnp.concatenate([gain_text[0], jnp.where(core == 0, key_bias_part, 0.0)])

    act_other = swap(act_mine, "sec", 1)
    taken = [taken] + [swap(taken, "tp", m) for m in range(1, n_tp)]
    half_cot = jnp.concatenate(in_order(taken, t), 1)
    other_cot = swap(half_cot, "sec", 1)
    image_cot = jnp.concatenate(in_order([half_cot, other_cot], core), 1)
    weight_rows = lax.dynamic_slice_in_dim(key_weight, core * col_half, col_half, 0)
    normed_grad = lax.dot_general(
        image_cot, weight_rows, (((1,), (1,)), ((), ())), preferred_element_type=f32
    )
    own_cot = lax.dynamic_slice_in_dim(image_cot, (z * n_sec + core) * half, half, 0)
    own_grad = lax.dot_general(
        own_cot, key_weight, (((1,), (1,)), ((), ())), preferred_element_type=f32
    )
    key_share = key_half // n_seq
    cot_own = jnp.concatenate(
        [lax.dynamic_slice_in_dim(c, z * key_share, key_share, 1) for c in (half_cot, other_cot)], 1
    )

    summed, normed_grad, own_grad = together(summed, normed_grad, own_grad)
    image_mine = (summed.astype(f32) + proj_bias).astype(bf16)
    if n_seq <= 4:
        way[0], way[1], image_mine = together(*way, image_mine)
    low, high = image_mine[:, :col_half], image_mine[:, col_half:]
    first_core = core == 0
    came = swap(jnp.where(first_core, high, low), "sec", 1)
    image = jnp.concatenate(in_order([jnp.where(first_core, low, high), came], core), 0)
    rows = lax.all_gather(image, "seq", axis=0, tiled=True)

    image_mine, came = together(image_mine, came)
    sums = total(row_sums(image_mine, own_grad, norm_gain[None]), "tp")
    size = sums.size
    sums = jnp.concatenate([sums.reshape(-1), early])
    if n_seq <= 4:
        sums = jnp.stack(in_order([sums] + [swap(sums, "seq", m) for m in range(1, n_seq)], z), 0)
    else:
        sums = lax.all_gather(sums, "seq", axis=0, tiled=False)
    early = jnp.sum(sums[:, size:], 0)
    sums = jnp.concatenate([sums[:, :size].reshape(-1), early])
    sums = jnp.stack(in_order([sums, swap(sums, "sec", 1)], core), 0)
    early = jnp.sum(sums[:, n_seq * size :], 0)
    sums = sums[:, : n_seq * size].reshape(n_sec, n_seq, 2, -1).transpose(1, 0, 2, 3)
    sums = sums.reshape(n_seq * n_sec, 2, -1)

    if n_seq <= 4:
        for step in range(3, n_seq):
            way = line_step(moment, "seq", step, way)
        moment = lax.dynamic_index_in_dim(moment, z, 0, keepdims=False).astype(f32)
        moment = moment + way[0].astype(f32) + way[1].astype(f32)
    gain_half = lax.dynamic_slice_in_dim(norm_gain, core * col_half, col_half, 0)[None]
    embed_grad, here, there, small = image_grads(
        core[None], normed_grad, gain_half, cot_own, sums, rows
    )
    there = swap(there, "sec", 1)
    small_other = swap(small, "sec", 1)
    act_turned = jnp.concatenate([act_mine, act_other], 0).T
    weight_grad = weight_product(act_turned, embed_grad)
    proj_weight_grad = weight_grad.reshape(features, 1, 1, col_half)

    both = in_order([here, there.astype(f32)], core)
    key_weight_grad = (moment + jnp.concatenate(both, 0)) * norm_gain[:, None]
    gain_image, proj_bias_grad = jnp.concatenate(in_order([small, small_other], core), 1)
    gain_grad = early[:columns] + gain_image
    key_bias_grad = early[columns:]
    return (proj_weight_grad, proj_bias_grad, key_weight_grad, key_bias_grad, gain_grad)


def solution(mesh):
    placed = (
        P("tp", "seq"),
        P("seq", "tp"),
        P("tp"),
        P("seq", "tp"),
        P("tp"),
        P("tp", None),
        P("seq", None),
        P(),
        P(),
        P(),
    )
    return jax.shard_map(
        on_device,
        mesh=mesh,
        in_specs=placed,
        out_specs=(P("seq", "tp", "sec", None), P("tp"), P("tp", ("sec", "seq")), P(), P("tp")),
        check_vma=False,
    )
```

```python
import jax
import jax.numpy as jnp
from jax import lax
from jax.experimental import pallas as pl
from jax.experimental.pallas import tpu as pltpu
from jax.sharding import PartitionSpec as P

D = 8192
TILE = 256
MAXT = 2
LANES = 128
EPSILON = 1e-06


def swap(x, axis, mask):
    count = lax.axis_size(axis)
    return lax.ppermute(x, axis, [(i, i ^ mask) for i in range(count)])


def total(x, axis):
    pieces = [x] + [swap(x, axis, m) for m in range(1, lax.axis_size(axis))]
    while len(pieces) > 1:
        pieces = [pieces[i] + pieces[i + 1] for i in range(0, len(pieces), 2)]
    return pieces[0]


def butterfly(x, axes):
    for axis in axes:
        mask = 1
        while mask < lax.axis_size(axis):
            x = x + swap(x, axis, mask)
            mask *= 2
    return x


def in_order(pieces, index):
    pieces = list(pieces)
    mask = 1
    while mask < len(pieces):
        odd = (index & mask) != 0
        pieces = [jnp.where(odd, pieces[m ^ mask], pieces[m]) for m in range(len(pieces))]
        mask *= 2
    return pieces


def reduce_to_owner(parts, axis):
    index = lax.axis_index(axis)
    count = parts.shape[0]
    while count > 1:
        pairs = parts.reshape(count // 2, 2, *parts.shape[1:])
        mask = lax.axis_size(axis) // count
        bit = (index // mask) % 2
        sent = lax.dynamic_index_in_dim(pairs, 1 - bit, 1, keepdims=False)
        kept = lax.dynamic_index_in_dim(pairs, bit, 1, keepdims=False)
        came = swap(sent.astype(jnp.bfloat16), axis, mask)
        parts = kept.astype(jnp.float32) + came.astype(jnp.float32)
        count //= 2
    return parts[0]


def along_line(x, axis):
    count = lax.axis_size(axis)
    up, down = [], []
    right = left = x
    for i in range(1, count):
        right = lax.ppermute(right, axis, [(j, j + 1) for j in range(i - 1, count - 1)])
        left = lax.ppermute(left, axis, [(j, j - 1) for j in range(1, count - i + 1)])
        up.append(right)
        down.append(left)
    return up, down


def weight_kernel(*refs):
    act_ref, own_ref, out_ref, grad_ref = refs[0], refs[1], refs[-2], refs[-1]
    others = refs[2:-2]
    count = len(others) // 2
    rows, width = own_ref.shape

    @pl.when(pl.program_id(0) == 0)
    def _():
        grad_ref[:rows, :] = own_ref[...]
        for i in range(count):
            grad_ref[(i + 1) * rows : (i + 2) * rows, :] = (
                others[i][...] + others[count + count - 1 - i][...]
            )

    step = act_ref.shape[1]
    groups = width // LANES
    product = lax.dot_general(
        act_ref[...], grad_ref[...], (((0,), (0,)), ((), ())), preferred_element_type=jnp.float32
    )
    for c in range(groups):
        out_ref[pl.ds(c, step, stride=groups), :] = product[:, c * LANES : (c + 1) * LANES]


def weight_product(act, own, others):
    rows, features = act.shape
    width = own.shape[1]
    groups = width // LANES
    step = 256
    piece = pl.BlockSpec(own.shape, lambda i: (0, 0))
    return pl.pallas_call(
        weight_kernel,
        grid=(features // step,),
        in_specs=[pl.BlockSpec((rows, step), lambda i: (0, i))] + [piece] * (1 + len(others)),
        out_specs=pl.BlockSpec((step * groups, LANES), lambda i: (i, 0)),
        out_shape=jax.ShapeDtypeStruct((features * groups, LANES), jnp.float32),
        scratch_shapes=[pltpu.VMEM((rows, width), jnp.bfloat16)],
        compiler_params=pltpu.CompilerParams(vmem_limit_bytes=40 * 1024 * 1024),
        cost_estimate=pl.CostEstimate(
            flops=2 * rows * features * width,
            bytes_accessed=4 * features * width + 2 * rows * (features + width),
            transcendentals=0,
        ),
    )(act, own, *others)


def on_device(
    vis_hidden,
    proj_weight,
    proj_bias,
    text_embed,
    norm_gain,
    key_weight,
    key_cotangent,
    tile_counts,
    text_counts,
    owner_map,
):
    f32, bf16 = jnp.float32, jnp.bfloat16
    n_sec, n_seq, n_tp = (lax.axis_size(a) for a in ("sec", "seq", "tp"))
    core, z, t = (lax.axis_index(a) for a in ("sec", "seq", "tp"))
    block_rows, features = vis_hidden.shape
    columns = proj_weight.shape[1]
    stream = block_rows * n_tp
    own = stream // n_seq
    part_rows = block_rows // n_sec
    sub = part_rows // n_seq
    keys = key_weight.shape[1]
    seq_len = text_embed.shape[0]
    tiles = stream // TILE

    mine = lax.dynamic_slice_in_dim(vis_hidden, core * part_rows, part_rows, 0)
    act = jax.nn.gelu(mine.astype(f32), approximate=False).astype(bf16)
    pieces = [act] + [swap(act, "tp", m) for m in range(1, n_tp)]
    pieces = [p.reshape(n_seq, sub, features) for p in pieces]

    starts = jnp.cumsum(tile_counts) - tile_counts
    tile_ids = jnp.arange(tiles, dtype=jnp.int32)[:, None]
    held = (tile_ids >= starts[None]) & (tile_ids < (starts + tile_counts)[None])
    tile_owner = jnp.sum(jnp.where(held, owner_map[None], 0), 1)
    tile_place = jnp.sum(jnp.where(held, tile_ids - starts[None], 0), 1)
    share = keys // n_tp
    front = lax.dynamic_slice_in_dim(key_cotangent[: MAXT * TILE], t * share, share, 1)
    front = front.reshape(MAXT, TILE, share)
    given = jnp.zeros((tiles, TILE, share), bf16)
    for place in range(MAXT):
        chosen = (tile_owner == z) & (tile_place == place)
        given = jnp.where(chosen[:, None, None], front[place][None], given)
    given = given.reshape(n_tp, n_sec, n_seq, sub, share).transpose(2, 1, 0, 3, 4)
    taken = lax.psum_scatter(
        given.reshape(stream, share), "seq", scatter_dimension=0, tiled=True
    )
    taken = [taken] + [swap(taken, "tp", m) for m in range(1, n_tp)]
    image_cot = jnp.concatenate(in_order(taken, t), 1)
    scaled = lax.dot_general(
        image_cot, key_weight, (((1,), (1,)), ((), ())), preferred_element_type=f32
    ) * norm_gain

    images = []
    for first in range(0, n_tp, 2):
        chunk = jnp.stack(pieces[first : first + 2], 1).reshape(2 * part_rows, features)
        partial = jnp.dot(chunk, proj_weight, preferred_element_type=f32).astype(bf16)
        summed = reduce_to_owner(partial.reshape(n_seq, 2 * sub, columns), "seq")
        images += list((summed + proj_bias).astype(bf16).reshape(2, sub, columns))
    image_mine = jnp.concatenate(in_order(images, t), 0)
    image = jnp.concatenate(in_order([image_mine, swap(image_mine, "sec", 1)], core), 0)

    act_half = jnp.stack(in_order(pieces, t), 1)
    act_pair = in_order([act_half, swap(act_half, "sec", 1)], core)
    act_full = jnp.stack(act_pair, 1).reshape(n_seq, own, features)

    is_mine = owner_map == z
    image_count = TILE * jnp.sum(jnp.where(is_mine, tile_counts, 0))
    text_count = jnp.sum(jnp.where(is_mine, text_counts, 0))
    text_values = text_embed.astype(f32)
    text_sq = total(jnp.sum(text_values * text_values, 1), "tp")
    text_inv = lax.rsqrt(text_sq / D + EPSILON)
    text_scale = jnp.where(jnp.arange(seq_len) < text_count, text_inv, 0.0)
    key_half = keys // n_sec
    cot_half = lax.dynamic_slice_in_dim(key_cotangent, core * key_half, key_half, 1)
    cot_padded = jnp.concatenate([cot_half, jnp.zeros((MAXT * TILE, key_half), bf16)], 0)
    cot_text = lax.dynamic_slice_in_dim(cot_padded, image_count, seq_len, 0)
    cot_text = (cot_text.astype(f32) * text_scale[:, None]).astype(bf16)
    rows_first = (((0,), (0,)), ((), ()))
    text_moment = lax.dot_general(text_embed, cot_text, rows_first, preferred_element_type=f32)

    values = image.astype(f32)
    sums = total(jnp.stack([jnp.sum(values * values, 1), jnp.sum(scaled * values, 1)]), "tp")
    inv = lax.rsqrt(sums[0] / D + EPSILON)
    mean = inv * sums[1] / D
    embed_grad = (inv[:, None] * (scaled - values * (inv * mean)[:, None])).astype(bf16)
    col_half = columns // n_sec
    grad_half = lax.dynamic_slice_in_dim(embed_grad, core * col_half, col_half, 1)

    cot_image = lax.dynamic_slice_in_dim(image_cot, core * key_half, key_half, 1)
    cot_image = (cot_image.astype(f32) * inv[:, None]).astype(bf16)
    moment = text_moment + lax.dot_general(
        image, cot_image, rows_first, preferred_element_type=f32
    )
    weight_half = lax.dynamic_slice_in_dim(key_weight, core * key_half, key_half, 1)
    gain_part = jnp.sum(moment * weight_half.astype(f32), 1)
    shares = (moment * norm_gain[:, None]).astype(bf16)
    shares = shares.reshape(columns, n_seq, key_half // n_seq).transpose(1, 0, 2)
    key_weight_grad = lax.psum_scatter(shares, "seq", scatter_dimension=0, tiled=False)
    key_weight_grad = key_weight_grad.astype(f32)

    key_bias_part = jnp.sum(key_cotangent.astype(f32), 0)
    bias_part = jnp.sum(embed_grad.astype(f32), 0)
    once = jnp.concatenate([key_bias_part, bias_part])
    small = total(jnp.concatenate([gain_part, jnp.where(core == 0, once, 0.0)]), "sec")

    if n_seq <= 4:
        up, down = along_line(grad_half, "seq")
        small, up[-1], down[-1] = lax.optimization_barrier((small, up[-1], down[-1]))
        small = total(small, "seq")
        around = jnp.concatenate([act_full[::-1], act_full[::-1]], 0)
        act_used = lax.dynamic_slice_in_dim(around, n_seq - 1 - z, n_seq, 0)
        product = weight_product(act_used.reshape(stream, features), grad_half, up + down)
    else:
        small = butterfly(small, ("seq",))
        grads = lax.all_gather(grad_half, "seq", axis=0, tiled=True)
        product = weight_product(act_full.reshape(stream, features), grads, [])
    gain_grad = small[:columns]
    key_bias_grad = small[columns : columns + keys]
    proj_bias_grad = small[columns + keys :]
    proj_weight_grad = product.reshape(features, 1, 1, col_half)
    return (proj_weight_grad, proj_bias_grad, key_weight_grad, key_bias_grad, gain_grad)


def solution(mesh):
    placed = (
        P("tp", "seq"),
        P("seq", "tp"),
        P("tp"),
        P("seq", "tp"),
        P("tp"),
        P("tp", None),
        P("seq", None),
        P(),
        P(),
        P(),
    )
    return jax.shard_map(
        on_device,
        mesh=mesh,
        in_specs=placed,
        out_specs=(P("seq", "tp", "sec", None), P("tp"), P("tp", ("sec", "seq")), P(), P("tp")),
        check_vma=False,
    )
```

```python
import jax
import jax.numpy as jnp
from jax import lax
from jax.experimental import pallas as pl
from jax.experimental.pallas import tpu as pltpu
from jax.sharding import PartitionSpec as P

D = 8192
TILE = 256
MAXT = 2
LANES = 128
EPSILON = 1e-06
VMEM = 32 * 1024 * 1024


def swap(x, axis, mask):
    count = lax.axis_size(axis)
    return lax.ppermute(x, axis, [(i, i ^ mask) for i in range(count)])


def total(x, axis):
    pieces = [x] + [swap(x, axis, m) for m in range(1, lax.axis_size(axis))]
    while len(pieces) > 1:
        pieces = [pieces[i] + pieces[i + 1] for i in range(0, len(pieces), 2)]
    return pieces[0]


def butterfly(x, axes, first=1):
    for axis in axes:
        mask = first
        while mask < lax.axis_size(axis):
            x = x + swap(x, axis, mask)
            mask *= 2
    return x


def in_order(pieces, index):
    pieces = list(pieces)
    mask = 1
    while mask < len(pieces):
        odd = (index & mask) != 0
        pieces = [jnp.where(odd, pieces[m ^ mask], pieces[m]) for m in range(len(pieces))]
        mask *= 2
    return pieces


def together(*values):
    return lax.optimization_barrier(values)


def reduce_to_owner(parts, axis):
    index = lax.axis_index(axis)
    count = parts.shape[0]
    while count > 1:
        pairs = parts.reshape(count // 2, 2, *parts.shape[1:])
        mask = lax.axis_size(axis) // count
        bit = (index // mask) % 2
        sent = lax.dynamic_index_in_dim(pairs, 1 - bit, 1, keepdims=False)
        kept = lax.dynamic_index_in_dim(pairs, bit, 1, keepdims=False)
        came = swap(sent.astype(jnp.bfloat16), axis, mask)
        parts = kept.astype(jnp.float32) + came.astype(jnp.float32)
        count //= 2
    return parts[0]


def line_step(parts, axis, step, before):
    count = lax.axis_size(axis)
    index = lax.axis_index(axis)
    out = []
    for sign in (1, -1):
        place = index + sign * (count - step)
        place = jnp.clip(place, 0, count - 1)
        sent = lax.dynamic_index_in_dim(parts, place, 0, keepdims=False)
        if before is not None:
            sent = (sent.astype(jnp.float32) + before[len(out)].astype(jnp.float32)).astype(sent.dtype)
        first = 0 if sign > 0 else count - 1
        pairs = [(first + sign * j, first + sign * (j + 1)) for j in range(step)]
        out.append(lax.ppermute(sent, axis, pairs))
    return out


def columns_of(row, count):
    parts = []
    for i in range(count // LANES):
        part = row[:, i * LANES : (i + 1) * LANES]
        parts.append(jnp.broadcast_to(part, (LANES, LANES)).T)
    return jnp.concatenate(parts, 0)


def row_of(folded):
    count = folded.shape[0]
    parts = [
        jnp.sum(folded[i * LANES : (i + 1) * LANES, :].T, 0, keepdims=True)
        for i in range(count // LANES)
    ]
    return jnp.concatenate(parts, 1)


def fold(values):
    width = values.shape[1]
    out = values[:, :LANES]
    for i in range(1, width // LANES):
        out = out + values[:, i * LANES : (i + 1) * LANES]
    return out


def project_kernel(*refs):
    index_ref, weight_ref = refs[:2]
    partial_ref, act_ref = refs[-2:]
    pieces = refs[2:-2]
    rows = pieces[0].shape[0]

    @pl.when(pl.program_id(0) == 0)
    def _():
        for m, piece in enumerate(pieces):
            at = jnp.bitwise_xor(index_ref[0], m) * rows
            act_ref[pl.ds(pl.multiple_of(at, rows), rows), :] = piece[...]

    product = jnp.dot(act_ref[...], weight_ref[...], preferred_element_type=jnp.float32)
    partial_ref[...] = product.astype(jnp.bfloat16)


def project(index, pieces, weight):
    rows, features = pieces[0].shape
    columns = weight.shape[1]
    total_rows = rows * len(pieces)
    step = 512
    return pl.pallas_call(
        project_kernel,
        grid=(columns // step,),
        in_specs=[
            pl.BlockSpec(memory_space=pltpu.SMEM),
            pl.BlockSpec((features, step), lambda i: (0, i)),
        ]
        + [pl.BlockSpec((rows, features), lambda i: (0, 0))] * len(pieces),
        out_specs=[
            pl.BlockSpec((total_rows, step), lambda i: (0, i)),
            pl.BlockSpec((total_rows, features), lambda i: (0, 0)),
        ],
        out_shape=[
            jax.ShapeDtypeStruct((total_rows, columns), jnp.bfloat16),
            jax.ShapeDtypeStruct((total_rows, features), jnp.bfloat16),
        ],
        compiler_params=pltpu.CompilerParams(vmem_limit_bytes=VMEM),
        cost_estimate=pl.CostEstimate(
            flops=2 * total_rows * features * columns,
            bytes_accessed=2 * (features * columns + total_rows * (columns + 2 * features)),
            transcendentals=0,
        ),
    )(index, weight, *pieces)


def opening_kernel(
    core_ref, z_ref, t_ref, tiles_ref, owners_ref, text_ref, cot_ref, *refs
):
    del core_ref, t_ref
    sums_ref, act_ref, given_ref = refs[-3:]
    groups = refs[:-3]

    @pl.when(pl.program_id(0) == 0)
    def _():
        rows = groups[0].shape[0]
        for i, group in enumerate(groups):
            hidden = group[...].astype(jnp.float32)
            act = 0.5 * hidden * (1.0 + lax.erf(hidden * 0.7071067811865476))
            act_ref[i * rows : (i + 1) * rows, :] = act.astype(jnp.bfloat16)
        for tile in range(given_ref.shape[0] // TILE):
            start = owner = place = jnp.int32(0)
            for s in range(tiles_ref.shape[0]):
                inside = (tile >= start) & (tile < start + tiles_ref[s])
                owner = jnp.where(inside, owners_ref[s], owner)
                place = jnp.where(inside, tile - start, place)
                start = start + tiles_ref[s]
            at = pl.multiple_of(jnp.clip(place, 0, MAXT - 1) * TILE, TILE)
            here = jnp.where(owner == z_ref[0], 1.0, 0.0)
            rows_of_tile = cot_ref[pl.ds(at, TILE), :].astype(jnp.float32) * here
            given_ref[tile * TILE : (tile + 1) * TILE, :] = rows_of_tile.astype(jnp.bfloat16)

    values = text_ref[...].astype(jnp.float32)
    sums_ref[...] = row_of(fold(values * values))


def opening(core, z, t, tile_counts, owner_map, text, hidden, cot, groups, n_sec, n_tp, stream):
    seq_len, columns = text.shape
    rows, features = hidden.shape
    half = rows // (groups * n_sec)
    share = cot.shape[1] // (n_sec * n_tp)
    step = 256
    part = [
        pl.BlockSpec((half, features), lambda i, c, *_, q=q: (q * n_sec + c[0], 0))
        for q in range(groups)
    ]
    return pl.pallas_call(
        opening_kernel,
        grid_spec=pltpu.PrefetchScalarGridSpec(
            num_scalar_prefetch=5,
            grid=(seq_len // step,),
            in_specs=[
                pl.BlockSpec((step, columns), lambda i, *_: (i, 0)),
                pl.BlockSpec((MAXT * TILE, share), lambda i, c, z, t, *_: (0, c[0] * n_tp + t[0])),
            ]
            + part,
            out_specs=[
                pl.BlockSpec((1, step), lambda i, *_: (0, i)),
                pl.BlockSpec((groups * half, features), lambda i, *_: (0, 0)),
                pl.BlockSpec((stream, share), lambda i, *_: (0, 0)),
            ],
        ),
        out_shape=[
            jax.ShapeDtypeStruct((1, seq_len), jnp.float32),
            jax.ShapeDtypeStruct((groups * half, features), jnp.bfloat16),
            jax.ShapeDtypeStruct((stream, share), jnp.bfloat16),
        ],
        compiler_params=pltpu.CompilerParams(vmem_limit_bytes=60 * 1024 * 1024),
        cost_estimate=pl.CostEstimate(
            flops=2 * seq_len * columns + 40 * groups * half * features,
            bytes_accessed=2 * seq_len * columns,
            transcendentals=0,
        ),
    )(core, z, t, tile_counts, owner_map, text, cot, *[hidden] * groups)


def text_kernel(
    core_ref, z_ref, tiles_ref, texts_ref, owners_ref, text_ref, weight_ref, cot_ref, *refs
):
    del core_ref
    moment_ref, gain_ref, long_ref, scaled_ref = refs[-4:]
    squares = refs[:-4]
    seq_len, width = cot_ref.shape

    @pl.when(pl.program_id(0) == 0)
    def _():
        parts = [r[...] for r in squares]
        while len(parts) > 1:
            parts = [parts[i] + parts[i + 1] for i in range(0, len(parts), 2)]
        image_tiles = text_count = jnp.int32(0)
        for s in range(owners_ref.shape[0]):
            mine = owners_ref[s] == z_ref[0]
            image_tiles = jnp.where(mine, tiles_ref[s], image_tiles)
            text_count = jnp.where(mine, texts_ref[s], text_count)
        begin = pl.multiple_of(jnp.clip(image_tiles, 0, MAXT) * TILE, TILE)
        places = lax.broadcasted_iota(jnp.int32, (1, seq_len), 1)
        scale = lax.rsqrt(parts[0] / D + EPSILON)
        scale = columns_of(jnp.where(places < text_count, scale, 0.0), seq_len)
        long_ref[:seq_len, :] = cot_ref[...]
        long_ref[seq_len:, :] = jnp.zeros((MAXT * TILE, width), jnp.bfloat16)
        for i in range(width // LANES):
            lanes = slice(i * LANES, (i + 1) * LANES)
            shifted = long_ref[pl.ds(begin, seq_len), lanes]
            scaled_ref[:, lanes] = (shifted.astype(jnp.float32) * scale).astype(jnp.bfloat16)

    moment = lax.dot_general(
        text_ref[...], scaled_ref[...], (((0,), (0,)), ((), ())), preferred_element_type=jnp.float32
    )
    for i in range(moment_ref.shape[0]):
        moment_ref[i] = moment[:, i * LANES : (i + 1) * LANES].astype(jnp.bfloat16)
    gain_ref[...] = row_of(fold(moment * weight_ref[...].astype(jnp.float32)))


def text_product(scalars, text, weight, cot, squares, width):
    seq_len, columns = text.shape
    groups = width // LANES
    step = 256
    return pl.pallas_call(
        text_kernel,
        grid_spec=pltpu.PrefetchScalarGridSpec(
            num_scalar_prefetch=len(scalars),
            grid=(columns // step,),
            in_specs=[
                pl.BlockSpec((seq_len, step), lambda i, *_: (0, i)),
                pl.BlockSpec((step, width), lambda i, c, *_: (i, c[0])),
                pl.BlockSpec((seq_len, width), lambda i, c, *_: (0, c[0])),
            ]
            + [pl.BlockSpec((1, seq_len), lambda i, *_: (0, 0))] * len(squares),
            out_specs=[
                pl.BlockSpec((groups, step, LANES), lambda i, *_: (0, i, 0)),
                pl.BlockSpec((1, step), lambda i, *_: (0, i)),
            ],
            scratch_shapes=[
                pltpu.VMEM((seq_len + MAXT * TILE, width), jnp.bfloat16),
                pltpu.VMEM((seq_len, width), jnp.bfloat16),
            ],
        ),
        out_shape=[
            jax.ShapeDtypeStruct((groups, columns, LANES), jnp.bfloat16),
            jax.ShapeDtypeStruct((1, columns), jnp.float32),
        ],
        compiler_params=pltpu.CompilerParams(vmem_limit_bytes=VMEM),
        cost_estimate=pl.CostEstimate(
            flops=2 * seq_len * columns * width,
            bytes_accessed=2 * (seq_len * (columns + width) + 2 * columns * width),
            transcendentals=0,
        ),
    )(*scalars, text, weight, cot, *squares)


def sums_kernel(rows_ref, grad_ref, gain_ref, sums_ref):
    values = rows_ref[...].astype(jnp.float32)
    more = sums_ref.shape[1] - values.shape[0]
    for i, terms in enumerate((values * values, values * grad_ref[...] * gain_ref[...])):
        folded = jnp.concatenate([fold(terms), jnp.zeros((more, LANES), jnp.float32)], 0)
        sums_ref[i : i + 1, :] = row_of(folded)


def row_sums(rows, grad, gain):
    count, width = rows.shape
    padded = -(-count // LANES) * LANES
    whole = pl.BlockSpec(memory_space=pltpu.VMEM)
    return pl.pallas_call(
        sums_kernel,
        in_specs=[whole] * 3,
        out_specs=whole,
        out_shape=jax.ShapeDtypeStruct((2, padded), jnp.float32),
        compiler_params=pltpu.CompilerParams(vmem_limit_bytes=16 * 1024 * 1024),
        cost_estimate=pl.CostEstimate(
            flops=8 * count * width, bytes_accessed=6 * count * width, transcendentals=0
        ),
    )(rows, grad, gain)


def image_kernel(core_ref, grad_ref, gain_ref, cot_ref, sums_ref, rows_ref, *out):
    embed_ref, here_ref, there_ref, small_ref = out
    stream, width = rows_ref.shape
    groups = sums_ref.shape[0]
    size = stream // groups
    inv, mean = [], []
    for i in range(groups):
        inv_row = lax.rsqrt(sums_ref[i, 0:1, :] / D + EPSILON)
        mean_row = inv_row * inv_row * inv_row * sums_ref[i, 1:2, :] / D
        inv.append(columns_of(inv_row, inv_row.shape[1])[:size])
        mean.append(columns_of(mean_row, mean_row.shape[1])[:size])
    all_inv = jnp.concatenate(inv, 0)
    gain_parts = [jnp.zeros((1, LANES), jnp.float32)] * (width // LANES)
    bias_parts = list(gain_parts)
    for g in range(groups):
        rows = slice(g * size, (g + 1) * size)
        to = jnp.bitwise_xor(core_ref[0], g % 2) * (stream // 2) + (g // 2) * size
        to_rows = pl.ds(pl.multiple_of(to, 16), size)
        for i in range(width // LANES):
            at = slice(i * LANES, (i + 1) * LANES)
            values = rows_ref[rows, at].astype(jnp.float32)
            scaled = grad_ref[rows, at] * inv[g]
            embed = (scaled * gain_ref[:, at] - values * mean[g]).astype(jnp.bfloat16)
            embed_ref[to_rows, at] = embed
            gain_parts[i] = gain_parts[i] + jnp.sum(scaled * values, 0, keepdims=True)
            bias_parts[i] = bias_parts[i] + jnp.sum(embed.astype(jnp.float32), 0, keepdims=True)
    small_ref[0:1, :] = jnp.concatenate(gain_parts, 1)
    small_ref[1:2, :] = jnp.concatenate(bias_parts, 1)
    lanes = cot_ref.shape[1]
    wide = [all_inv] * (lanes // LANES) if lanes >= LANES else [all_inv[:, :lanes]]
    cot = (cot_ref[...].astype(jnp.float32) * jnp.concatenate(wide, 1)).astype(jnp.bfloat16)
    moment = lax.dot_general(
        rows_ref[...], cot, (((0,), (0,)), ((), ())), preferred_element_type=jnp.float32
    )
    share = here_ref.shape[1]
    here_ref[...] = moment[:, :share]
    there_ref[...] = moment[:, share:].astype(jnp.bfloat16)


def image_grads(core, grad, gain, cot, sums, rows):
    stream, width = grad.shape
    share = cot.shape[1] // 2
    whole = pl.BlockSpec(memory_space=pltpu.VMEM)
    return pl.pallas_call(
        image_kernel,
        in_specs=[pl.BlockSpec(memory_space=pltpu.SMEM)] + [whole] * 5,
        out_specs=[whole] * 4,
        out_shape=[
            jax.ShapeDtypeStruct((stream, width), jnp.bfloat16),
            jax.ShapeDtypeStruct((width, share), jnp.float32),
            jax.ShapeDtypeStruct((width, share), jnp.bfloat16),
            jax.ShapeDtypeStruct((2, width), jnp.float32),
        ],
        compiler_params=pltpu.CompilerParams(vmem_limit_bytes=56 * 1024 * 1024),
        cost_estimate=pl.CostEstimate(
            flops=4 * stream * width * share, bytes_accessed=8 * stream * width, transcendentals=0
        ),
    )(core, grad, gain, cot, sums, rows)


def weight_kernel(act_ref, grad_ref, out_ref):
    step = act_ref.shape[0]
    groups = grad_ref.shape[1] // LANES
    product = jnp.dot(act_ref[...], grad_ref[...], preferred_element_type=jnp.float32)
    for c in range(groups):
        out_ref[pl.ds(c, step, stride=groups), :] = product[:, c * LANES : (c + 1) * LANES]


def weight_product(act, grad):
    features, rows = act.shape
    width = grad.shape[1]
    groups = width // LANES
    step = 256
    return pl.pallas_call(
        weight_kernel,
        grid=(features // step,),
        in_specs=[
            pl.BlockSpec((step, rows), lambda i: (i, 0)),
            pl.BlockSpec((rows, width), lambda i: (0, 0)),
        ],
        out_specs=pl.BlockSpec((step * groups, LANES), lambda i: (i, 0)),
        out_shape=jax.ShapeDtypeStruct((features * groups, LANES), jnp.float32),
        compiler_params=pltpu.CompilerParams(vmem_limit_bytes=VMEM),
        cost_estimate=pl.CostEstimate(
            flops=2 * rows * features * width,
            bytes_accessed=4 * features * width + 2 * rows * (features + width),
            transcendentals=0,
        ),
    )(act, grad)


def on_device(
    vis_hidden,
    proj_weight,
    proj_bias,
    text_embed,
    norm_gain,
    key_weight,
    key_cotangent,
    tile_counts,
    text_counts,
    owner_map,
):
    f32, bf16 = jnp.float32, jnp.bfloat16
    n_sec, n_seq, n_tp = (lax.axis_size(a) for a in ("sec", "seq", "tp"))
    core, z, t = (lax.axis_index(a) for a in ("sec", "seq", "tp"))
    block_rows, features = vis_hidden.shape
    columns = proj_weight.shape[1]
    col_half = columns // n_sec
    stream = block_rows * n_tp
    own = stream // n_seq
    half = own // n_sec
    groups = block_rows // own
    keys = key_weight.shape[1]
    key_half = keys // n_sec
    seq_len = text_embed.shape[0]

    text_sq, act, given = opening(
        core[None], z[None], t[None], tile_counts, owner_map,
        text_embed, vis_hidden, key_cotangent, groups, n_sec, n_tp, stream,
    )
    pieces = [act] + [swap(act, "tp", m) for m in range(1, n_tp)]
    text_sq = [text_sq] + [swap(text_sq, "tp", m) for m in range(1, n_tp)]
    given = given + swap(given, "seq", 1)
    text_sq[0], pieces[1], given = together(text_sq[0], pieces[1], given)

    scalars = (core[None], z[None], tile_counts, text_counts, owner_map)
    moment, gain_text = text_product(
        scalars, text_embed, key_weight, key_cotangent, text_sq, key_half
    )
    taken = butterfly(given, ("seq",), 2)
    if n_seq <= 4:
        way = line_step(moment, "seq", 1, None)
    else:
        share = key_half // n_seq
        moment = moment.reshape(-1, columns, LANES // share, share).transpose(0, 2, 1, 3)
        moment = reduce_to_owner(moment.reshape(n_seq, columns, share), "seq")

    partial, act_mine = project(t[None], pieces, proj_weight)
    if n_seq <= 4:
        way[0], way[1], partial = together(*way, partial)
        way = line_step(moment, "seq", 2, way)
    taken, partial = together(taken, partial)
    summed = lax.psum_scatter(partial, "seq", scatter_dimension=0, tiled=True)

    key_bias_part = jnp.sum(key_cotangent.astype(f32), 0)
    early = jnp.concatenate([gain_text[0], jnp.where(core == 0, key_bias_part, 0.0)])

    act_other = swap(act_mine, "sec", 1)
    taken = [taken] + [swap(taken, "tp", m) for m in range(1, n_tp)]
    half_cot = jnp.concatenate(in_order(taken, t), 1)
    other_cot = swap(half_cot, "sec", 1)
    image_cot = jnp.concatenate(in_order([half_cot, other_cot], core), 1)
    weight_rows = lax.dynamic_slice_in_dim(key_weight, core * col_half, col_half, 0)
    normed_grad = lax.dot_general(
        image_cot, weight_rows, (((1,), (1,)), ((), ())), preferred_element_type=f32
    )
    own_cot = lax.dynamic_slice_in_dim(image_cot, (z * n_sec + core) * half, half, 0)
    own_grad = lax.dot_general(
        own_cot, key_weight, (((1,), (1,)), ((), ())), preferred_element_type=f32
    )
    key_share = key_half // n_seq
    cot_own = jnp.concatenate(
        [lax.dynamic_slice_in_dim(c, z * key_share, key_share, 1) for c in (half_cot, other_cot)], 1
    )

    summed, normed_grad, own_grad = together(summed, normed_grad, own_grad)
    image_mine = (summed.astype(f32) + proj_bias).astype(bf16)
    if n_seq <= 4:
        way[0], way[1], image_mine = together(*way, image_mine)
    low, high = image_mine[:, :col_half], image_mine[:, col_half:]
    first_core = core == 0
    came = swap(jnp.where(first_core, high, low), "sec", 1)
    image = jnp.concatenate(in_order([jnp.where(first_core, low, high), came], core), 0)
    rows = lax.all_gather(image, "seq", axis=0, tiled=True)

    image_mine, came = together(image_mine, came)
    sums = total(row_sums(image_mine, own_grad, norm_gain[None]), "tp")
    size = sums.size
    sums = jnp.concatenate([sums.reshape(-1), early])
    if n_seq <= 4:
        sums = jnp.stack(in_order([sums] + [swap(sums, "seq", m) for m in range(1, n_seq)], z), 0)
    else:
        sums = lax.all_gather(sums, "seq", axis=0, tiled=False)
    early = jnp.sum(sums[:, size:], 0)
    sums = jnp.concatenate([sums[:, :size].reshape(-1), early])
    sums = jnp.stack(in_order([sums, swap(sums, "sec", 1)], core), 0)
    early = jnp.sum(sums[:, n_seq * size :], 0)
    sums = sums[:, : n_seq * size].reshape(n_sec, n_seq, 2, -1).transpose(1, 0, 2, 3)
    sums = sums.reshape(n_seq * n_sec, 2, -1)

    if n_seq <= 4:
        for step in range(3, n_seq):
            way = line_step(moment, "seq", step, way)
        moment = lax.dynamic_index_in_dim(moment, z, 0, keepdims=False).astype(f32)
        moment = moment + way[0].astype(f32) + way[1].astype(f32)
    gain_half = lax.dynamic_slice_in_dim(norm_gain, core * col_half, col_half, 0)[None]
    embed_grad, here, there, small = image_grads(
        core[None], normed_grad, gain_half, cot_own, sums, rows
    )
    there = swap(there, "sec", 1)
    small_other = swap(small, "sec", 1)
    act_turned = jnp.concatenate([act_mine, act_other], 0).T
    weight_grad = weight_product(act_turned, embed_grad)
    proj_weight_grad = weight_grad.reshape(features, 1, 1, col_half)

    both = in_order([here, there.astype(f32)], core)
    key_weight_grad = (moment + jnp.concatenate(both, 0)) * norm_gain[:, None]
    gain_image, proj_bias_grad = jnp.concatenate(in_order([small, small_other], core), 1)
    gain_grad = early[:columns] + gain_image
    key_bias_grad = early[columns:]
    return (proj_weight_grad, proj_bias_grad, key_weight_grad, key_bias_grad, gain_grad)


def solution(mesh):
    placed = (
        P("tp", "seq"),
        P("seq", "tp"),
        P("tp"),
        P("seq", "tp"),
        P("tp"),
        P("tp", None),
        P("seq", None),
        P(),
        P(),
        P(),
    )
    return jax.shard_map(
        on_device,
        mesh=mesh,
        in_specs=placed,
        out_specs=(P("seq", "tp", "sec", None), P("tp"), P("tp", ("sec", "seq")), P(), P("tp")),
        check_vma=False,
    )
```

```python
import jax
import jax.numpy as jnp
from jax import lax
from jax.experimental import pallas as pl
from jax.experimental.pallas import tpu as pltpu
from jax.sharding import PartitionSpec as P

D = 8192
TILE = 256
MAXT = 2
LANES = 128
EPSILON = 1e-06
VMEM = 32 * 1024 * 1024


def swap(x, axis, mask):
    count = lax.axis_size(axis)
    return lax.ppermute(x, axis, [(i, i ^ mask) for i in range(count)])


def total(x, axis):
    pieces = [x] + [swap(x, axis, m) for m in range(1, lax.axis_size(axis))]
    while len(pieces) > 1:
        pieces = [pieces[i] + pieces[i + 1] for i in range(0, len(pieces), 2)]
    return pieces[0]


def butterfly(x, axes, first=1):
    for axis in axes:
        mask = first
        while mask < lax.axis_size(axis):
            x = x + swap(x, axis, mask)
            mask *= 2
    return x


def in_order(pieces, index):
    pieces = list(pieces)
    mask = 1
    while mask < len(pieces):
        odd = (index & mask) != 0
        pieces = [jnp.where(odd, pieces[m ^ mask], pieces[m]) for m in range(len(pieces))]
        mask *= 2
    return pieces


def together(*values):
    return lax.optimization_barrier(values)


def reduce_to_owner(parts, axis):
    index = lax.axis_index(axis)
    count = parts.shape[0]
    while count > 1:
        pairs = parts.reshape(count // 2, 2, *parts.shape[1:])
        mask = lax.axis_size(axis) // count
        bit = (index // mask) % 2
        sent = lax.dynamic_index_in_dim(pairs, 1 - bit, 1, keepdims=False)
        kept = lax.dynamic_index_in_dim(pairs, bit, 1, keepdims=False)
        came = swap(sent.astype(jnp.bfloat16), axis, mask)
        parts = kept.astype(jnp.float32) + came.astype(jnp.float32)
        count //= 2
    return parts[0]


def line_step(parts, axis, step, before):
    count = lax.axis_size(axis)
    index = lax.axis_index(axis)
    out = []
    for sign in (1, -1):
        place = index + sign * (count - step)
        place = jnp.clip(place, 0, count - 1)
        sent = lax.dynamic_index_in_dim(parts, place, 0, keepdims=False)
        if before is not None:
            sent = (sent.astype(jnp.float32) + before[len(out)].astype(jnp.float32)).astype(sent.dtype)
        first = 0 if sign > 0 else count - 1
        pairs = [(first + sign * j, first + sign * (j + 1)) for j in range(step)]
        out.append(lax.ppermute(sent, axis, pairs))
    return out


def columns_of(row, count):
    parts = []
    for i in range(count // LANES):
        part = row[:, i * LANES : (i + 1) * LANES]
        parts.append(jnp.broadcast_to(part, (LANES, LANES)).T)
    return jnp.concatenate(parts, 0)


def row_of(folded):
    count = folded.shape[0]
    parts = [
        jnp.sum(folded[i * LANES : (i + 1) * LANES, :].T, 0, keepdims=True)
        for i in range(count // LANES)
    ]
    return jnp.concatenate(parts, 1)


def fold(values):
    width = values.shape[1]
    out = values[:, :LANES]
    for i in range(1, width // LANES):
        out = out + values[:, i * LANES : (i + 1) * LANES]
    return out


def project_kernel(*refs):
    index_ref, weight_ref = refs[:2]
    partial_ref, act_ref = refs[-2:]
    pieces = refs[2:-2]
    rows = pieces[0].shape[0]

    @pl.when(pl.program_id(0) == 0)
    def _():
        for m, piece in enumerate(pieces):
            at = jnp.bitwise_xor(index_ref[0], m) * rows
            act_ref[pl.ds(pl.multiple_of(at, rows), rows), :] = piece[...]

    product = jnp.dot(act_ref[...], weight_ref[...], preferred_element_type=jnp.float32)
    partial_ref[...] = product.astype(jnp.bfloat16)


def project(index, pieces, weight):
    rows, features = pieces[0].shape
    columns = weight.shape[1]
    total_rows = rows * len(pieces)
    step = 512
    return pl.pallas_call(
        project_kernel,
        grid=(columns // step,),
        in_specs=[
            pl.BlockSpec(memory_space=pltpu.SMEM),
            pl.BlockSpec((features, step), lambda i: (0, i)),
        ]
        + [pl.BlockSpec((rows, features), lambda i: (0, 0))] * len(pieces),
        out_specs=[
            pl.BlockSpec((total_rows, step), lambda i: (0, i)),
            pl.BlockSpec((total_rows, features), lambda i: (0, 0)),
        ],
        out_shape=[
            jax.ShapeDtypeStruct((total_rows, columns), jnp.bfloat16),
            jax.ShapeDtypeStruct((total_rows, features), jnp.bfloat16),
        ],
        compiler_params=pltpu.CompilerParams(vmem_limit_bytes=VMEM),
        cost_estimate=pl.CostEstimate(
            flops=2 * total_rows * features * columns,
            bytes_accessed=2 * (features * columns + total_rows * (columns + 2 * features)),
            transcendentals=0,
        ),
    )(index, weight, *pieces)


def opening_kernel(
    core_ref, z_ref, t_ref, tiles_ref, owners_ref, text_ref, cot_ref, *refs
):
    del core_ref, t_ref
    sums_ref, act_ref, given_ref = refs[-3:]
    groups = refs[:-3]

    @pl.when(pl.program_id(0) == 0)
    def _():
        rows = groups[0].shape[0]
        for i, group in enumerate(groups):
            hidden = group[...].astype(jnp.float32)
            act = 0.5 * hidden * (1.0 + lax.erf(hidden * 0.7071067811865476))
            act_ref[i * rows : (i + 1) * rows, :] = act.astype(jnp.bfloat16)
        for tile in range(given_ref.shape[0] // TILE):
            start = owner = place = jnp.int32(0)
            for s in range(tiles_ref.shape[0]):
                inside = (tile >= start) & (tile < start + tiles_ref[s])
                owner = jnp.where(inside, owners_ref[s], owner)
                place = jnp.where(inside, tile - start, place)
                start = start + tiles_ref[s]
            at = pl.multiple_of(jnp.clip(place, 0, MAXT - 1) * TILE, TILE)
            here = jnp.where(owner == z_ref[0], 1.0, 0.0)
            rows_of_tile = cot_ref[pl.ds(at, TILE), :].astype(jnp.float32) * here
            given_ref[tile * TILE : (tile + 1) * TILE, :] = rows_of_tile.astype(jnp.bfloat16)

    values = text_ref[...].astype(jnp.float32)
    sums_ref[...] = row_of(fold(values * values))


def opening(core, z, t, tile_counts, owner_map, text, hidden, cot, groups, n_sec, n_tp, stream):
    seq_len, columns = text.shape
    rows, features = hidden.shape
    half = rows // (groups * n_sec)
    share = cot.shape[1] // (n_sec * n_tp)
    step = 256
    part = [
        pl.BlockSpec((half, features), lambda i, c, *_, q=q: (q * n_sec + c[0], 0))
        for q in range(groups)
    ]
    return pl.pallas_call(
        opening_kernel,
        grid_spec=pltpu.PrefetchScalarGridSpec(
            num_scalar_prefetch=5,
            grid=(seq_len // step,),
            in_specs=[
                pl.BlockSpec((step, columns), lambda i, *_: (i, 0)),
                pl.BlockSpec((MAXT * TILE, share), lambda i, c, z, t, *_: (0, c[0] * n_tp + t[0])),
            ]
            + part,
            out_specs=[
                pl.BlockSpec((1, step), lambda i, *_: (0, i)),
                pl.BlockSpec((groups * half, features), lambda i, *_: (0, 0)),
                pl.BlockSpec((stream, share), lambda i, *_: (0, 0)),
            ],
        ),
        out_shape=[
            jax.ShapeDtypeStruct((1, seq_len), jnp.float32),
            jax.ShapeDtypeStruct((groups * half, features), jnp.bfloat16),
            jax.ShapeDtypeStruct((stream, share), jnp.bfloat16),
        ],
        compiler_params=pltpu.CompilerParams(vmem_limit_bytes=60 * 1024 * 1024),
        cost_estimate=pl.CostEstimate(
            flops=2 * seq_len * columns + 40 * groups * half * features,
            bytes_accessed=2 * seq_len * columns,
            transcendentals=0,
        ),
    )(core, z, t, tile_counts, owner_map, text, cot, *[hidden] * groups)


def text_kernel(
    core_ref, z_ref, tiles_ref, texts_ref, owners_ref, text_ref, weight_ref, cot_ref, *refs
):
    del core_ref
    moment_ref, gain_ref, long_ref, scaled_ref = refs[-4:]
    squares = refs[:-4]
    seq_len, width = cot_ref.shape

    @pl.when(pl.program_id(0) == 0)
    def _():
        parts = [r[...] for r in squares]
        while len(parts) > 1:
            parts = [parts[i] + parts[i + 1] for i in range(0, len(parts), 2)]
        image_tiles = text_count = jnp.int32(0)
        for s in range(owners_ref.shape[0]):
            mine = owners_ref[s] == z_ref[0]
            image_tiles = jnp.where(mine, tiles_ref[s], image_tiles)
            text_count = jnp.where(mine, texts_ref[s], text_count)
        begin = pl.multiple_of(jnp.clip(image_tiles, 0, MAXT) * TILE, TILE)
        places = lax.broadcasted_iota(jnp.int32, (1, seq_len), 1)
        scale = lax.rsqrt(parts[0] / D + EPSILON)
        scale = columns_of(jnp.where(places < text_count, scale, 0.0), seq_len)
        long_ref[:seq_len, :] = cot_ref[...]
        long_ref[seq_len:, :] = jnp.zeros((MAXT * TILE, width), jnp.bfloat16)
        for i in range(width // LANES):
            lanes = slice(i * LANES, (i + 1) * LANES)
            shifted = long_ref[pl.ds(begin, seq_len), lanes]
            scaled_ref[:, lanes] = (shifted.astype(jnp.float32) * scale).astype(jnp.bfloat16)

    moment = lax.dot_general(
        text_ref[...], scaled_ref[...], (((0,), (0,)), ((), ())), preferred_element_type=jnp.float32
    )
    for i in range(moment_ref.shape[0]):
        moment_ref[i] = moment[:, i * LANES : (i + 1) * LANES].astype(jnp.bfloat16)
    gain_ref[...] = row_of(fold(moment * weight_ref[...].astype(jnp.float32)))


def text_product(scalars, text, weight, cot, squares, width):
    seq_len, columns = text.shape
    groups = width // LANES
    step = 256
    return pl.pallas_call(
        text_kernel,
        grid_spec=pltpu.PrefetchScalarGridSpec(
            num_scalar_prefetch=len(scalars),
            grid=(columns // step,),
            in_specs=[
                pl.BlockSpec((seq_len, step), lambda i, *_: (0, i)),
                pl.BlockSpec((step, width), lambda i, c, *_: (i, c[0])),
                pl.BlockSpec((seq_len, width), lambda i, c, *_: (0, c[0])),
            ]
            + [pl.BlockSpec((1, seq_len), lambda i, *_: (0, 0))] * len(squares),
            out_specs=[
                pl.BlockSpec((groups, step, LANES), lambda i, *_: (0, i, 0)),
                pl.BlockSpec((1, step), lambda i, *_: (0, i)),
            ],
            scratch_shapes=[
                pltpu.VMEM((seq_len + MAXT * TILE, width), jnp.bfloat16),
                pltpu.VMEM((seq_len, width), jnp.bfloat16),
            ],
        ),
        out_shape=[
            jax.ShapeDtypeStruct((groups, columns, LANES), jnp.bfloat16),
            jax.ShapeDtypeStruct((1, columns), jnp.float32),
        ],
        compiler_params=pltpu.CompilerParams(vmem_limit_bytes=VMEM),
        cost_estimate=pl.CostEstimate(
            flops=2 * seq_len * columns * width,
            bytes_accessed=2 * (seq_len * (columns + width) + 2 * columns * width),
            transcendentals=0,
        ),
    )(*scalars, text, weight, cot, *squares)


def sums_kernel(rows_ref, grad_ref, gain_ref, sums_ref):
    values = rows_ref[...].astype(jnp.float32)
    more = sums_ref.shape[1] - values.shape[0]
    for i, terms in enumerate((values * values, values * grad_ref[...] * gain_ref[...])):
        folded = jnp.concatenate([fold(terms), jnp.zeros((more, LANES), jnp.float32)], 0)
        sums_ref[i : i + 1, :] = row_of(folded)


def row_sums(rows, grad, gain):
    count, width = rows.shape
    padded = -(-count // LANES) * LANES
    whole = pl.BlockSpec(memory_space=pltpu.VMEM)
    return pl.pallas_call(
        sums_kernel,
        in_specs=[whole] * 3,
        out_specs=whole,
        out_shape=jax.ShapeDtypeStruct((2, padded), jnp.float32),
        compiler_params=pltpu.CompilerParams(vmem_limit_bytes=16 * 1024 * 1024),
        cost_estimate=pl.CostEstimate(
            flops=8 * count * width, bytes_accessed=6 * count * width, transcendentals=0
        ),
    )(rows, grad, gain)


def image_kernel(core_ref, grad_ref, gain_ref, cot_ref, sums_ref, rows_ref, *out):
    embed_ref, here_ref, there_ref, small_ref = out
    stream, width = rows_ref.shape
    groups = sums_ref.shape[0]
    size = stream // groups
    inv, mean = [], []
    for i in range(groups):
        inv_row = lax.rsqrt(sums_ref[i, 0:1, :] / D + EPSILON)
        mean_row = inv_row * inv_row * inv_row * sums_ref[i, 1:2, :] / D
        inv.append(columns_of(inv_row, inv_row.shape[1])[:size])
        mean.append(columns_of(mean_row, mean_row.shape[1])[:size])
    all_inv = jnp.concatenate(inv, 0)
    gain_parts = [jnp.zeros((1, LANES), jnp.float32)] * (width // LANES)
    bias_parts = list(gain_parts)
    for g in range(groups):
        rows = slice(g * size, (g + 1) * size)
        to = jnp.bitwise_xor(core_ref[0], g % 2) * (stream // 2) + (g // 2) * size
        to_rows = pl.ds(pl.multiple_of(to, 16), size)
        for i in range(width // LANES):
            at = slice(i * LANES, (i + 1) * LANES)
            values = rows_ref[rows, at].astype(jnp.float32)
            scaled = grad_ref[rows, at] * inv[g]
            embed = (scaled * gain_ref[:, at] - values * mean[g]).astype(jnp.bfloat16)
            embed_ref[to_rows, at] = embed
            gain_parts[i] = gain_parts[i] + jnp.sum(scaled * values, 0, keepdims=True)
            bias_parts[i] = bias_parts[i] + jnp.sum(embed.astype(jnp.float32), 0, keepdims=True)
    small_ref[0:1, :] = jnp.concatenate(gain_parts, 1)
    small_ref[1:2, :] = jnp.concatenate(bias_parts, 1)
    lanes = cot_ref.shape[1]
    wide = [all_inv] * (lanes // LANES) if lanes >= LANES else [all_inv[:, :lanes]]
    cot = (cot_ref[...].astype(jnp.float32) * jnp.concatenate(wide, 1)).astype(jnp.bfloat16)
    moment = lax.dot_general(
        rows_ref[...], cot, (((0,), (0,)), ((), ())), preferred_element_type=jnp.float32
    )
    share = here_ref.shape[1]
    here_ref[...] = moment[:, :share]
    there_ref[...] = moment[:, share:].astype(jnp.bfloat16)


def image_grads(core, grad, gain, cot, sums, rows):
    stream, width = grad.shape
    share = cot.shape[1] // 2
    whole = pl.BlockSpec(memory_space=pltpu.VMEM)
    return pl.pallas_call(
        image_kernel,
        in_specs=[pl.BlockSpec(memory_space=pltpu.SMEM)] + [whole] * 5,
        out_specs=[whole] * 4,
        out_shape=[
            jax.ShapeDtypeStruct((stream, width), jnp.bfloat16),
            jax.ShapeDtypeStruct((width, share), jnp.float32),
            jax.ShapeDtypeStruct((width, share), jnp.bfloat16),
            jax.ShapeDtypeStruct((2, width), jnp.float32),
        ],
        compiler_params=pltpu.CompilerParams(vmem_limit_bytes=56 * 1024 * 1024),
        cost_estimate=pl.CostEstimate(
            flops=4 * stream * width * share, bytes_accessed=8 * stream * width, transcendentals=0
        ),
    )(core, grad, gain, cot, sums, rows)


def weight_kernel(act_ref, grad_ref, out_ref):
    step = act_ref.shape[0]
    groups = grad_ref.shape[1] // LANES
    product = jnp.dot(act_ref[...], grad_ref[...], preferred_element_type=jnp.float32)
    for c in range(groups):
        out_ref[pl.ds(c, step, stride=groups), :] = product[:, c * LANES : (c + 1) * LANES]


def weight_product(act, grad):
    features, rows = act.shape
    width = grad.shape[1]
    groups = width // LANES
    step = 256
    return pl.pallas_call(
        weight_kernel,
        grid=(features // step,),
        in_specs=[
            pl.BlockSpec((step, rows), lambda i: (i, 0)),
            pl.BlockSpec((rows, width), lambda i: (0, 0)),
        ],
        out_specs=pl.BlockSpec((step * groups, LANES), lambda i: (i, 0)),
        out_shape=jax.ShapeDtypeStruct((features * groups, LANES), jnp.float32),
        compiler_params=pltpu.CompilerParams(vmem_limit_bytes=VMEM),
        cost_estimate=pl.CostEstimate(
            flops=2 * rows * features * width,
            bytes_accessed=4 * features * width + 2 * rows * (features + width),
            transcendentals=0,
        ),
    )(act, grad)


def on_device(
    vis_hidden,
    proj_weight,
    proj_bias,
    text_embed,
    norm_gain,
    key_weight,
    key_cotangent,
    tile_counts,
    text_counts,
    owner_map,
):
    f32, bf16 = jnp.float32, jnp.bfloat16
    n_sec, n_seq, n_tp = (lax.axis_size(a) for a in ("sec", "seq", "tp"))
    core, z, t = (lax.axis_index(a) for a in ("sec", "seq", "tp"))
    block_rows, features = vis_hidden.shape
    columns = proj_weight.shape[1]
    col_half = columns // n_sec
    stream = block_rows * n_tp
    own = stream // n_seq
    half = own // n_sec
    groups = block_rows // own
    keys = key_weight.shape[1]
    key_half = keys // n_sec
    seq_len = text_embed.shape[0]

    text_sq, act, given = opening(
        core[None], z[None], t[None], tile_counts, owner_map,
        text_embed, vis_hidden, key_cotangent, groups, n_sec, n_tp, stream,
    )
    pieces = [act] + [swap(act, "tp", m) for m in range(1, n_tp)]
    text_sq = [text_sq] + [swap(text_sq, "tp", m) for m in range(1, n_tp)]
    given = given + swap(given, "seq", 1)
    text_sq[0], pieces[1], given = together(text_sq[0], pieces[1], given)

    scalars = (core[None], z[None], tile_counts, text_counts, owner_map)
    moment, gain_text = text_product(
        scalars, text_embed, key_weight, key_cotangent, text_sq, key_half
    )
    taken = butterfly(given, ("seq",), 2)
    if n_seq <= 4:
        way = line_step(moment, "seq", 1, None)
    else:
        share = key_half // n_seq
        moment = moment.reshape(-1, columns, LANES // share, share).transpose(0, 2, 1, 3)
        moment = reduce_to_owner(moment.reshape(n_seq, columns, share), "seq")

    partial, act_mine = project(t[None], pieces, proj_weight)
    if n_seq <= 4:
        way[0], way[1], taken, _ = together(*way, taken, partial)
        way = line_step(moment, "seq", 2, way)
    summed = lax.psum_scatter(partial, "seq", scatter_dimension=0, tiled=True)

    key_bias_part = jnp.sum(key_cotangent.astype(f32), 0)
    early = jnp.concatenate([gain_text[0], jnp.where(core == 0, key_bias_part, 0.0)])

    act_other = swap(act_mine, "sec", 1)
    taken = [taken] + [swap(taken, "tp", m) for m in range(1, n_tp)]
    half_cot = jnp.concatenate(in_order(taken, t), 1)
    other_cot = swap(half_cot, "sec", 1)
    image_cot = jnp.concatenate(in_order([half_cot, other_cot], core), 1)
    weight_rows = lax.dynamic_slice_in_dim(key_weight, core * col_half, col_half, 0)
    normed_grad = lax.dot_general(
        image_cot, weight_rows, (((1,), (1,)), ((), ())), preferred_element_type=f32
    )
    own_cot = lax.dynamic_slice_in_dim(image_cot, (z * n_sec + core) * half, half, 0)
    own_grad = lax.dot_general(
        own_cot, key_weight, (((1,), (1,)), ((), ())), preferred_element_type=f32
    )
    key_share = key_half // n_seq
    cot_own = jnp.concatenate(
        [lax.dynamic_slice_in_dim(c, z * key_share, key_share, 1) for c in (half_cot, other_cot)], 1
    )

    summed, normed_grad, own_grad = together(summed, normed_grad, own_grad)
    image_mine = (summed.astype(f32) + proj_bias).astype(bf16)
    if n_seq <= 4:
        way[0], way[1], image_mine = together(*way, image_mine)
    low, high = image_mine[:, :col_half], image_mine[:, col_half:]
    first_core = core == 0
    came = swap(jnp.where(first_core, high, low), "sec", 1)
    image = jnp.concatenate(in_order([jnp.where(first_core, low, high), came], core), 0)
    rows = lax.all_gather(image, "seq", axis=0, tiled=True)

    image_mine, came = together(image_mine, came)
    sums = total(row_sums(image_mine, own_grad, norm_gain[None]), "tp")
    size = sums.size
    sums = jnp.concatenate([sums.reshape(-1), early])
    if n_seq <= 4:
        sums = jnp.stack(in_order([sums] + [swap(sums, "seq", m) for m in range(1, n_seq)], z), 0)
    else:
        sums = lax.all_gather(sums, "seq", axis=0, tiled=False)
    early = jnp.sum(sums[:, size:], 0)
    sums = jnp.concatenate([sums[:, :size].reshape(-1), early])
    sums = jnp.stack(in_order([sums, swap(sums, "sec", 1)], core), 0)
    early = jnp.sum(sums[:, n_seq * size :], 0)
    sums = sums[:, : n_seq * size].reshape(n_sec, n_seq, 2, -1).transpose(1, 0, 2, 3)
    sums = sums.reshape(n_seq * n_sec, 2, -1)

    if n_seq <= 4:
        for step in range(3, n_seq):
            way = line_step(moment, "seq", step, way)
        moment = lax.dynamic_index_in_dim(moment, z, 0, keepdims=False).astype(f32)
        moment = moment + way[0].astype(f32) + way[1].astype(f32)
    gain_half = lax.dynamic_slice_in_dim(norm_gain, core * col_half, col_half, 0)[None]
    embed_grad, here, there, small = image_grads(
        core[None], normed_grad, gain_half, cot_own, sums, rows
    )
    there = swap(there, "sec", 1)
    small_other = swap(small, "sec", 1)
    act_turned = jnp.concatenate([act_mine, act_other], 0).T
    weight_grad = weight_product(act_turned, embed_grad)
    proj_weight_grad = weight_grad.reshape(features, 1, 1, col_half)

    both = in_order([here, there.astype(f32)], core)
    key_weight_grad = (moment + jnp.concatenate(both, 0)) * norm_gain[:, None]
    gain_image, proj_bias_grad = jnp.concatenate(in_order([small, small_other], core), 1)
    gain_grad = early[:columns] + gain_image
    key_bias_grad = early[columns:]
    return (proj_weight_grad, proj_bias_grad, key_weight_grad, key_bias_grad, gain_grad)


def solution(mesh):
    placed = (
        P("tp", "seq"),
        P("seq", "tp"),
        P("tp"),
        P("seq", "tp"),
        P("tp"),
        P("tp", None),
        P("seq", None),
        P(),
        P(),
        P(),
    )
    return jax.shard_map(
        on_device,
        mesh=mesh,
        in_specs=placed,
        out_specs=(P("seq", "tp", "sec", None), P("tp"), P("tp", ("sec", "seq")), P(), P("tp")),
        check_vma=False,
    )
```
